32 devices in a mesh: dp: 8 (over z, y), tm: 4 (over x, core).
Axes of the slice: x: 2, y: 2, z: 4, core: 2. Of those that a mesh axis runs over, the one named last changes fastest.
Arguments:
- latents: bfloat16 [8, 24, 16, 128, 128], P('dp', 'tm'), may hold values from -6 to 6
- cotangent: bfloat16 [8, 24, 16, 128, 128], P('dp', 'tm'), may hold values from -6 to 6
- first_spatial: bfloat16 [3, 3, 128, 128], replicated, may hold values from -0.1875 to 0.1875
- last_spatial: bfloat16 [3, 3, 128, 128], replicated, may hold values from -0.1875 to 0.1875
- first_temporal: bfloat16 [3, 128, 128], replicated, may hold values from -0.3125 to 0.3125
- second_temporal: bfloat16 [3, 128, 128], replicated, may hold values from -0.3125 to 0.3125
- frame_counts: int32 [8], P('dp'), may hold values from 12 to 24, as said below
- dilations: int32 [2], replicated, may hold values from 1 to 4, as said below
Outputs:
- decoded: bfloat16 [8, 24, 16, 128, 128], P('dp', 'tm')
- latent_grad: bfloat16 [8, 24, 16, 128, 128], P('dp', 'tm')
- first_spatial_grad: float32 [3, 3, 128, 128], replicated
- last_spatial_grad: float32 [3, 3, 128, 128], replicated
- first_temporal_grad: float32 [3, 128, 128], replicated
- second_temporal_grad: float32 [3, 128, 128], replicated
The draws below stay inside these ranges and needn't reach their ends.
Inputs may be any that keep to these rules, and one draw needn't show every extreme that they name: `frame_counts`: each clip's valid frames stand at the start of its 24 slots; some clip has 24. At least one of the two dilations is 4.
All inputs are finite; a program needn't handle non-finite values.
Results may differ from the reference program's by a relative error of at most 0.0079.
Values may be sent and summed in bfloat16 or wider, within the bound.
No kernel may reach another device: no remote copies, remote signals or barrier semaphores. Data moves between devices by JAX's collectives and lax.ppermute only.
A program may use at most 256 MiB of HBM per device.

```python
import jax
import jax.numpy as jnp
from jax import lax

C = 128
WIDTH = 128
ROWS = 16
SLOTS = 24
MIN_FRAMES = 12
MAX_FRAMES = 24
TAPS = 3
DILATION_MAX = 4
CLIPS = 8


def draw_frame_counts(key, part):
    key_counts = jax.random.fold_in(key, 11)
    key_longest = jax.random.fold_in(key, 12)
    counts = jax.random.randint(key_counts, (CLIPS,), MIN_FRAMES, MAX_FRAMES + 1)
    longest = jax.random.randint(key_longest, (), 0, CLIPS)
    return jnp.where(jnp.arange(CLIPS) == longest, MAX_FRAMES, counts).astype(jnp.int32)


def draw_dilations(key, part):
    key_other = jax.random.fold_in(key, 21)
    key_which = jax.random.fold_in(key, 22)
    other = jax.random.randint(key_other, (), 1, DILATION_MAX + 1)
    which = jax.random.randint(key_which, (), 0, 2)
    return jnp.where(jnp.arange(2) == which, DILATION_MAX, other).astype(jnp.int32)


def shard_levels(stream_key, extent, pieces, smallest, high):
    loudness, own = 1.0, jax.random.fold_in(stream_key, 6)
    for axis_at, shards_of in pieces:
        steps = jnp.exp(jax.random.uniform(jax.random.fold_in(own, axis_at), (shards_of,), jnp.float32, smallest / len(pieces), high / len(pieces)))
        loudness = loudness * jnp.repeat(steps, extent[axis_at] // shards_of).reshape([-1 if axis == axis_at else 1 for axis in range(len(extent))])
    return loudness


def bell_draw(rng, dims, scale, limit, cuts=(), kind=jnp.bfloat16):
    factor_of = shard_levels(rng, dims, cuts, -0.22, 0.18) if cuts else 1.0
    entries = jax.random.normal(rng, dims, jnp.float32) * scale * factor_of
    return jnp.minimum(jnp.maximum(entries, -limit), limit).astype(kind)


def setup_inputs(seed: int = 0) -> dict:
    seeds = jax.random.split(jax.random.key(seed), 9)
    return {
        "latents": bell_draw(seeds[0], (CLIPS, SLOTS, ROWS, WIDTH, C), 1.0, 6.0, ((0, 8), (1, 4))),
        "cotangent": bell_draw(seeds[1], (CLIPS, SLOTS, ROWS, WIDTH, C), 1.0, 6.0, ((0, 8), (1, 4))),
        "first_spatial": bell_draw(seeds[2], (3, 3, C, C), (9 * C) ** -0.5, 0.1875),
        "last_spatial": bell_draw(seeds[3], (3, 3, C, C), (9 * C) ** -0.5, 0.1875),
        "first_temporal": bell_draw(seeds[4], (TAPS, C, C), (TAPS * C) ** -0.5, 0.3125),
        "second_temporal": bell_draw(seeds[5], (TAPS, C, C), (TAPS * C) ** -0.5, 0.3125),
        "frame_counts": draw_frame_counts(jax.random.fold_in(seeds[8], 71), 0),
        "dilations": draw_dilations(jax.random.fold_in(seeds[8], 71), 0),
    }


def silu_slope(values):
    sigma = jax.nn.sigmoid(values)
    return sigma * (1.0 + values * (1.0 - sigma))


def spatial(source, kernel):
    row_count, col_count, channels = source.shape[-3:]
    leading = source.shape[:-3]
    padded = jnp.pad(source, [(0, 0)] * len(leading) + [(1, 1), (1, 1), (0, 0)])
    summed = jnp.zeros(leading + (row_count, col_count, kernel.shape[3]), jnp.float32)
    for row_shift in range(3):
        for col_shift in range(3):
            window = padded[..., row_shift:row_shift + row_count, col_shift:col_shift + col_count, :]
            window = window.reshape(-1, channels).astype(jnp.float32)
            product = jnp.dot(window, kernel[row_shift, col_shift].astype(jnp.float32),
                              precision=lax.Precision.HIGHEST)
            summed = summed + product.reshape(summed.shape)
    return summed


def spatial_back(incoming, kernel):
    return spatial(incoming, jnp.transpose(kernel[::-1, ::-1], (0, 1, 3, 2)))


def spatial_kernel(source, incoming):
    row_count, col_count, channels = source.shape[-3:]
    leading = source.shape[:-3]
    padded = jnp.pad(source, [(0, 0)] * len(leading) + [(1, 1), (1, 1), (0, 0)])
    flat_in = incoming.reshape(-1, incoming.shape[-1]).astype(jnp.float32)
    result_rows = []
    for row_shift in range(3):
        result_cols = []
        for col_shift in range(3):
            window = padded[..., row_shift:row_shift + row_count, col_shift:col_shift + col_count, :]
            window = window.reshape(-1, channels).astype(jnp.float32)
            result_cols.append(lax.dot_general(window, flat_in, (((0,), (0,)), ((), ())),
                                               precision=lax.Precision.HIGHEST))
        result_rows.append(jnp.stack(result_cols))
    return jnp.stack(result_rows)


def temporal(source, kernel, dilation):
    margin = (TAPS - 1) * DILATION_MAX
    slot_count = source.shape[1]
    padded = jnp.pad(source, ((0, 0), (margin, 0), (0, 0), (0, 0), (0, 0)))
    summed = jnp.zeros(source.shape[:-1] + (kernel.shape[2],), jnp.float32)
    for tap_index in range(kernel.shape[0]):
        begin_at = (margin - tap_index * dilation).astype(jnp.int32)
        window = lax.dynamic_slice_in_dim(padded, begin_at, slot_count, 1)
        window = window.reshape(-1, source.shape[-1]).astype(jnp.float32)
        product = jnp.dot(window, kernel[tap_index].astype(jnp.float32), precision=lax.Precision.HIGHEST)
        summed = summed + product.reshape(summed.shape)
    return summed


def temporal_back(incoming, kernel, dilation):
    margin = (TAPS - 1) * DILATION_MAX
    slot_count = incoming.shape[1]
    padded = jnp.pad(incoming, ((0, 0), (0, margin), (0, 0), (0, 0), (0, 0)))
    summed = jnp.zeros(incoming.shape[:-1] + (kernel.shape[1],), jnp.float32)
    for tap_index in range(kernel.shape[0]):
        begin_at = (tap_index * dilation).astype(jnp.int32)
        window = lax.dynamic_slice_in_dim(padded, begin_at, slot_count, 1)
        window = window.reshape(-1, incoming.shape[-1]).astype(jnp.float32)
        product = jnp.dot(window, kernel[tap_index].astype(jnp.float32).T, precision=lax.Precision.HIGHEST)
        summed = summed + product.reshape(summed.shape)
    return summed


def temporal_kernel(source, incoming, dilation):
    margin = (TAPS - 1) * DILATION_MAX
    slot_count = source.shape[1]
    padded = jnp.pad(source, ((0, 0), (margin, 0), (0, 0), (0, 0), (0, 0)))
    flat_in = incoming.reshape(-1, incoming.shape[-1]).astype(jnp.float32)
    result = []
    for tap_index in range(TAPS):
        begin_at = (margin - tap_index * dilation).astype(jnp.int32)
        window = lax.dynamic_slice_in_dim(padded, begin_at, slot_count, 1)
        window = window.reshape(-1, source.shape[-1]).astype(jnp.float32)
        result.append(lax.dot_general(window, flat_in, (((0,), (0,)), ((), ())),
                                      precision=lax.Precision.HIGHEST))
    return jnp.stack(result)


def reference(latents, cotangent, first_spatial, last_spatial, first_temporal, second_temporal,
              frame_counts, dilations):
    slot_ids = jnp.arange(SLOTS, dtype=jnp.int32)
    is_valid = (slot_ids[None, :] < frame_counts[:, None])[:, :, None, None, None]
    factor = float(CLIPS * SLOTS * ROWS * WIDTH) ** -0.5
    pre_in = spatial(latents, first_spatial)
    act_in = jax.nn.silu(pre_in).astype(jnp.bfloat16)
    pre_mid = temporal(act_in, first_temporal, dilations[0])
    act_mid = jax.nn.silu(pre_mid).astype(jnp.bfloat16)
    act_out = temporal(act_mid, second_temporal, dilations[1]).astype(jnp.bfloat16)
    decoded = jnp.where(is_valid, latents.astype(jnp.float32) + spatial(act_out, last_spatial),
                        jnp.float32(0.0)).astype(jnp.bfloat16)
    masked = jnp.where(is_valid, cotangent, jnp.zeros_like(cotangent))
    last_grad = factor * spatial_kernel(act_out, masked)
    back_out = spatial_back(masked, last_spatial).astype(jnp.bfloat16)
    second_grad = factor * temporal_kernel(act_mid, back_out, dilations[1])
    slope_mid = (temporal_back(back_out, second_temporal, dilations[1]) * silu_slope(pre_mid)).astype(jnp.bfloat16)
    first_grad = factor * temporal_kernel(act_in, slope_mid, dilations[0])
    back_in = temporal_back(slope_mid, first_temporal, dilations[0]).astype(jnp.bfloat16)
    slope_in = (back_in.astype(jnp.float32) * silu_slope(pre_in)).astype(jnp.bfloat16)
    spatial_grad = factor * spatial_kernel(latents, slope_in)
    latent_grad = (masked.astype(jnp.float32) + spatial_back(slope_in, first_spatial)).astype(jnp.bfloat16)
    return (decoded, latent_grad, spatial_grad, last_grad, first_grad, second_grad)
```

```python
import functools

import jax
import jax.numpy as jnp
from jax import lax
from jax.experimental import pallas as pl
from jax.experimental.pallas import tpu as pltpu
from jax.sharding import PartitionSpec as P

TAPS = 3
DILATION_MAX = 4


def silu_slope(values):
    sigma = jax.nn.sigmoid(values)
    return sigma * (1.0 + values * (1.0 - sigma))


def spatial(source, kernel):
    row_count, col_count, channels = source.shape[-3:]
    leading = source.shape[:-3]
    padded = jnp.pad(source, [(0, 0)] * len(leading) + [(1, 1), (1, 1), (0, 0)])
    summed = jnp.zeros(leading + (row_count, col_count, kernel.shape[3]), jnp.float32)
    for row_shift in range(3):
        for col_shift in range(3):
            window = padded[
                ..., row_shift : row_shift + row_count, col_shift : col_shift + col_count, :
            ]
            product = jnp.dot(
                window.reshape(-1, channels),
                kernel[row_shift, col_shift],
                preferred_element_type=jnp.float32,
            )
            summed = summed + product.reshape(summed.shape)
    return summed


def spatial_back(incoming, kernel):
    return spatial(incoming, jnp.transpose(kernel[::-1, ::-1], (0, 1, 3, 2)))


def spatial_kernel(source, incoming):
    row_count, col_count, channels = source.shape[-3:]
    leading = source.shape[:-3]
    padded = jnp.pad(source, [(0, 0)] * len(leading) + [(1, 1), (1, 1), (0, 0)])
    flat_in = incoming.reshape(-1, incoming.shape[-1])
    result_rows = []
    for row_shift in range(3):
        result_cols = []
        for col_shift in range(3):
            window = padded[
                ..., row_shift : row_shift + row_count, col_shift : col_shift + col_count, :
            ]
            result_cols.append(
                lax.dot_general(
                    window.reshape(-1, channels),
                    flat_in,
                    (((0,), (0,)), ((), ())),
                    preferred_element_type=jnp.float32,
                )
            )
        result_rows.append(jnp.stack(result_cols))
    return jnp.stack(result_rows)


def temporal(source, kernel, dilation):
    margin = (TAPS - 1) * DILATION_MAX
    slot_count = source.shape[1]
    padded = jnp.pad(source, ((0, 0), (margin, 0), (0, 0), (0, 0), (0, 0)))
    summed = jnp.zeros(source.shape[:-1] + (kernel.shape[2],), jnp.float32)
    for tap_index in range(kernel.shape[0]):
        begin_at = margin - tap_index * dilation
        window = lax.dynamic_slice_in_dim(padded, begin_at, slot_count, 1)
        product = jnp.dot(
            window.reshape(-1, source.shape[-1]),
            kernel[tap_index],
            preferred_element_type=jnp.float32,
        )
        summed = summed + product.reshape(summed.shape)
    return summed


def temporal_back(incoming, kernel, dilation):
    margin = (TAPS - 1) * DILATION_MAX
    slot_count = incoming.shape[1]
    padded = jnp.pad(incoming, ((0, 0), (0, margin), (0, 0), (0, 0), (0, 0)))
    summed = jnp.zeros(incoming.shape[:-1] + (kernel.shape[1],), jnp.float32)
    for tap_index in range(kernel.shape[0]):
        begin_at = tap_index * dilation
        window = lax.dynamic_slice_in_dim(padded, begin_at, slot_count, 1)
        product = jnp.dot(
            window.reshape(-1, incoming.shape[-1]),
            kernel[tap_index].T,
            preferred_element_type=jnp.float32,
        )
        summed = summed + product.reshape(summed.shape)
    return summed


def temporal_kernel(source, incoming, dilation):
    margin = (TAPS - 1) * DILATION_MAX
    slot_count = source.shape[1]
    padded = jnp.pad(source, ((0, 0), (margin, 0), (0, 0), (0, 0), (0, 0)))
    flat_in = incoming.reshape(-1, incoming.shape[-1])
    result = []
    for tap_index in range(TAPS):
        begin_at = margin - tap_index * dilation
        window = lax.dynamic_slice_in_dim(padded, begin_at, slot_count, 1)
        result.append(
            lax.dot_general(
                window.reshape(-1, source.shape[-1]),
                flat_in,
                (((0,), (0,)), ((), ())),
                preferred_element_type=jnp.float32,
            )
        )
    return jnp.stack(result)


def forward_bands(band_in, first_temporal, second_temporal, dilations):
    pre_mid = temporal(band_in, first_temporal, dilations[0])
    act_mid = jax.nn.silu(pre_mid).astype(jnp.bfloat16)
    act_out = temporal(act_mid, second_temporal, dilations[1]).astype(jnp.bfloat16)
    return (pre_mid, act_mid, act_out)


def on_device(
    latents,
    cotangent,
    first_spatial,
    last_spatial,
    first_temporal,
    second_temporal,
    frame_counts,
    dilations,
):
    local_slots = latents.shape[1]
    first_slot = lax.axis_index("tm") * local_slots
    slot_ids = first_slot + jnp.arange(local_slots, dtype=jnp.int32)
    is_valid = (slot_ids[None, :] < frame_counts[:, None])[:, :, None, None, None]
    total_count = (
        latents.shape[0]
        * lax.axis_size("dp")
        * local_slots
        * lax.axis_size("tm")
        * latents.shape[2]
        * latents.shape[3]
    )
    factor = float(total_count) ** (-0.5)
    pre_in = spatial(latents, first_spatial)
    act_in = jax.nn.silu(pre_in).astype(jnp.bfloat16)
    masked = jnp.where(is_valid, cotangent, jnp.zeros_like(cotangent))
    band_in = lax.all_to_all(act_in, "tm", split_axis=2, concat_axis=1, tiled=True)
    pre_mid, act_mid, act_out = forward_bands(band_in, first_temporal, second_temporal, dilations)
    back_out = spatial_back(masked, last_spatial).astype(jnp.bfloat16)
    band_back = lax.all_to_all(back_out, "tm", split_axis=2, concat_axis=1, tiled=True)
    second_grad = temporal_kernel(act_mid, band_back, dilations[1])
    slope_mid = (
        temporal_back(band_back, second_temporal, dilations[1]) * silu_slope(pre_mid)
    ).astype(jnp.bfloat16)
    first_grad = temporal_kernel(band_in, slope_mid, dilations[0])
    back_in = temporal_back(slope_mid, first_temporal, dilations[0]).astype(jnp.bfloat16)
    frame_out, frame_back = (
        lax.all_to_all(act_out, "tm", split_axis=1, concat_axis=2, tiled=True),
        lax.all_to_all(back_in, "tm", split_axis=1, concat_axis=2, tiled=True),
    )
    decoded = jnp.where(
        is_valid, latents.astype(jnp.float32) + spatial(frame_out, last_spatial), jnp.float32(0.0)
    ).astype(jnp.bfloat16)
    last_grad = spatial_kernel(frame_out, masked)
    slope_in = (frame_back.astype(jnp.float32) * silu_slope(pre_in)).astype(jnp.bfloat16)
    spatial_grad = spatial_kernel(latents, slope_in)
    latent_grad = (masked.astype(jnp.float32) + spatial_back(slope_in, first_spatial)).astype(
        jnp.bfloat16
    )
    partials = (
        factor * spatial_grad,
        factor * last_grad,
        factor * first_grad,
        factor * second_grad,
    )
    reduced = lax.psum((partials[0], partials[1], partials[2], partials[3]), ("dp", "tm"))
    return (decoded, latent_grad, reduced[0], reduced[1], reduced[2], reduced[3])


REACH = (TAPS - 1) * DILATION_MAX
CHUNKS = 2
VMEM_LIMIT = 56 * 1024 * 1024
BF = jnp.bfloat16
F32 = jnp.float32


def params():
    return pltpu.CompilerParams(
        dimension_semantics=("arbitrary",), vmem_limit_bytes=VMEM_LIMIT
    )


def cost(flops, nbytes):
    return pl.CostEstimate(flops=int(flops), bytes_accessed=int(nbytes), transcendentals=0)


def zero_borders(pad, pairs):
    pad[...] = jnp.zeros(pad.shape, F32)
    lanes = pairs.shape[2]
    width = pairs.shape[1]
    pairs[0, :, 0 : lanes // 2] = jnp.zeros((width, lanes // 2), BF)
    pairs[pairs.shape[0] - 1, :, lanes // 2 : lanes] = jnp.zeros((width, lanes // 2), BF)


def fill_pairs(frame, pad, pairs):
    rows, width, chans = frame.shape
    pad[:, 8 : 8 + width, :] = frame[...].astype(F32)
    for shift in range(3):
        if shift == 1:
            seen = frame[...]
        else:
            seen = pad[:, 7 + shift : 7 + shift + width, :].astype(BF)
        seen = seen.reshape(rows // 2, 2, width, chans)
        low = shift * chans
        pairs[0 : rows // 2, :, (3 * chans + low) : (3 * chans + low + chans)] = seen[:, 0]
        pairs[1 : rows // 2 + 1, :, low : low + chans] = seen[:, 1]


def two_row_conv(pairs, weights, first, count):
    width = pairs.shape[1]
    lanes = pairs.shape[2]
    upper = pairs[first : first + count].reshape(count * width, lanes)
    lower = pairs[first + 1 : first + 1 + count].reshape(count * width, lanes)
    return jnp.dot(
        jnp.concatenate([upper, lower], axis=1), weights[...], preferred_element_type=F32
    )


def front_kernel(
    ids, latents, cotangent, w_in, w_back,
    act_keep, act_send, back_keep, back_send, slope,
    pad, pairs, frame, result,
):
    at = pl.program_id(0)
    core = ids[1]
    rows, width, chans = frame.shape
    half = rows // 2
    step = half // 2

    @pl.when(at == 0)
    def _():
        zero_borders(pad, pairs)

    frame[...] = latents[0]
    fill_pairs(frame, pad, pairs)
    for part in range(2):
        pre = two_row_conv(pairs, w_in, part * step, step)
        sigma = jax.nn.sigmoid(pre)
        act = (pre * sigma).astype(BF).reshape(step, width, 2 * chans)
        grad = (sigma * (1.0 + pre * (1.0 - sigma))).astype(BF).reshape(step, width, 2 * chans)
        for pair in range(step):
            for odd in range(2):
                row = part * half + 2 * pair + odd
                lanes = slice(odd * chans, odd * chans + chans)
                result[row] = act[pair, :, lanes]
                slope[0, row] = grad[pair, :, lanes]
    act_keep[0] = result[pl.ds(core * half, half)]
    act_send[0] = result[pl.ds(half - core * half, half)]

    keep = jnp.where(at < ids[2], 1.0, 0.0).astype(F32)
    frame[...] = (cotangent[0].astype(F32) * keep).astype(BF)
    fill_pairs(frame, pad, pairs)
    for part in range(2):
        back = two_row_conv(pairs, w_back, part * step, step)
        back = back.astype(BF).reshape(step, width, 2 * chans)
        for pair in range(step):
            for odd in range(2):
                row = part * half + 2 * pair + odd
                result[row] = back[pair, :, odd * chans : odd * chans + chans]
    back_keep[0] = result[pl.ds(core * half, half)]
    back_send[0] = result[pl.ds(half - core * half, half)]


def front(ids, latents, cotangent, w_in, w_back):
    slots, rows, width, chans = latents.shape
    half = rows // 2
    whole = pl.BlockSpec((1, rows, width, chans), lambda i, ids: (i, 0, 0, 0))
    part = pl.BlockSpec((1, half, width, chans), lambda i, ids: (i, 0, 0, 0))
    fixed = pl.BlockSpec(w_in.shape, lambda i, ids: (0, 0))
    halves = jax.ShapeDtypeStruct((slots, half, width, chans), BF)
    return pl.pallas_call(
        front_kernel,
        grid_spec=pltpu.PrefetchScalarGridSpec(
            num_scalar_prefetch=1,
            grid=(slots,),
            in_specs=[whole, whole, fixed, fixed],
            out_specs=[part, part, part, part, whole],
            scratch_shapes=[
                pltpu.VMEM((rows, width + 16, chans), F32),
                pltpu.VMEM((half + 1, width, 6 * chans), BF),
                pltpu.VMEM((rows, width, chans), BF),
                pltpu.VMEM((rows, width, chans), BF),
            ],
        ),
        out_shape=[halves, halves, halves, halves, jax.ShapeDtypeStruct(latents.shape, BF)],
        compiler_params=params(),
        cost_estimate=cost(4 * latents.size * chans * 12, 10 * latents.size),
        name="front",
    )(ids, latents, cotangent, w_in, w_back)


def taps_of(held, start, step, count):
    size = held.shape[1]
    chans = held.shape[2]
    seen = []
    for tap in range(TAPS):
        seen.append(held[pl.ds(start + tap * step, count)].reshape(count * size, chans))
    return jnp.concatenate(seen, axis=1)


def outer(left, right):
    return lax.dot_general(left, right, (((0,), (0,)), ((), ())), preferred_element_type=F32)


def middle_kernel(
    ids, own_in, got_in, own_back, got_back, halo, w_mid, w_mid_back, w_first,
    mid_send, mid_keep, first_keep, first_send, grad_first, grad_second,
    held_in, held_back, held_mid, result,
):
    at = pl.program_id(0)
    side, core, near, far = ids[0], ids[1], ids[3], ids[4]
    slots = own_in.shape[0]
    frames = 2 * slots
    mine = core * slots
    other = slots - mine

    @pl.when(at == 0)
    def _():
        blank = jnp.zeros((REACH,) + held_in.shape[1:], BF)
        held_in[0:REACH] = blank
        held_back[frames : frames + REACH] = blank
        held_mid[0:REACH] = blank
        held_mid[REACH + frames : 2 * REACH + frames] = blank
        grad_first[...] = jnp.zeros_like(grad_first)
        grad_second[...] = jnp.zeros_like(grad_second)

    held_in[pl.ds(REACH + mine, slots)] = own_in[:, 0]
    held_in[pl.ds(REACH + other, slots)] = got_in[:, 0]
    held_back[pl.ds(mine, slots)] = own_back[:, 0]
    held_back[pl.ds(other, slots)] = got_back[:, 0]

    @pl.when(side == 0)
    def _():
        held_back[frames : frames + REACH] = halo[:, 0]

    @pl.when(side == 1)
    def _():
        held_in[0:REACH] = halo[:, 0]

    size, chans = held_in.shape[1:]
    taps_in = taps_of(held_in, REACH, -near, frames)
    taps_back = taps_of(held_back, 0, far, frames)
    pre = jnp.dot(taps_in, w_mid[...], preferred_element_type=F32)
    sigma = jax.nn.sigmoid(pre)
    act = (pre * sigma).astype(BF)
    back = jnp.dot(taps_back, w_mid_back[...], preferred_element_type=F32)
    grad = (back * (sigma * (1.0 + pre * (1.0 - sigma)))).astype(BF)
    grad_second[...] += outer(act, taps_back)
    grad_first[...] += outer(grad, taps_in)
    act = act.reshape(frames, size, chans)
    grad = grad.reshape(frames, size, chans)

    @pl.when(side == 0)
    def _():
        held_mid[REACH : REACH + frames] = act
        mid_keep[:, 0] = grad
        mid_send[:, 0] = act[frames - REACH :]

    @pl.when(side == 1)
    def _():
        held_mid[REACH : REACH + frames] = grad
        mid_keep[:, 0] = act
        mid_send[:, 0] = grad[:REACH]

    step = jnp.where(side == 0, -far, near)
    first = jnp.dot(
        taps_of(held_mid, REACH, step, frames), w_first[...], preferred_element_type=F32
    )
    result[...] = first.astype(BF).reshape(frames, size, chans)
    first_keep[:, 0] = result[pl.ds(mine, slots)]
    first_send[:, 0] = result[pl.ds(other, slots)]


def middle(chunk, ids, own_in, got_in, own_back, got_back, halo, w_mid, w_mid_back, w_first):
    slots, half, width, chans = own_in.shape
    frames = 2 * slots
    rows = halo.shape[1]
    source = pl.BlockSpec((slots, 1, width, chans), lambda i, ids: (0, chunk * rows + i, 0, 0))
    fixed = pl.BlockSpec(w_mid.shape, lambda i, ids: (0, 0))
    sums = pl.BlockSpec((chans, TAPS * chans), lambda i, ids: (0, 0))

    def rowwise(count):
        return pl.BlockSpec((count, 1, width, chans), lambda i, ids: (0, i, 0, 0))

    def shaped(count):
        return jax.ShapeDtypeStruct((count, rows, width, chans), BF)

    summed = jax.ShapeDtypeStruct((chans, TAPS * chans), F32)
    return pl.pallas_call(
        middle_kernel,
        grid_spec=pltpu.PrefetchScalarGridSpec(
            num_scalar_prefetch=1,
            grid=(rows,),
            in_specs=[source, source, source, source, rowwise(REACH), fixed, fixed, fixed],
            out_specs=[
                rowwise(REACH), rowwise(frames), rowwise(slots), rowwise(slots), sums, sums,
            ],
            scratch_shapes=[
                pltpu.VMEM((REACH + frames, width, chans), BF),
                pltpu.VMEM((REACH + frames, width, chans), BF),
                pltpu.VMEM((2 * REACH + frames, width, chans), BF),
                pltpu.VMEM((frames, width, chans), BF),
            ],
        ),
        out_shape=[
            shaped(REACH), shaped(frames), shaped(slots), shaped(slots), summed, summed,
        ],
        compiler_params=params(),
        cost_estimate=cost(
            2 * frames * rows * width * chans * chans * 30, 14 * frames * rows * width * chans
        ),
        name="middle",
    )(ids, own_in, got_in, own_back, got_back, halo, w_mid, w_mid_back, w_first)


def second_kernel(ids, mid, halo, w_second, keep, send, held, result):
    at = pl.program_id(0)
    side, core, near, far = ids[0], ids[1], ids[3], ids[4]
    frames = mid.shape[0]
    slots = frames // 2
    mine = core * slots

    @pl.when(at == 0)
    def _():
        blank = jnp.zeros((REACH,) + held.shape[1:], BF)
        held[0:REACH] = blank
        held[REACH + frames : 2 * REACH + frames] = blank

    held[REACH : REACH + frames] = mid[:, 0]

    @pl.when(side == 0)
    def _():
        held[REACH + frames : 2 * REACH + frames] = halo[:, 0]

    @pl.when(side == 1)
    def _():
        held[0:REACH] = halo[:, 0]

    step = jnp.where(side == 0, near, -far)
    made = jnp.dot(
        taps_of(held, REACH, step, frames), w_second[...], preferred_element_type=F32
    )
    result[...] = made.astype(BF).reshape(result.shape)
    keep[:, 0] = result[pl.ds(mine, slots)]
    send[:, 0] = result[pl.ds(slots - mine, slots)]


def second(ids, mid, halo, w_second):
    frames, rows, width, chans = mid.shape
    slots = frames // 2

    def rowwise(count):
        return pl.BlockSpec((count, 1, width, chans), lambda i, ids: (0, i, 0, 0))

    shape = jax.ShapeDtypeStruct((slots, rows, width, chans), BF)
    return pl.pallas_call(
        second_kernel,
        grid_spec=pltpu.PrefetchScalarGridSpec(
            num_scalar_prefetch=1,
            grid=(rows,),
            in_specs=[
                rowwise(frames), rowwise(REACH),
                pl.BlockSpec(w_second.shape, lambda i, ids: (0, 0)),
            ],
            out_specs=[rowwise(slots), rowwise(slots)],
            scratch_shapes=[
                pltpu.VMEM((2 * REACH + frames, width, chans), BF),
                pltpu.VMEM((frames, width, chans), BF),
            ],
        ),
        out_shape=[shape, shape],
        compiler_params=params(),
        cost_estimate=cost(2 * mid.size * chans * 6, 6 * mid.size),
        name="second",
    )(ids, mid, halo, w_second)


def ending_kernel(factor, ids, *refs):
    own, got = refs[0:CHUNKS], refs[CHUNKS : 2 * CHUNKS]
    latents, cotangent, slope, weights, out, sums, pad, pairs, frame, beside, total = refs[
        2 * CHUNKS :
    ]
    at = pl.program_id(0)
    core, role = ids[1], ids[5]
    rows, width, chans = frame.shape
    half = rows // 2
    step = half // 2
    piece = half // CHUNKS

    @pl.when(at == 0)
    def _():
        zero_borders(pad, pairs)
        total[...] = jnp.zeros_like(total)

    for chunk in range(CHUNKS):
        frame[pl.ds(core * half + chunk * piece, piece)] = own[chunk][0]
        frame[pl.ds(half - core * half + chunk * piece, piece)] = got[chunk][0]

    @pl.when(role == 1)
    def _():
        frame[...] = (frame[...].astype(F32) * slope[0].astype(F32)).astype(BF)

    fill_pairs(frame, pad, pairs)
    valid = jnp.where(at < ids[2], 1.0, 0.0).astype(F32)

    @pl.when(role == 0)
    def _():
        masked = (cotangent[0].astype(F32) * valid).astype(BF)
        masked = masked.reshape(half, 2, width, chans)
        beside[:, :, 0:chans] = masked[:, 0]
        beside[:, :, chans : 2 * chans] = masked[:, 1]
        frame[...] = latents[0]

    @pl.when(role == 1)
    def _():
        plain = latents[0].reshape(half, 2, width, chans)
        beside[:, :, 0:chans] = plain[:, 0]
        beside[:, :, chans : 2 * chans] = plain[:, 1]
        frame[...] = cotangent[0]

    scale = jnp.where(role == 0, valid, 1.0).astype(F32)
    for part in range(2):
        made = two_row_conv(pairs, weights, part * step, step) * scale
        made = made.reshape(step, width, 2 * chans)
        for pair in range(step):
            for odd in range(2):
                row = part * half + 2 * pair + odd
                plus = frame[row].astype(F32) * valid
                out[0, row] = (plus + made[pair, :, odd * chans : odd * chans + chans]).astype(BF)

    lanes = pairs.shape[2]
    flat = beside[...].reshape(half * width, 2 * chans)
    for part in range(2):
        seen = pairs[part : part + half].reshape(half * width, lanes)
        total[:, part * lanes : (part + 1) * lanes] += outer(flat, seen)

    @pl.when(at == pl.num_programs(0) - 1)
    def _():
        span = 9 * chans
        sums[...] = factor * (
            total[0:chans, 0:span] + total[chans : 2 * chans, 3 * chans : 3 * chans + span]
        )


def ending(factor, ids, own, got, latents, cotangent, slope, weights):
    slots, rows, width, chans = latents.shape
    half = rows // 2
    whole = pl.BlockSpec((1, rows, width, chans), lambda i, ids: (i, 0, 0, 0))
    part = pl.BlockSpec((1, half // CHUNKS, width, chans), lambda i, ids: (i, 0, 0, 0))
    gated = pl.BlockSpec((1, rows, width, chans), lambda i, ids: (i * ids[5], 0, 0, 0))
    return pl.pallas_call(
        functools.partial(ending_kernel, factor),
        grid_spec=pltpu.PrefetchScalarGridSpec(
            num_scalar_prefetch=1,
            grid=(slots,),
            in_specs=[part] * (2 * CHUNKS)
            + [whole, whole, gated, pl.BlockSpec(weights.shape, lambda i, ids: (0, 0))],
            out_specs=[whole, pl.BlockSpec((chans, 9 * chans), lambda i, ids: (0, 0))],
            scratch_shapes=[
                pltpu.VMEM((rows, width + 16, chans), F32),
                pltpu.VMEM((half + 1, width, 6 * chans), BF),
                pltpu.VMEM((rows, width, chans), BF),
                pltpu.VMEM((half, width, 2 * chans), BF),
                pltpu.VMEM((2 * chans, 12 * chans), F32),
            ],
        ),
        out_shape=[
            jax.ShapeDtypeStruct(latents.shape, BF),
            jax.ShapeDtypeStruct((chans, 9 * chans), F32),
        ],
        compiler_params=params(),
        cost_estimate=cost(4 * latents.size * chans * 12, 10 * latents.size),
        name="ending",
    )(ids, *own, *got, latents, cotangent, slope, weights)


def two_row_weights(kernel):
    flat = kernel.reshape(-1, kernel.shape[3])
    shift = 3 * kernel.shape[2]
    return jnp.concatenate(
        [jnp.pad(flat, ((0, shift), (0, 0))), jnp.pad(flat, ((shift, 0), (0, 0)))], axis=1
    )


def turned(kernel):
    return jnp.transpose(kernel[::-1, ::-1], (0, 1, 3, 2))


def flips(dp_size, tm_size):
    count = dp_size * tm_size
    digit = 1
    result = []
    while digit < count:
        result.append([(place, place ^ digit) for place in range(count)])
        digit *= 2
    return result


def halve(values, digits, pairs, place):
    for digit in digits:
        size = values.shape[0] // 2
        upper = (place >> digit) & 1
        keep = lax.dynamic_slice_in_dim(values, upper * size, size, 0)
        send = lax.dynamic_slice_in_dim(values, (1 - upper) * size, size, 0)
        values = keep + lax.ppermute(send, ("dp", "tm"), pairs[digit])
    return values


def double(values, digits, pairs, place, axis=0):
    for digit in digits:
        upper = (place >> digit) & 1
        other = lax.ppermute(values, ("dp", "tm"), pairs[digit])
        values = jnp.where(
            upper == 0,
            jnp.concatenate([values, other], axis),
            jnp.concatenate([other, values], axis),
        )
    return values


def on_chip_pair(
    dp_size,
    latents,
    cotangent,
    first_spatial,
    last_spatial,
    first_temporal,
    second_temporal,
    frame_counts,
    dilations,
):
    latents, cotangent = latents[0], cotangent[0]
    slots, rows, width, chans = latents.shape
    half = rows // 2
    tm_index = lax.axis_index("tm")
    side, core = tm_index // 2, tm_index % 2
    factor = float(dp_size * 4 * slots * rows * width) ** (-0.5)

    def ids_for(role):
        return jnp.stack(
            [side, core, frame_counts[0] - tm_index * slots, dilations[0], dilations[1], role]
        ).astype(jnp.int32)

    ids = ids_for(side)
    swap_cores = [(0, 1), (1, 0), (2, 3), (3, 2)]
    swap_sides = [(0, 2), (2, 0), (1, 3), (3, 1)]

    w_in = two_row_weights(first_spatial)
    w_out = two_row_weights(last_spatial)
    w_in_back = two_row_weights(turned(first_spatial))
    w_out_back = two_row_weights(turned(last_spatial))
    w_one = first_temporal.reshape(-1, chans)
    w_two = second_temporal.reshape(-1, chans)
    w_one_back = jnp.transpose(first_temporal, (0, 2, 1)).reshape(-1, chans)
    w_two_back = jnp.transpose(second_temporal, (0, 2, 1)).reshape(-1, chans)
    at_zero = side == 0

    act_own, act_send, back_own, back_send, slope = front(
        ids, latents, cotangent, w_in, w_out_back
    )
    act_got = lax.ppermute(act_send, "tm", swap_cores)
    back_got = lax.ppermute(back_send, "tm", swap_cores)

    size = half // CHUNKS
    tail = REACH - slots
    middles = []
    for chunk in range(CHUNKS):
        low = chunk * size
        pieces = [value[:, low : low + size] for value in (act_own, act_got, back_own, back_got)]
        act_low = jnp.where(core == 0, pieces[0][slots - tail :], pieces[1][slots - tail :])
        act_high = jnp.where(core == 0, pieces[1], pieces[0])
        back_low = jnp.where(core == 0, pieces[2], pieces[3])
        back_high = jnp.where(core == 0, pieces[3][:tail], pieces[2][:tail])
        leaving = jnp.where(
            at_zero,
            jnp.concatenate([act_low, act_high], 0),
            jnp.concatenate([back_low, back_high], 0),
        )
        halo = lax.ppermute(leaving, "tm", swap_sides)
        middles.append(
            middle(
                chunk, ids, act_own, act_got, back_own, back_got, halo,
                w_one, w_two_back, jnp.where(at_zero, w_two, w_one_back),
            )
        )
    halos = [lax.ppermute(made[0], "tm", swap_sides) for made in middles]

    first_own = [made[2] for made in middles]
    first_got = [lax.ppermute(made[3], "tm", swap_cores) for made in middles]
    out_first, sums_first = ending(
        factor, ids, first_own, first_got, latents, cotangent, slope,
        jnp.where(at_zero, w_out, w_in_back),
    )

    w_second = jnp.where(at_zero, w_one_back, w_two)
    seconds = [second(ids, made[1], halo, w_second) for made, halo in zip(middles, halos)]
    second_own = [made[0] for made in seconds]
    second_got = [lax.ppermute(made[1], "tm", swap_cores) for made in seconds]
    out_second, sums_second = ending(
        factor, ids_for(1 - side), second_own, second_got, latents, cotangent, slope,
        jnp.where(at_zero, w_in_back, w_out),
    )

    pairs = flips(dp_size, 4)
    place = lax.axis_index("dp") * 4 + tm_index
    digits = [0] + list(range(2, len(pairs)))
    temporal_sums = factor * jnp.concatenate(
        [sum(made[4] for made in middles), sum(made[5] for made in middles)], 0
    )
    temporal_sums = halve(temporal_sums, digits + [1], pairs, place)
    temporal_sums = double(temporal_sums, [1] + digits[::-1], pairs, place)
    early = halve(sums_first, digits, pairs, place)
    late = halve(sums_second, digits, pairs, place)
    both = jnp.stack([early, late])
    other = lax.ppermute(both, ("dp", "tm"), pairs[1])
    spatial_sums = jnp.where(
        at_zero,
        jnp.stack([early + other[1], late + other[0]]),
        jnp.stack([late + other[0], early + other[1]]),
    )
    spatial_sums = double(spatial_sums, digits[::-1], pairs, place, 1)

    decoded = jnp.where(at_zero, out_first, out_second)
    latent_grad = jnp.where(at_zero, out_second, out_first)
    last_grad = jnp.transpose(spatial_sums[0].reshape(chans, 3, 3, chans), (1, 2, 3, 0))
    first_grad = jnp.transpose(spatial_sums[1].reshape(chans, 3, 3, chans), (1, 2, 0, 3))
    first_grad = first_grad[::-1, ::-1]
    near_grad = jnp.transpose(temporal_sums[:chans].reshape(chans, TAPS, chans), (1, 2, 0))
    far_grad = jnp.transpose(temporal_sums[chans:].reshape(chans, TAPS, chans), (1, 0, 2))
    return (decoded[None], latent_grad[None], first_grad, last_grad, near_grad, far_grad)


def on_any_device(dp_size, tm_size, latents, cotangent, *rest):
    clips, slots, rows = latents.shape[:3]
    fits = clips == 1 and tm_size == 4 and slots <= REACH <= 2 * slots and rows % 8 == 0
    if fits and dp_size & (dp_size - 1) == 0:
        return on_chip_pair(dp_size, latents, cotangent, *rest)
    return on_device(latents, cotangent, *rest)


def solution(mesh):
    in_specs = (
        P("dp", "tm", None, None, None),
        P("dp", "tm", None, None, None),
        P(),
        P(),
        P(),
        P(),
        P("dp"),
        P(),
    )
    out_specs = (
        P("dp", "tm", None, None, None),
        P("dp", "tm", None, None, None),
        P(),
        P(),
        P(),
        P(),
    )
    return jax.shard_map(
        functools.partial(on_any_device, mesh.shape["dp"], mesh.shape["tm"]), mesh=mesh, in_specs=in_specs, out_specs=out_specs, check_vma=False
    )
```

```python
import functools

import jax
import jax.numpy as jnp
from jax import lax
from jax.experimental import pallas as pl
from jax.experimental.pallas import tpu as pltpu
from jax.sharding import PartitionSpec as P

TAPS = 3
DILATION_MAX = 4


def silu_slope(values):
    sigma = jax.nn.sigmoid(values)
    return sigma * (1.0 + values * (1.0 - sigma))


def spatial(source, kernel):
    row_count, col_count, channels = source.shape[-3:]
    leading = source.shape[:-3]
    padded = jnp.pad(source, [(0, 0)] * len(leading) + [(1, 1), (1, 1), (0, 0)])
    summed = jnp.zeros(leading + (row_count, col_count, kernel.shape[3]), jnp.float32)
    for row_shift in range(3):
        for col_shift in range(3):
            window = padded[
                ..., row_shift : row_shift + row_count, col_shift : col_shift + col_count, :
            ]
            product = jnp.dot(
                window.reshape(-1, channels),
                kernel[row_shift, col_shift],
                preferred_element_type=jnp.float32,
            )
            summed = summed + product.reshape(summed.shape)
    return summed


def spatial_back(incoming, kernel):
    return spatial(incoming, jnp.transpose(kernel[::-1, ::-1], (0, 1, 3, 2)))


def spatial_kernel(source, incoming):
    row_count, col_count, channels = source.shape[-3:]
    leading = source.shape[:-3]
    padded = jnp.pad(source, [(0, 0)] * len(leading) + [(1, 1), (1, 1), (0, 0)])
    flat_in = incoming.reshape(-1, incoming.shape[-1])
    result_rows = []
    for row_shift in range(3):
        result_cols = []
        for col_shift in range(3):
            window = padded[
                ..., row_shift : row_shift + row_count, col_shift : col_shift + col_count, :
            ]
            result_cols.append(
                lax.dot_general(
                    window.reshape(-1, channels),
                    flat_in,
                    (((0,), (0,)), ((), ())),
                    preferred_element_type=jnp.float32,
                )
            )
        result_rows.append(jnp.stack(result_cols))
    return jnp.stack(result_rows)


def temporal(source, kernel, dilation):
    margin = (TAPS - 1) * DILATION_MAX
    slot_count = source.shape[1]
    padded = jnp.pad(source, ((0, 0), (margin, 0), (0, 0), (0, 0), (0, 0)))
    summed = jnp.zeros(source.shape[:-1] + (kernel.shape[2],), jnp.float32)
    for tap_index in range(kernel.shape[0]):
        begin_at = margin - tap_index * dilation
        window = lax.dynamic_slice_in_dim(padded, begin_at, slot_count, 1)
        product = jnp.dot(
            window.reshape(-1, source.shape[-1]),
            kernel[tap_index],
            preferred_element_type=jnp.float32,
        )
        summed = summed + product.reshape(summed.shape)
    return summed


def temporal_back(incoming, kernel, dilation):
    margin = (TAPS - 1) * DILATION_MAX
    slot_count = incoming.shape[1]
    padded = jnp.pad(incoming, ((0, 0), (0, margin), (0, 0), (0, 0), (0, 0)))
    summed = jnp.zeros(incoming.shape[:-1] + (kernel.shape[1],), jnp.float32)
    for tap_index in range(kernel.shape[0]):
        begin_at = tap_index * dilation
        window = lax.dynamic_slice_in_dim(padded, begin_at, slot_count, 1)
        product = jnp.dot(
            window.reshape(-1, incoming.shape[-1]),
            kernel[tap_index].T,
            preferred_element_type=jnp.float32,
        )
        summed = summed + product.reshape(summed.shape)
    return summed


def temporal_kernel(source, incoming, dilation):
    margin = (TAPS - 1) * DILATION_MAX
    slot_count = source.shape[1]
    padded = jnp.pad(source, ((0, 0), (margin, 0), (0, 0), (0, 0), (0, 0)))
    flat_in = incoming.reshape(-1, incoming.shape[-1])
    result = []
    for tap_index in range(TAPS):
        begin_at = margin - tap_index * dilation
        window = lax.dynamic_slice_in_dim(padded, begin_at, slot_count, 1)
        result.append(
            lax.dot_general(
                window.reshape(-1, source.shape[-1]),
                flat_in,
                (((0,), (0,)), ((), ())),
                preferred_element_type=jnp.float32,
            )
        )
    return jnp.stack(result)


def forward_bands(band_in, first_temporal, second_temporal, dilations):
    pre_mid = temporal(band_in, first_temporal, dilations[0])
    act_mid = jax.nn.silu(pre_mid).astype(jnp.bfloat16)
    act_out = temporal(act_mid, second_temporal, dilations[1]).astype(jnp.bfloat16)
    return (pre_mid, act_mid, act_out)


def on_device(
    latents,
    cotangent,
    first_spatial,
    last_spatial,
    first_temporal,
    second_temporal,
    frame_counts,
    dilations,
):
    local_slots = latents.shape[1]
    first_slot = lax.axis_index("tm") * local_slots
    slot_ids = first_slot + jnp.arange(local_slots, dtype=jnp.int32)
    is_valid = (slot_ids[None, :] < frame_counts[:, None])[:, :, None, None, None]
    total_count = (
        latents.shape[0]
        * lax.axis_size("dp")
        * local_slots
        * lax.axis_size("tm")
        * latents.shape[2]
        * latents.shape[3]
    )
    factor = float(total_count) ** (-0.5)
    pre_in = spatial(latents, first_spatial)
    act_in = jax.nn.silu(pre_in).astype(jnp.bfloat16)
    masked = jnp.where(is_valid, cotangent, jnp.zeros_like(cotangent))
    band_in = lax.all_to_all(act_in, "tm", split_axis=2, concat_axis=1, tiled=True)
    pre_mid, act_mid, act_out = forward_bands(band_in, first_temporal, second_temporal, dilations)
    back_out = spatial_back(masked, last_spatial).astype(jnp.bfloat16)
    band_back = lax.all_to_all(back_out, "tm", split_axis=2, concat_axis=1, tiled=True)
    second_grad = temporal_kernel(act_mid, band_back, dilations[1])
    slope_mid = (
        temporal_back(band_back, second_temporal, dilations[1]) * silu_slope(pre_mid)
    ).astype(jnp.bfloat16)
    first_grad = temporal_kernel(band_in, slope_mid, dilations[0])
    back_in = temporal_back(slope_mid, first_temporal, dilations[0]).astype(jnp.bfloat16)
    frame_out, frame_back = (
        lax.all_to_all(act_out, "tm", split_axis=1, concat_axis=2, tiled=True),
        lax.all_to_all(back_in, "tm", split_axis=1, concat_axis=2, tiled=True),
    )
    decoded = jnp.where(
        is_valid, latents.astype(jnp.float32) + spatial(frame_out, last_spatial), jnp.float32(0.0)
    ).astype(jnp.bfloat16)
    last_grad = spatial_kernel(frame_out, masked)
    slope_in = (frame_back.astype(jnp.float32) * silu_slope(pre_in)).astype(jnp.bfloat16)
    spatial_grad = spatial_kernel(latents, slope_in)
    latent_grad = (masked.astype(jnp.float32) + spatial_back(slope_in, first_spatial)).astype(
        jnp.bfloat16
    )
    partials = (
        factor * spatial_grad,
        factor * last_grad,
        factor * first_grad,
        factor * second_grad,
    )
    reduced = lax.psum((partials[0], partials[1], partials[2], partials[3]), ("dp", "tm"))
    return (decoded, latent_grad, reduced[0], reduced[1], reduced[2], reduced[3])


REACH = (TAPS - 1) * DILATION_MAX
CHUNKS = 2
VMEM_LIMIT = 56 * 1024 * 1024
BF = jnp.bfloat16
F32 = jnp.float32


def params():
    return pltpu.CompilerParams(
        dimension_semantics=("arbitrary",), vmem_limit_bytes=VMEM_LIMIT
    )


COST = 0.1


def cost(micros):
    return pl.CostEstimate(flops=int(micros * COST * 1e9), bytes_accessed=1000, transcendentals=0)


def pair_range(chunk, rows):
    size = rows // CHUNKS
    low = 0 if chunk == 0 else chunk * size // 2 - 1
    high = rows // 2 if chunk == CHUNKS - 1 else (chunk + 1) * size // 2 - 1
    return low, high


def seen_rows(low, high, rows):
    return max(0, 2 * low - 1), min(rows, 2 * high + 1)


def zero_borders(pad, pairs, low, high, rows):
    pad[...] = jnp.zeros(pad.shape, F32)
    frames, _, width, lanes = pairs.shape
    for frame in range(frames):
        if low == 0:
            pairs[frame, 0, :, 0 : lanes // 2] = jnp.zeros((width, lanes // 2), BF)
        if 2 * high == rows:
            pairs[frame, high - low, :, lanes // 2 : lanes] = jnp.zeros((width, lanes // 2), BF)


def fill_pairs(read_row, pad, pairs, low, high, rows):
    frames, _, width, lanes = pairs.shape
    chans = lanes // 6
    begin, end = seen_rows(low, high, rows)
    for frame in range(frames):
        for row in range(begin, end):
            pad[frame, row - begin, 8 : 8 + width, :] = read_row(frame, row).astype(F32)
    for frame in range(frames):
        for row in range(begin, end):
            at = (row + 1) // 2 - low
            side = 3 * chans * (1 - row % 2)
            pairs[frame, at, :, side + chans : side + 2 * chans] = read_row(frame, row)
            for shift in (0, 2):
                seen = pad[frame, row - begin, 7 + shift : 7 + shift + width, :].astype(BF)
                lane = side + shift * chans
                pairs[frame, at, :, lane : lane + chans] = seen


def front_kernel(ids, *refs):
    latents, cotangent = refs[0:2], refs[2:4]
    w_in, w_back, act, back, slope, pad, pairs = refs[4:]
    at = pl.program_id(0)
    core, shift_rows = ids[1], ids[7]
    spread, width, chans = latents[0].shape[1:]
    count = spread // 2 - 1
    lanes = 6 * chans
    slots = pl.num_programs(0)

    @pl.when(at == 0)
    def _():
        pad[...] = jnp.zeros(pad.shape, F32)

    def conv(blocks, weights):
        for index in range(2):
            for row in range(spread):
                place = index * (spread + 2) + 1 + row
                pad[place, 8 : 8 + width, :] = blocks[index][0, row].astype(F32)
        for index in range(2):
            for row in range(spread):
                place = index * (spread + 2) + 1 + row + shift_rows
                side = 3 * chans * (row % 2)
                to = index * (count + 1) + row // 2
                for shift in range(3):
                    seen = pad[place, 7 + shift : 7 + shift + width, :].astype(BF)
                    pairs[to, :, side + shift * chans : side + (shift + 1) * chans] = seen
        stacked = []
        for lower in range(2):
            both = [
                pairs[index * (count + 1) + lower : index * (count + 1) + lower + count]
                for index in range(2)
            ]
            stacked.append(jnp.concatenate(both, axis=0).reshape(2 * count * width, lanes))
        return jnp.dot(
            jnp.concatenate(stacked, axis=1), weights[...], preferred_element_type=F32
        )

    def store(target, values):
        values = values.reshape(2 * count, width, 2 * chans)
        for index in range(2):
            owner = core if index == 0 else 1 - core
            for row in range(2 * count):
                lane = row % 2 * chans
                target[owner, 0, row] = values[index * count + row // 2, :, lane : lane + chans]

    pre = conv(latents, w_in)
    sigma = jax.nn.sigmoid(pre)
    store(act, (pre * sigma).astype(BF))
    store(slope, (sigma * (1.0 + pre * (1.0 - sigma))).astype(BF))
    summed = conv(cotangent, w_back)
    half = count * width
    mine = jnp.where(core * slots + at < ids[2], 1.0, 0.0).astype(F32)
    other = jnp.where((1 - core) * slots + at < ids[2], 1.0, 0.0).astype(F32)
    store(back, jnp.concatenate([summed[:half] * mine, summed[half:] * other], 0).astype(BF))


def front(ids, latents, cotangent, w_in, w_back):
    slots, spread, width, chans = latents[1].shape
    rows = spread - 2
    own = pl.BlockSpec(
        (pl.Element(1), pl.Element(spread), pl.Element(width), pl.Element(chans)),
        lambda i, ids: (i, ids[6], 0, 0),
    )
    got = pl.BlockSpec((1, spread, width, chans), lambda i, ids: (i, 0, 0, 0))
    target = pl.BlockSpec((2, 1, rows, width, chans), lambda i, ids: (0, i, 0, 0, 0))
    fixed = pl.BlockSpec(w_in.shape, lambda i, ids: (0, 0))
    made = pl.pallas_call(
        front_kernel,
        grid_spec=pltpu.PrefetchScalarGridSpec(
            num_scalar_prefetch=1,
            grid=(slots,),
            in_specs=[own, got, own, got, fixed, fixed],
            out_specs=[target] * 3,
            scratch_shapes=[
                pltpu.VMEM((2 * (spread + 2), width + 16, chans), F32),
                pltpu.VMEM((spread, width, 6 * chans), BF),
            ],
        ),
        out_shape=[jax.ShapeDtypeStruct((2, slots, rows, width, chans), BF)] * 3,
        compiler_params=params(),
        cost_estimate=cost(22.0 / CHUNKS),
        name="front",
    )(ids, *latents, *cotangent, w_in, w_back)
    return [value.reshape(2 * slots, rows, width, chans) for value in made]


def taps_of(held, start, step, count):
    size = held.shape[1]
    chans = held.shape[2]
    seen = []
    for tap in range(TAPS):
        seen.append(held[pl.ds(start + tap * step, count)].reshape(count * size, chans))
    return jnp.concatenate(seen, axis=1)


def outer(left, right):
    return lax.dot_general(left, right, (((0,), (0,)), ((), ())), preferred_element_type=F32)


def middle_kernel(
    ids, act_in, act_back, slope, halo, w_mid, w_mid_back, w_first,
    mid_send, mid_keep, first_keep, first_send, grad_first, grad_second,
    held_in, held_back, held_mid, result,
):
    at = pl.program_id(0)
    side, core, near, far = ids[0], ids[1], ids[3], ids[4]
    frames = act_in.shape[0]
    slots = frames // 2
    mine = core * slots
    other = slots - mine

    @pl.when(at == 0)
    def _():
        blank = jnp.zeros((REACH,) + held_in.shape[1:], BF)
        held_in[0:REACH] = blank
        held_back[frames : frames + REACH] = blank
        held_mid[0:REACH] = blank
        held_mid[REACH + frames : 2 * REACH + frames] = blank
        grad_first[...] = jnp.zeros_like(grad_first)
        grad_second[...] = jnp.zeros_like(grad_second)

    held_in[REACH : REACH + frames] = act_in[:, 0]
    held_back[0:frames] = act_back[:, 0]

    @pl.when(side == 0)
    def _():
        held_back[frames : frames + REACH] = halo[:, 0]

    @pl.when(side == 1)
    def _():
        held_in[0:REACH] = halo[:, 0]

    size, chans = held_in.shape[1:]
    taps_in = taps_of(held_in, REACH, -near, frames)
    taps_back = taps_of(held_back, 0, far, frames)
    pre = jnp.dot(taps_in, w_mid[...], preferred_element_type=F32)
    sigma = jax.nn.sigmoid(pre)
    act = (pre * sigma).astype(BF)
    back = jnp.dot(taps_back, w_mid_back[...], preferred_element_type=F32)
    grad = (back * (sigma * (1.0 + pre * (1.0 - sigma)))).astype(BF)
    grad_second[...] += outer(act, taps_back)
    grad_first[...] += outer(grad, taps_in)
    act = act.reshape(frames, size, chans)
    grad = grad.reshape(frames, size, chans)

    @pl.when(side == 0)
    def _():
        held_mid[REACH : REACH + frames] = act
        mid_keep[:, 0] = grad
        mid_send[:, 0] = act[frames - REACH :]

    @pl.when(side == 1)
    def _():
        held_mid[REACH : REACH + frames] = grad
        mid_keep[:, 0] = act
        mid_send[:, 0] = grad[:REACH]

    step = jnp.where(side == 0, -far, near)
    first = jnp.dot(
        taps_of(held_mid, REACH, step, frames), w_first[...], preferred_element_type=F32
    )
    result[...] = first.astype(BF).reshape(frames, size, chans)

    @pl.when(side == 1)
    def _():
        result[...] = (result[...].astype(F32) * slope[:, 0].astype(F32)).astype(BF)

    first_keep[:, 0] = result[pl.ds(mine, slots)]
    first_send[:, 0] = result[pl.ds(other, slots)]


def middle(ids, act_in, act_back, slope, halo, w_mid, w_mid_back, w_first):
    frames, rows, width, chans = act_in.shape
    slots = frames // 2
    fixed = pl.BlockSpec(w_mid.shape, lambda i, ids: (0, 0))
    sums = pl.BlockSpec((chans, TAPS * chans), lambda i, ids: (0, 0))

    def rowwise(count):
        return pl.BlockSpec((count, 1, width, chans), lambda i, ids: (0, i, 0, 0))

    def shaped(count):
        return jax.ShapeDtypeStruct((count, rows, width, chans), BF)

    summed = jax.ShapeDtypeStruct((chans, TAPS * chans), F32)
    return pl.pallas_call(
        middle_kernel,
        grid_spec=pltpu.PrefetchScalarGridSpec(
            num_scalar_prefetch=1,
            grid=(rows,),
            in_specs=[rowwise(frames)] * 3 + [rowwise(REACH), fixed, fixed, fixed],
            out_specs=[
                rowwise(REACH), rowwise(frames), rowwise(slots), rowwise(slots), sums, sums,
            ],
            scratch_shapes=[
                pltpu.VMEM((REACH + frames, width, chans), BF),
                pltpu.VMEM((REACH + frames, width, chans), BF),
                pltpu.VMEM((2 * REACH + frames, width, chans), BF),
                pltpu.VMEM((frames, width, chans), BF),
            ],
        ),
        out_shape=[
            shaped(REACH), shaped(frames), shaped(slots), shaped(slots), summed, summed,
        ],
        compiler_params=params(),
        cost_estimate=cost(24.0 / CHUNKS),
        name="middle",
    )(ids, act_in, act_back, slope, halo, w_mid, w_mid_back, w_first)


def second_kernel(ids, mid, slope, halo, w_second, keep, send, held, result):
    at = pl.program_id(0)
    side, core, near, far = ids[0], ids[1], ids[3], ids[4]
    frames = mid.shape[0]
    slots = frames // 2
    mine = core * slots

    @pl.when(at == 0)
    def _():
        blank = jnp.zeros((REACH,) + held.shape[1:], BF)
        held[0:REACH] = blank
        held[REACH + frames : 2 * REACH + frames] = blank

    held[REACH : REACH + frames] = mid[:, 0]

    @pl.when(side == 0)
    def _():
        held[REACH + frames : 2 * REACH + frames] = halo[:, 0]

    @pl.when(side == 1)
    def _():
        held[0:REACH] = halo[:, 0]

    step = jnp.where(side == 0, near, -far)
    made = jnp.dot(
        taps_of(held, REACH, step, frames), w_second[...], preferred_element_type=F32
    )
    result[...] = made.astype(BF).reshape(result.shape)

    @pl.when(side == 0)
    def _():
        result[...] = (result[...].astype(F32) * slope[:, 0].astype(F32)).astype(BF)

    keep[:, 0] = result[pl.ds(mine, slots)]
    send[:, 0] = result[pl.ds(slots - mine, slots)]


def second(ids, mid, slope, halo, w_second):
    frames, rows, width, chans = mid.shape
    slots = frames // 2

    def rowwise(count):
        return pl.BlockSpec((count, 1, width, chans), lambda i, ids: (0, i, 0, 0))

    shape = jax.ShapeDtypeStruct((slots, rows, width, chans), BF)
    return pl.pallas_call(
        second_kernel,
        grid_spec=pltpu.PrefetchScalarGridSpec(
            num_scalar_prefetch=1,
            grid=(rows,),
            in_specs=[
                rowwise(frames), rowwise(frames), rowwise(REACH),
                pl.BlockSpec(w_second.shape, lambda i, ids: (0, 0)),
            ],
            out_specs=[rowwise(slots), rowwise(slots)],
            scratch_shapes=[
                pltpu.VMEM((2 * REACH + frames, width, chans), BF),
                pltpu.VMEM((frames, width, chans), BF),
            ],
        ),
        out_shape=[shape, shape],
        compiler_params=params(),
        cost_estimate=cost(10.0 / CHUNKS),
        name="second",
    )(ids, mid, slope, halo, w_second)


def ending_kernel(chunk, rows, factor, with_outs, ids, *refs):
    refs = list(refs)
    used = 1 if chunk == 0 else 2
    own = [refs.pop(0) for _ in range(used)]
    got = [refs.pop(0) for _ in range(used)]
    latents, cotangent, weights, before = [refs.pop(0) for _ in range(4)]
    if with_outs:
        refs.pop(0), refs.pop(0)
    outs = (refs.pop(0), refs.pop(0))
    sums, pad, pairs, frame, buffer, sems, beside, total = refs
    at = pl.program_id(0)
    last = pl.num_programs(0) - 1
    core, role = ids[1], ids[5]
    frames, _, width, lanes = pairs.shape
    chans = lanes // 6
    low, high = pair_range(chunk, rows)
    size = rows // CHUNKS
    half = size // 2
    base = (chunk + 1 - used) * size
    count = high - low

    def each_copy(step, act):
        for way in range(2):
            @pl.when(role == way)
            def _():
                target = outs[way].at[pl.ds(step * frames, frames), pl.ds(2 * low, 2 * count)]
                act(pltpu.make_async_copy(buffer.at[step % 2], target, sems.at[step % 2]))

    @pl.when(at == 0)
    def _():
        zero_borders(pad, pairs, low, high, rows)
        total[...] = jnp.zeros_like(total)

    @pl.when(at >= 2)
    def _():
        each_copy(at - 2, lambda copy: copy.wait())

    for index in range(used):
        frame[:, pl.ds(index * size + core * half, half)] = own[index][...]
        frame[:, pl.ds(index * size + half - core * half, half)] = got[index][...]
    fill_pairs(lambda which, row: frame[which, row - base], pad, pairs, low, high, rows)
    slot = at % 2
    one = jnp.where(role == 1, 1.0, 0.0).astype(F32)
    for which in range(frames):
        place = (core * (last + 1) + at) * frames + which
        valid = jnp.where(place < ids[2], 1.0, 0.0).astype(F32)
        zero = (1.0 - one) * valid
        upper = pairs[which, 0:count].reshape(count * width, lanes)
        lower = pairs[which, 1 : 1 + count].reshape(count * width, lanes)
        made = jnp.dot(
            jnp.concatenate([upper, lower], axis=1), weights[...], preferred_element_type=F32
        )
        made = made.reshape(count, width, 2 * chans)
        for row in range(2 * count):
            lane = row % 2 * chans
            latent = latents[which, row].astype(F32)
            arriving = cotangent[which, row].astype(F32)
            beside[which, row // 2, :, lane : lane + chans] = (
                latent * one + arriving * zero
            ).astype(BF)
            buffer[slot, which, row] = (
                latent * zero
                + arriving * (one * valid)
                + made[row // 2, :, lane : lane + chans] * (one + zero)
            ).astype(BF)
    flat = beside[...].reshape(frames * count * width, 2 * chans)
    for part in range(2):
        seen = pairs[:, part : part + count].reshape(frames * count * width, lanes)
        total[:, part * lanes : (part + 1) * lanes] += outer(flat, seen)
    each_copy(at, lambda copy: copy.start())

    @pl.when(at == last)
    def _():
        span = 9 * chans
        sums[...] = before[...] + factor * (
            total[0:chans, 0:span] + total[chans : 2 * chans, 3 * chans : 3 * chans + span]
        )
        each_copy(at - 1, lambda copy: copy.wait())
        each_copy(at, lambda copy: copy.wait())


def ending(chunk, factor, ids, own, got, latents, cotangent, weights, before, outs=None):
    slots, rows, width, chans = latents.shape
    size = rows // CHUNKS
    low, high = pair_range(chunk, rows)
    count = high - low
    begin, end = seen_rows(low, high, rows)
    used = 1 if chunk == 0 else 2
    each = 2
    area = pl.BlockSpec(
        (pl.Element(each), pl.Element(2 * count), pl.Element(width), pl.Element(chans)),
        lambda i, ids: (i * each, 2 * low, 0, 0),
    )
    part = pl.BlockSpec((each, size // 2, width, chans), lambda i, ids: (i, 0, 0, 0))
    summed = pl.BlockSpec((chans, 9 * chans), lambda i, ids: (0, 0))
    anywhere = pl.BlockSpec(memory_space=pl.ANY)
    pick = slice(chunk + 1 - used, chunk + 1)
    args = [*own[pick], *got[pick], latents, cotangent, weights, before]
    in_specs = [part] * (2 * used) + [area, area]
    in_specs += [pl.BlockSpec(weights.shape, lambda i, ids: (0, 0)), summed]
    aliases = {}
    if outs is not None:
        aliases = {1 + len(args): 0, 2 + len(args): 1}
        args += list(outs)
        in_specs += [anywhere, anywhere]
    return pl.pallas_call(
        functools.partial(ending_kernel, chunk, rows, factor, outs is not None),
        grid_spec=pltpu.PrefetchScalarGridSpec(
            num_scalar_prefetch=1,
            grid=(slots // each,),
            in_specs=in_specs,
            out_specs=[anywhere, anywhere, summed],
            scratch_shapes=[
                pltpu.VMEM((each, end - begin, width + 16, chans), F32),
                pltpu.VMEM((each, count + 1, width, 6 * chans), BF),
                pltpu.VMEM((each, used * size, width, chans), BF),
                pltpu.VMEM((2, each, 2 * count, width, chans), BF),
                pltpu.SemaphoreType.DMA((2,)),
                pltpu.VMEM((each, count, width, 2 * chans), BF),
                pltpu.VMEM((2 * chans, 12 * chans), F32),
            ],
        ),
        out_shape=[
            jax.ShapeDtypeStruct(latents.shape, BF),
            jax.ShapeDtypeStruct(latents.shape, BF),
            jax.ShapeDtypeStruct((chans, 9 * chans), F32),
        ],
        input_output_aliases=aliases,
        compiler_params=params(),
        cost_estimate=cost(26.0 / CHUNKS),
        name="ending",
    )(ids, *args)


def two_row_weights(kernel):
    flat = kernel.reshape(-1, kernel.shape[3])
    shift = 3 * kernel.shape[2]
    return jnp.concatenate(
        [jnp.pad(flat, ((0, shift), (0, 0))), jnp.pad(flat, ((shift, 0), (0, 0)))], axis=1
    )


def after(value, *earlier):
    return lax.optimization_barrier((value,) + earlier)[0]


def turned(kernel):
    return jnp.transpose(kernel[::-1, ::-1], (0, 1, 3, 2))


def flips(dp_size, tm_size):
    count = dp_size * tm_size
    digit = 1
    result = []
    while digit < count:
        result.append([(place, place ^ digit) for place in range(count)])
        digit *= 2
    return result


def halve(values, digits, pairs, place):
    for digit in digits:
        size = values.shape[0] // 2
        upper = (place >> digit) & 1
        keep = lax.dynamic_slice_in_dim(values, upper * size, size, 0)
        send = lax.dynamic_slice_in_dim(values, (1 - upper) * size, size, 0)
        values = keep + lax.ppermute(send, ("dp", "tm"), pairs[digit])
    return values


def double(values, digits, pairs, place, axis=0):
    for digit in digits:
        upper = (place >> digit) & 1
        other = lax.ppermute(values, ("dp", "tm"), pairs[digit])
        values = jnp.where(
            upper == 0,
            jnp.concatenate([values, other], axis),
            jnp.concatenate([other, values], axis),
        )
    return values


def on_chip_pair(
    dp_size,
    latents,
    cotangent,
    first_spatial,
    last_spatial,
    first_temporal,
    second_temporal,
    frame_counts,
    dilations,
):
    latents, cotangent = latents[0], cotangent[0]
    slots, rows, width, chans = latents.shape
    half = rows // 2
    tm_index = lax.axis_index("tm")
    side, core = tm_index // 2, tm_index % 2
    factor = float(dp_size * 4 * slots * rows * width) ** (-0.5)

    def ids_for(role):
        return jnp.stack(
            [side, core, frame_counts[0] - side * 2 * slots, dilations[0], dilations[1], role]
        ).astype(jnp.int32)

    ids = ids_for(side)
    swap_cores = [(0, 1), (1, 0), (2, 3), (3, 2)]
    swap_sides = [(0, 2), (2, 0), (1, 3), (3, 1)]

    w_in = two_row_weights(first_spatial)
    w_out = two_row_weights(last_spatial)
    w_in_back = two_row_weights(turned(first_spatial))
    w_out_back = two_row_weights(turned(last_spatial))
    w_one = first_temporal.reshape(-1, chans)
    w_two = second_temporal.reshape(-1, chans)
    w_one_back = jnp.transpose(first_temporal, (0, 2, 1)).reshape(-1, chans)
    w_two_back = jnp.transpose(second_temporal, (0, 2, 1)).reshape(-1, chans)
    at_zero = side == 0
    w_first = jnp.where(at_zero, w_two, w_one_back)
    w_second = jnp.where(at_zero, w_one_back, w_two)
    w_ending = jnp.where(at_zero, w_out, w_in_back)
    w_other = jnp.where(at_zero, w_in_back, w_out)

    band = rows // CHUNKS // 2
    got = []
    for chunk in range(CHUNKS):
        start = chunk * 2 * band + (1 - core) * band - 1
        sent = [
            lax.dynamic_slice_in_dim(value, jnp.clip(start, 0, rows - band - 2), band + 2, 1)
            for value in (latents, cotangent)
        ]
        if chunk > 0:
            sent = [after(value, *got[0]) for value in sent]
        got.append([lax.ppermute(value, "tm", swap_cores) for value in sent])
    middles, slopes = [], []
    for chunk in range(CHUNKS):
        start = chunk * 2 * band + core * band - 1
        kept = jnp.clip(start, 0, rows - band - 2)
        front_ids = jnp.concatenate([ids, jnp.stack([kept, start - kept]).astype(jnp.int32)])
        act, back, slope = front(
            front_ids, [latents, got[chunk][0]], [cotangent, got[chunk][1]], w_in, w_out_back
        )
        slopes.append(slope)
        leaving = jnp.where(at_zero, act[2 * slots - REACH :], back[:REACH])
        if chunk > 0:
            leaving = after(leaving, halo)
        halo = lax.ppermute(leaving, "tm", swap_sides)
        middles.append(middle(ids, act, back, slope, halo, w_one, w_two_back, w_first))
    halos, own, got = [], [], []
    outs = None
    sums_first = jnp.zeros((chans, 9 * chans), F32)
    for chunk, made in enumerate(middles):
        halo = lax.ppermute(after(made[0], halo, sums_first), "tm", swap_sides)
        halos.append(halo)
        own.append(made[2])
        leaving = made[3] if chunk == 0 else after(made[3], sums_first)
        got.append(lax.ppermute(leaving, "tm", swap_cores))
        *outs, sums_first = ending(
            chunk, factor, ids, own, got, latents, cotangent, w_ending, sums_first, outs
        )

    halos[-1] = after(halos[-1], sums_first)
    seconds = [
        second(ids, made[1], slope, halo, w_second)
        for made, slope, halo in zip(middles, slopes, halos)
    ]
    own = [made[0] for made in seconds]
    got = [lax.ppermute(made[1], "tm", swap_cores) for made in seconds]
    ids = ids_for(1 - side)
    sums_second = jnp.zeros((chans, 9 * chans), F32)
    for chunk in range(CHUNKS):
        *outs, sums_second = ending(
            chunk, factor, ids, own, got, latents, cotangent, w_other, sums_second, outs
        )
    decoded, latent_grad = outs

    pairs = flips(dp_size, 4)
    place = lax.axis_index("dp") * 4 + tm_index
    digits = [0] + list(range(2, len(pairs)))
    span = 9 * chans
    early = jnp.concatenate(
        [
            sums_first,
            factor * sum(made[4] for made in middles),
            factor * sum(made[5] for made in middles),
        ],
        1,
    )
    early = after(early, halos[-2])
    early = halve(early, digits, pairs, place)
    late = halve(sums_second, digits, pairs, place)
    both = jnp.concatenate([early, late], 1)
    other = lax.ppermute(both, ("dp", "tm"), pairs[1])
    swapped = jnp.concatenate([other[:, -span:], other[:, span:-span], other[:, :span]], 1)
    both = both + swapped
    both = jnp.where(
        at_zero, both, jnp.concatenate([both[:, -span:], both[:, span:-span], both[:, :span]], 1)
    )
    both = double(both, digits[::-1], pairs, place)
    spatial_sums = (both[:, :span], both[:, -span:])
    temporal_sums = both[:, span:-span]

    last_grad = jnp.transpose(spatial_sums[0].reshape(chans, 3, 3, chans), (1, 2, 3, 0))
    first_grad = jnp.transpose(spatial_sums[1].reshape(chans, 3, 3, chans), (1, 2, 0, 3))
    first_grad = first_grad[::-1, ::-1]
    near_grad = jnp.transpose(temporal_sums[:, : TAPS * chans].reshape(chans, TAPS, chans), (1, 2, 0))
    far_grad = jnp.transpose(temporal_sums[:, TAPS * chans :].reshape(chans, TAPS, chans), (1, 0, 2))
    return (decoded[None], latent_grad[None], first_grad, last_grad, near_grad, far_grad)


def on_any_device(dp_size, tm_size, latents, cotangent, *rest):
    clips, slots, rows = latents.shape[:3]
    fits = clips == 1 and tm_size == 4 and slots <= REACH <= 2 * slots and rows % 8 == 0 and slots % 2 == 0
    if fits and dp_size & (dp_size - 1) == 0:
        return on_chip_pair(dp_size, latents, cotangent, *rest)
    return on_device(latents, cotangent, *rest)


def solution(mesh):
    in_specs = (
        P("dp", "tm", None, None, None),
        P("dp", "tm", None, None, None),
        P(),
        P(),
        P(),
        P(),
        P("dp"),
        P(),
    )
    out_specs = (
        P("dp", "tm", None, None, None),
        P("dp", "tm", None, None, None),
        P(),
        P(),
        P(),
        P(),
    )
    return jax.shard_map(
        functools.partial(on_any_device, mesh.shape["dp"], mesh.shape["tm"]), mesh=mesh, in_specs=in_specs, out_specs=out_specs, check_vma=False
    )
```

```python
import functools

import jax
import jax.numpy as jnp
from jax import lax
from jax.experimental import pallas as pl
from jax.experimental.pallas import tpu as pltpu
from jax.sharding import PartitionSpec as P

TAPS = 3
DILATION_MAX = 4


def silu_slope(values):
    sigma = jax.nn.sigmoid(values)
    return sigma * (1.0 + values * (1.0 - sigma))


def spatial(source, kernel):
    row_count, col_count, channels = source.shape[-3:]
    leading = source.shape[:-3]
    padded = jnp.pad(source, [(0, 0)] * len(leading) + [(1, 1), (1, 1), (0, 0)])
    summed = jnp.zeros(leading + (row_count, col_count, kernel.shape[3]), jnp.float32)
    for row_shift in range(3):
        for col_shift in range(3):
            window = padded[
                ..., row_shift : row_shift + row_count, col_shift : col_shift + col_count, :
            ]
            product = jnp.dot(
                window.reshape(-1, channels),
                kernel[row_shift, col_shift],
                preferred_element_type=jnp.float32,
            )
            summed = summed + product.reshape(summed.shape)
    return summed


def spatial_back(incoming, kernel):
    return spatial(incoming, jnp.transpose(kernel[::-1, ::-1], (0, 1, 3, 2)))


def spatial_kernel(source, incoming):
    row_count, col_count, channels = source.shape[-3:]
    leading = source.shape[:-3]
    padded = jnp.pad(source, [(0, 0)] * len(leading) + [(1, 1), (1, 1), (0, 0)])
    flat_in = incoming.reshape(-1, incoming.shape[-1])
    result_rows = []
    for row_shift in range(3):
        result_cols = []
        for col_shift in range(3):
            window = padded[
                ..., row_shift : row_shift + row_count, col_shift : col_shift + col_count, :
            ]
            result_cols.append(
                lax.dot_general(
                    window.reshape(-1, channels),
                    flat_in,
                    (((0,), (0,)), ((), ())),
                    preferred_element_type=jnp.float32,
                )
            )
        result_rows.append(jnp.stack(result_cols))
    return jnp.stack(result_rows)


def temporal(source, kernel, dilation):
    margin = (TAPS - 1) * DILATION_MAX
    slot_count = source.shape[1]
    padded = jnp.pad(source, ((0, 0), (margin, 0), (0, 0), (0, 0), (0, 0)))
    summed = jnp.zeros(source.shape[:-1] + (kernel.shape[2],), jnp.float32)
    for tap_index in range(kernel.shape[0]):
        begin_at = margin - tap_index * dilation
        window = lax.dynamic_slice_in_dim(padded, begin_at, slot_count, 1)
        product = jnp.dot(
            window.reshape(-1, source.shape[-1]),
            kernel[tap_index],
            preferred_element_type=jnp.float32,
        )
        summed = summed + product.reshape(summed.shape)
    return summed


def temporal_back(incoming, kernel, dilation):
    margin = (TAPS - 1) * DILATION_MAX
    slot_count = incoming.shape[1]
    padded = jnp.pad(incoming, ((0, 0), (0, margin), (0, 0), (0, 0), (0, 0)))
    summed = jnp.zeros(incoming.shape[:-1] + (kernel.shape[1],), jnp.float32)
    for tap_index in range(kernel.shape[0]):
        begin_at = tap_index * dilation
        window = lax.dynamic_slice_in_dim(padded, begin_at, slot_count, 1)
        product = jnp.dot(
            window.reshape(-1, incoming.shape[-1]),
            kernel[tap_index].T,
            preferred_element_type=jnp.float32,
        )
        summed = summed + product.reshape(summed.shape)
    return summed


def temporal_kernel(source, incoming, dilation):
    margin = (TAPS - 1) * DILATION_MAX
    slot_count = source.shape[1]
    padded = jnp.pad(source, ((0, 0), (margin, 0), (0, 0), (0, 0), (0, 0)))
    flat_in = incoming.reshape(-1, incoming.shape[-1])
    result = []
    for tap_index in range(TAPS):
        begin_at = margin - tap_index * dilation
        window = lax.dynamic_slice_in_dim(padded, begin_at, slot_count, 1)
        result.append(
            lax.dot_general(
                window.reshape(-1, source.shape[-1]),
                flat_in,
                (((0,), (0,)), ((), ())),
                preferred_element_type=jnp.float32,
            )
        )
    return jnp.stack(result)


def forward_bands(band_in, first_temporal, second_temporal, dilations):
    pre_mid = temporal(band_in, first_temporal, dilations[0])
    act_mid = jax.nn.silu(pre_mid).astype(jnp.bfloat16)
    act_out = temporal(act_mid, second_temporal, dilations[1]).astype(jnp.bfloat16)
    return (pre_mid, act_mid, act_out)


def on_device(
    latents,
    cotangent,
    first_spatial,
    last_spatial,
    first_temporal,
    second_temporal,
    frame_counts,
    dilations,
):
    local_slots = latents.shape[1]
    first_slot = lax.axis_index("tm") * local_slots
    slot_ids = first_slot + jnp.arange(local_slots, dtype=jnp.int32)
    is_valid = (slot_ids[None, :] < frame_counts[:, None])[:, :, None, None, None]
    total_count = (
        latents.shape[0]
        * lax.axis_size("dp")
        * local_slots
        * lax.axis_size("tm")
        * latents.shape[2]
        * latents.shape[3]
    )
    factor = float(total_count) ** (-0.5)
    pre_in = spatial(latents, first_spatial)
    act_in = jax.nn.silu(pre_in).astype(jnp.bfloat16)
    masked = jnp.where(is_valid, cotangent, jnp.zeros_like(cotangent))
    band_in = lax.all_to_all(act_in, "tm", split_axis=2, concat_axis=1, tiled=True)
    pre_mid, act_mid, act_out = forward_bands(band_in, first_temporal, second_temporal, dilations)
    back_out = spatial_back(masked, last_spatial).astype(jnp.bfloat16)
    band_back = lax.all_to_all(back_out, "tm", split_axis=2, concat_axis=1, tiled=True)
    second_grad = temporal_kernel(act_mid, band_back, dilations[1])
    slope_mid = (
        temporal_back(band_back, second_temporal, dilations[1]) * silu_slope(pre_mid)
    ).astype(jnp.bfloat16)
    first_grad = temporal_kernel(band_in, slope_mid, dilations[0])
    back_in = temporal_back(slope_mid, first_temporal, dilations[0]).astype(jnp.bfloat16)
    frame_out, frame_back = (
        lax.all_to_all(act_out, "tm", split_axis=1, concat_axis=2, tiled=True),
        lax.all_to_all(back_in, "tm", split_axis=1, concat_axis=2, tiled=True),
    )
    decoded = jnp.where(
        is_valid, latents.astype(jnp.float32) + spatial(frame_out, last_spatial), jnp.float32(0.0)
    ).astype(jnp.bfloat16)
    last_grad = spatial_kernel(frame_out, masked)
    slope_in = (frame_back.astype(jnp.float32) * silu_slope(pre_in)).astype(jnp.bfloat16)
    spatial_grad = spatial_kernel(latents, slope_in)
    latent_grad = (masked.astype(jnp.float32) + spatial_back(slope_in, first_spatial)).astype(
        jnp.bfloat16
    )
    partials = (
        factor * spatial_grad,
        factor * last_grad,
        factor * first_grad,
        factor * second_grad,
    )
    reduced = lax.psum((partials[0], partials[1], partials[2], partials[3]), ("dp", "tm"))
    return (decoded, latent_grad, reduced[0], reduced[1], reduced[2], reduced[3])


REACH = (TAPS - 1) * DILATION_MAX
CHUNKS = 2
VMEM_LIMIT = 56 * 1024 * 1024
BF = jnp.bfloat16
F32 = jnp.float32


def params():
    return pltpu.CompilerParams(
        dimension_semantics=("arbitrary",), vmem_limit_bytes=VMEM_LIMIT
    )


COST = 0.02


def cost(micros):
    return pl.CostEstimate(flops=int(micros * COST * 1e9), bytes_accessed=1000, transcendentals=0)


def pair_range(chunk, rows):
    size = rows // CHUNKS
    low = 0 if chunk == 0 else chunk * size // 2 - 1
    high = rows // 2 if chunk == CHUNKS - 1 else (chunk + 1) * size // 2 - 1
    return low, high


def seen_rows(low, high, rows):
    return max(0, 2 * low - 1), min(rows, 2 * high + 1)


def zero_borders(pad, pairs, low, high, rows):
    pad[...] = jnp.zeros(pad.shape, F32)
    frames, _, width, lanes = pairs.shape
    for frame in range(frames):
        if low == 0:
            pairs[frame, 0, :, 0 : lanes // 2] = jnp.zeros((width, lanes // 2), BF)
        if 2 * high == rows:
            pairs[frame, high - low, :, lanes // 2 : lanes] = jnp.zeros((width, lanes // 2), BF)


def fill_pairs(read_row, pad, pairs, low, high, rows):
    frames, _, width, lanes = pairs.shape
    chans = lanes // 6
    begin, end = seen_rows(low, high, rows)
    for frame in range(frames):
        for row in range(begin, end):
            pad[frame, row - begin, 8 : 8 + width, :] = read_row(frame, row).astype(F32)
    for frame in range(frames):
        for row in range(begin, end):
            at = (row + 1) // 2 - low
            side = 3 * chans * (1 - row % 2)
            pairs[frame, at, :, side + chans : side + 2 * chans] = read_row(frame, row)
            for shift in (0, 2):
                seen = pad[frame, row - begin, 7 + shift : 7 + shift + width, :].astype(BF)
                lane = side + shift * chans
                pairs[frame, at, :, lane : lane + chans] = seen


def front_kernel(ids, *refs):
    latents, cotangent = refs[0:2], refs[2:4]
    w_in, w_back, act, back, slope, pad, pairs = refs[4:]
    at = pl.program_id(0)
    core, shift_rows = ids[1], ids[7]
    spread, width, chans = latents[0].shape[1:]
    count = spread // 2 - 1
    lanes = 6 * chans
    slots = pl.num_programs(0)

    @pl.when(at == 0)
    def _():
        pad[...] = jnp.zeros(pad.shape, F32)

    def conv(blocks, weights):
        for index in range(2):
            for row in range(spread):
                place = index * (spread + 2) + 1 + row
                pad[place, 8 : 8 + width, :] = blocks[index][0, row].astype(F32)
        for index in range(2):
            for row in range(spread):
                place = index * (spread + 2) + 1 + row + shift_rows
                side = 3 * chans * (row % 2)
                to = index * (count + 1) + row // 2
                for shift in range(3):
                    seen = pad[place, 7 + shift : 7 + shift + width, :].astype(BF)
                    pairs[to, :, side + shift * chans : side + (shift + 1) * chans] = seen
        stacked = []
        for lower in range(2):
            both = [
                pairs[index * (count + 1) + lower : index * (count + 1) + lower + count]
                for index in range(2)
            ]
            stacked.append(jnp.concatenate(both, axis=0).reshape(2 * count * width, lanes))
        return jnp.dot(
            jnp.concatenate(stacked, axis=1), weights[...], preferred_element_type=F32
        )

    def store(target, values):
        values = values.reshape(2 * count, width, 2 * chans)
        for index in range(2):
            owner = core if index == 0 else 1 - core
            for row in range(2 * count):
                lane = row % 2 * chans
                target[owner, 0, row] = values[index * count + row // 2, :, lane : lane + chans]

    pre = conv(latents, w_in)
    sigma = jax.nn.sigmoid(pre)
    store(act, (pre * sigma).astype(BF))
    store(slope, (sigma * (1.0 + pre * (1.0 - sigma))).astype(BF))
    summed = conv(cotangent, w_back)
    half = count * width
    mine = jnp.where(core * slots + at < ids[2], 1.0, 0.0).astype(F32)
    other = jnp.where((1 - core) * slots + at < ids[2], 1.0, 0.0).astype(F32)
    store(back, jnp.concatenate([summed[:half] * mine, summed[half:] * other], 0).astype(BF))


def front(ids, latents, cotangent, w_in, w_back):
    slots, spread, width, chans = latents[1].shape
    rows = spread - 2
    own = pl.BlockSpec(
        (pl.Element(1), pl.Element(spread), pl.Element(width), pl.Element(chans)),
        lambda i, ids: (i, ids[6], 0, 0),
    )
    got = pl.BlockSpec((1, spread, width, chans), lambda i, ids: (i, 0, 0, 0))
    target = pl.BlockSpec((2, 1, rows, width, chans), lambda i, ids: (0, i, 0, 0, 0))
    fixed = pl.BlockSpec(w_in.shape, lambda i, ids: (0, 0))
    made = pl.pallas_call(
        front_kernel,
        grid_spec=pltpu.PrefetchScalarGridSpec(
            num_scalar_prefetch=1,
            grid=(slots,),
            in_specs=[own, got, own, got, fixed, fixed],
            out_specs=[target] * 3,
            scratch_shapes=[
                pltpu.VMEM((2 * (spread + 2), width + 16, chans), F32),
                pltpu.VMEM((spread, width, 6 * chans), BF),
            ],
        ),
        out_shape=[jax.ShapeDtypeStruct((2, slots, rows, width, chans), BF)] * 3,
        compiler_params=params(),
        cost_estimate=cost(22.0 / CHUNKS),
        name="front",
    )(ids, *latents, *cotangent, w_in, w_back)
    return [value.reshape(2 * slots, rows, width, chans) for value in made]


def taps_of(held, start, step, count):
    size = held.shape[1]
    chans = held.shape[2]
    seen = []
    for tap in range(TAPS):
        seen.append(held[pl.ds(start + tap * step, count)].reshape(count * size, chans))
    return jnp.concatenate(seen, axis=1)


def outer(left, right):
    return lax.dot_general(left, right, (((0,), (0,)), ((), ())), preferred_element_type=F32)


def middle_kernel(
    ids, act_in, act_back, slope, halo, w_mid, w_mid_back, w_first,
    mid_send, mid_keep, first_keep, first_send, grad_first, grad_second,
    held_in, held_back, held_mid, result,
):
    at = pl.program_id(0)
    side, core, near, far = ids[0], ids[1], ids[3], ids[4]
    frames = act_in.shape[0]
    slots = frames // 2
    mine = core * slots
    other = slots - mine

    @pl.when(at == 0)
    def _():
        blank = jnp.zeros((REACH,) + held_in.shape[1:], BF)
        held_in[0:REACH] = blank
        held_back[frames : frames + REACH] = blank
        held_mid[0:REACH] = blank
        held_mid[REACH + frames : 2 * REACH + frames] = blank
        grad_first[...] = jnp.zeros_like(grad_first)
        grad_second[...] = jnp.zeros_like(grad_second)

    held_in[REACH : REACH + frames] = act_in[:, 0]
    held_back[0:frames] = act_back[:, 0]

    @pl.when(side == 0)
    def _():
        held_back[frames : frames + REACH] = halo[:, 0]

    @pl.when(side == 1)
    def _():
        held_in[0:REACH] = halo[:, 0]

    size, chans = held_in.shape[1:]
    taps_in = taps_of(held_in, REACH, -near, frames)
    taps_back = taps_of(held_back, 0, far, frames)
    pre = jnp.dot(taps_in, w_mid[...], preferred_element_type=F32)
    sigma = jax.nn.sigmoid(pre)
    act = (pre * sigma).astype(BF)
    back = jnp.dot(taps_back, w_mid_back[...], preferred_element_type=F32)
    grad = (back * (sigma * (1.0 + pre * (1.0 - sigma)))).astype(BF)
    grad_second[...] += outer(act, taps_back)
    grad_first[...] += outer(grad, taps_in)
    act = act.reshape(frames, size, chans)
    grad = grad.reshape(frames, size, chans)

    @pl.when(side == 0)
    def _():
        held_mid[REACH : REACH + frames] = act
        mid_keep[:, 0] = grad
        mid_send[:, 0] = act[frames - REACH :]

    @pl.when(side == 1)
    def _():
        held_mid[REACH : REACH + frames] = grad
        mid_keep[:, 0] = act
        mid_send[:, 0] = grad[:REACH]

    step = jnp.where(side == 0, -far, near)
    first = jnp.dot(
        taps_of(held_mid, REACH, step, frames), w_first[...], preferred_element_type=F32
    )
    result[...] = first.astype(BF).reshape(frames, size, chans)

    @pl.when(side == 1)
    def _():
        result[...] = (result[...].astype(F32) * slope[:, 0].astype(F32)).astype(BF)

    first_keep[:, 0] = result[pl.ds(mine, slots)]
    first_send[:, 0] = result[pl.ds(other, slots)]


def middle(ids, act_in, act_back, slope, halo, w_mid, w_mid_back, w_first):
    frames, rows, width, chans = act_in.shape
    slots = frames // 2
    fixed = pl.BlockSpec(w_mid.shape, lambda i, ids: (0, 0))
    sums = pl.BlockSpec((chans, TAPS * chans), lambda i, ids: (0, 0))

    def rowwise(count):
        return pl.BlockSpec((count, 1, width, chans), lambda i, ids: (0, i, 0, 0))

    def shaped(count):
        return jax.ShapeDtypeStruct((count, rows, width, chans), BF)

    summed = jax.ShapeDtypeStruct((chans, TAPS * chans), F32)
    return pl.pallas_call(
        middle_kernel,
        grid_spec=pltpu.PrefetchScalarGridSpec(
            num_scalar_prefetch=1,
            grid=(rows,),
            in_specs=[rowwise(frames)] * 3 + [rowwise(REACH), fixed, fixed, fixed],
            out_specs=[
                rowwise(REACH), rowwise(frames), rowwise(slots), rowwise(slots), sums, sums,
            ],
            scratch_shapes=[
                pltpu.VMEM((REACH + frames, width, chans), BF),
                pltpu.VMEM((REACH + frames, width, chans), BF),
                pltpu.VMEM((2 * REACH + frames, width, chans), BF),
                pltpu.VMEM((frames, width, chans), BF),
            ],
        ),
        out_shape=[
            shaped(REACH), shaped(frames), shaped(slots), shaped(slots), summed, summed,
        ],
        compiler_params=params(),
        cost_estimate=cost(24.0 / CHUNKS),
        name="middle",
    )(ids, act_in, act_back, slope, halo, w_mid, w_mid_back, w_first)


def second_kernel(ids, mid, slope, halo, w_second, keep, send, held, result):
    at = pl.program_id(0)
    side, core, near, far = ids[0], ids[1], ids[3], ids[4]
    frames = mid.shape[0]
    slots = frames // 2
    mine = core * slots

    @pl.when(at == 0)
    def _():
        blank = jnp.zeros((REACH,) + held.shape[1:], BF)
        held[0:REACH] = blank
        held[REACH + frames : 2 * REACH + frames] = blank

    held[REACH : REACH + frames] = mid[:, 0]

    @pl.when(side == 0)
    def _():
        held[REACH + frames : 2 * REACH + frames] = halo[:, 0]

    @pl.when(side == 1)
    def _():
        held[0:REACH] = halo[:, 0]

    step = jnp.where(side == 0, near, -far)
    made = jnp.dot(
        taps_of(held, REACH, step, frames), w_second[...], preferred_element_type=F32
    )
    result[...] = made.astype(BF).reshape(result.shape)

    @pl.when(side == 0)
    def _():
        result[...] = (result[...].astype(F32) * slope[:, 0].astype(F32)).astype(BF)

    keep[:, 0] = result[pl.ds(mine, slots)]
    send[:, 0] = result[pl.ds(slots - mine, slots)]


def second(ids, mid, slope, halo, w_second):
    frames, rows, width, chans = mid.shape
    slots = frames // 2

    def rowwise(count):
        return pl.BlockSpec((count, 1, width, chans), lambda i, ids: (0, i, 0, 0))

    shape = jax.ShapeDtypeStruct((slots, rows, width, chans), BF)
    return pl.pallas_call(
        second_kernel,
        grid_spec=pltpu.PrefetchScalarGridSpec(
            num_scalar_prefetch=1,
            grid=(rows,),
            in_specs=[
                rowwise(frames), rowwise(frames), rowwise(REACH),
                pl.BlockSpec(w_second.shape, lambda i, ids: (0, 0)),
            ],
            out_specs=[rowwise(slots), rowwise(slots)],
            scratch_shapes=[
                pltpu.VMEM((2 * REACH + frames, width, chans), BF),
                pltpu.VMEM((frames, width, chans), BF),
            ],
        ),
        out_shape=[shape, shape],
        compiler_params=params(),
        cost_estimate=cost(10.0 / CHUNKS),
        name="second",
    )(ids, mid, slope, halo, w_second)


def ending_kernel(chunk, rows, factor, with_outs, ids, *refs):
    refs = list(refs)
    used = 1 if chunk == 0 else 2
    own = [refs.pop(0) for _ in range(used)]
    got = [refs.pop(0) for _ in range(used)]
    latents, cotangent, weights, before = [refs.pop(0) for _ in range(4)]
    if with_outs:
        refs.pop(0), refs.pop(0)
    outs = (refs.pop(0), refs.pop(0))
    sums, pad, pairs, frame, buffer, sems, beside, total = refs
    at = pl.program_id(0)
    last = pl.num_programs(0) - 1
    core, role = ids[1], ids[5]
    frames, _, width, lanes = pairs.shape
    chans = lanes // 6
    low, high = pair_range(chunk, rows)
    size = rows // CHUNKS
    half = size // 2
    base = (chunk + 1 - used) * size
    count = high - low

    def each_copy(step, act):
        for way in range(2):
            @pl.when(role == way)
            def _():
                target = outs[way].at[pl.ds(step * frames, frames), pl.ds(2 * low, 2 * count)]
                act(pltpu.make_async_copy(buffer.at[step % 2], target, sems.at[step % 2]))

    @pl.when(at == 0)
    def _():
        zero_borders(pad, pairs, low, high, rows)
        total[...] = jnp.zeros_like(total)

    @pl.when(at >= 2)
    def _():
        each_copy(at - 2, lambda copy: copy.wait())

    for index in range(used):
        frame[:, pl.ds(index * size + core * half, half)] = own[index][...]
        frame[:, pl.ds(index * size + half - core * half, half)] = got[index][...]
    fill_pairs(lambda which, row: frame[which, row - base], pad, pairs, low, high, rows)
    slot = at % 2
    one = jnp.where(role == 1, 1.0, 0.0).astype(F32)
    for which in range(frames):
        place = (core * (last + 1) + at) * frames + which
        valid = jnp.where(place < ids[2], 1.0, 0.0).astype(F32)
        zero = (1.0 - one) * valid
        upper = pairs[which, 0:count].reshape(count * width, lanes)
        lower = pairs[which, 1 : 1 + count].reshape(count * width, lanes)
        made = jnp.dot(
            jnp.concatenate([upper, lower], axis=1), weights[...], preferred_element_type=F32
        )
        made = made.reshape(count, width, 2 * chans)
        for row in range(2 * count):
            lane = row % 2 * chans
            latent = latents[which, row].astype(F32)
            arriving = cotangent[which, row].astype(F32)
            beside[which, row // 2, :, lane : lane + chans] = (
                latent * one + arriving * zero
            ).astype(BF)
            buffer[slot, which, row] = (
                latent * zero
                + arriving * (one * valid)
                + made[row // 2, :, lane : lane + chans] * (one + zero)
            ).astype(BF)
    flat = beside[...].reshape(frames * count * width, 2 * chans)
    for part in range(2):
        seen = pairs[:, part : part + count].reshape(frames * count * width, lanes)
        total[:, part * lanes : (part + 1) * lanes] += outer(flat, seen)
    each_copy(at, lambda copy: copy.start())

    @pl.when(at == last)
    def _():
        span = 9 * chans
        sums[...] = before[...] + factor * (
            total[0:chans, 0:span] + total[chans : 2 * chans, 3 * chans : 3 * chans + span]
        )
        each_copy(at - 1, lambda copy: copy.wait())
        each_copy(at, lambda copy: copy.wait())


def ending(chunk, factor, ids, own, got, latents, cotangent, weights, before, outs=None):
    slots, rows, width, chans = latents.shape
    size = rows // CHUNKS
    low, high = pair_range(chunk, rows)
    count = high - low
    begin, end = seen_rows(low, high, rows)
    used = 1 if chunk == 0 else 2
    each = 2
    area = pl.BlockSpec(
        (pl.Element(each), pl.Element(2 * count), pl.Element(width), pl.Element(chans)),
        lambda i, ids: (i * each, 2 * low, 0, 0),
    )
    part = pl.BlockSpec((each, size // 2, width, chans), lambda i, ids: (i, 0, 0, 0))
    summed = pl.BlockSpec((chans, 9 * chans), lambda i, ids: (0, 0))
    anywhere = pl.BlockSpec(memory_space=pl.ANY)
    pick = slice(chunk + 1 - used, chunk + 1)
    args = [*own[pick], *got[pick], latents, cotangent, weights, before]
    in_specs = [part] * (2 * used) + [area, area]
    in_specs += [pl.BlockSpec(weights.shape, lambda i, ids: (0, 0)), summed]
    aliases = {}
    if outs is not None:
        aliases = {1 + len(args): 0, 2 + len(args): 1}
        args += list(outs)
        in_specs += [anywhere, anywhere]
    return pl.pallas_call(
        functools.partial(ending_kernel, chunk, rows, factor, outs is not None),
        grid_spec=pltpu.PrefetchScalarGridSpec(
            num_scalar_prefetch=1,
            grid=(slots // each,),
            in_specs=in_specs,
            out_specs=[anywhere, anywhere, summed],
            scratch_shapes=[
                pltpu.VMEM((each, end - begin, width + 16, chans), F32),
                pltpu.VMEM((each, count + 1, width, 6 * chans), BF),
                pltpu.VMEM((each, used * size, width, chans), BF),
                pltpu.VMEM((2, each, 2 * count, width, chans), BF),
                pltpu.SemaphoreType.DMA((2,)),
                pltpu.VMEM((each, count, width, 2 * chans), BF),
                pltpu.VMEM((2 * chans, 12 * chans), F32),
            ],
        ),
        out_shape=[
            jax.ShapeDtypeStruct(latents.shape, BF),
            jax.ShapeDtypeStruct(latents.shape, BF),
            jax.ShapeDtypeStruct((chans, 9 * chans), F32),
        ],
        input_output_aliases=aliases,
        compiler_params=params(),
        cost_estimate=cost(26.0 / CHUNKS),
        name="ending",
    )(ids, *args)


def two_row_weights(kernel):
    flat = kernel.reshape(-1, kernel.shape[3])
    shift = 3 * kernel.shape[2]
    return jnp.concatenate(
        [jnp.pad(flat, ((0, shift), (0, 0))), jnp.pad(flat, ((shift, 0), (0, 0)))], axis=1
    )


def after(value, *earlier):
    return lax.optimization_barrier((value,) + earlier)[0]


def turned(kernel):
    return jnp.transpose(kernel[::-1, ::-1], (0, 1, 3, 2))


def flips(dp_size, tm_size):
    count = dp_size * tm_size
    digit = 1
    result = []
    while digit < count:
        result.append([(place, place ^ digit) for place in range(count)])
        digit *= 2
    return result


def halve(values, digits, pairs, place):
    for digit in digits:
        size = values.shape[0] // 2
        upper = (place >> digit) & 1
        keep = lax.dynamic_slice_in_dim(values, upper * size, size, 0)
        send = lax.dynamic_slice_in_dim(values, (1 - upper) * size, size, 0)
        values = keep + lax.ppermute(send, ("dp", "tm"), pairs[digit])
    return values


def double(values, digits, pairs, place, axis=0):
    for digit in digits:
        upper = (place >> digit) & 1
        other = lax.ppermute(values, ("dp", "tm"), pairs[digit])
        values = jnp.where(
            upper == 0,
            jnp.concatenate([values, other], axis),
            jnp.concatenate([other, values], axis),
        )
    return values


def on_chip_pair(
    dp_size,
    latents,
    cotangent,
    first_spatial,
    last_spatial,
    first_temporal,
    second_temporal,
    frame_counts,
    dilations,
):
    latents, cotangent = latents[0], cotangent[0]
    slots, rows, width, chans = latents.shape
    half = rows // 2
    tm_index = lax.axis_index("tm")
    side, core = tm_index // 2, tm_index % 2
    factor = float(dp_size * 4 * slots * rows * width) ** (-0.5)

    def ids_for(role):
        return jnp.stack(
            [side, core, frame_counts[0] - side * 2 * slots, dilations[0], dilations[1], role]
        ).astype(jnp.int32)

    ids = ids_for(side)
    swap_cores = [(0, 1), (1, 0), (2, 3), (3, 2)]
    swap_sides = [(0, 2), (2, 0), (1, 3), (3, 1)]

    w_in = two_row_weights(first_spatial)
    w_out = two_row_weights(last_spatial)
    w_in_back = two_row_weights(turned(first_spatial))
    w_out_back = two_row_weights(turned(last_spatial))
    w_one = first_temporal.reshape(-1, chans)
    w_two = second_temporal.reshape(-1, chans)
    w_one_back = jnp.transpose(first_temporal, (0, 2, 1)).reshape(-1, chans)
    w_two_back = jnp.transpose(second_temporal, (0, 2, 1)).reshape(-1, chans)
    at_zero = side == 0
    w_first = jnp.where(at_zero, w_two, w_one_back)
    w_second = jnp.where(at_zero, w_one_back, w_two)
    w_ending = jnp.where(at_zero, w_out, w_in_back)
    w_other = jnp.where(at_zero, w_in_back, w_out)

    band = rows // CHUNKS // 2
    entries, slopes = [], []
    for chunk in range(CHUNKS):
        start = chunk * 2 * band + (1 - core) * band - 1
        sent = [
            lax.dynamic_slice_in_dim(value, jnp.clip(start, 0, rows - band - 2), band + 2, 1)
            for value in (latents, cotangent)
        ]
        if chunk > 0:
            sent = [after(value, act) for value in sent]
        got = [lax.ppermute(value, "tm", swap_cores) for value in sent]
        start = chunk * 2 * band + core * band - 1
        kept = jnp.clip(start, 0, rows - band - 2)
        front_ids = jnp.concatenate([ids, jnp.stack([kept, start - kept]).astype(jnp.int32)])
        act, back, slope = front(
            front_ids, [latents, got[0]], [cotangent, got[1]], w_in, w_out_back
        )
        slopes.append(slope)
        leaving = jnp.where(at_zero, act[2 * slots - REACH :], back[:REACH])
        if chunk > 0:
            leaving = after(leaving, halo)
        halo = lax.ppermute(leaving, "tm", swap_sides)
        entries.append([act, back, slope, halo])
    middles, halos, own, got = [], [], [], []
    outs = None
    sums_first = jnp.zeros((chans, 9 * chans), F32)
    for chunk in range(CHUNKS):
        act, back, slope, arrived = entries[chunk]
        made = middle(ids, act, back, slope, arrived, w_one, w_two_back, w_first)
        middles.append(made)
        own.append(made[2])
        got.append(lax.ppermute(made[3], "tm", swap_cores))
        *outs, sums_first = ending(
            chunk, factor, ids, own, got, latents, cotangent, w_ending, sums_first, outs
        )
        halo = lax.ppermute(after(made[0], halo, sums_first), "tm", swap_sides)
        halos.append(halo)

    pairs = flips(dp_size, 4)
    place = lax.axis_index("dp") * 4 + tm_index
    digits = [0] + list(range(2, len(pairs)))
    span = 9 * chans
    ids = ids_for(1 - side)
    own, got = [], []
    sums_second = jnp.zeros((chans, span), F32)
    for chunk, made in enumerate(middles):
        keep, leaving = second(ids, made[1], slopes[chunk], halos[chunk], w_second)
        own.append(keep)
        got.append(lax.ppermute(leaving, "tm", swap_cores))
        *outs, sums_second = ending(
            chunk, factor, ids, own, got, latents, cotangent, w_other, sums_second, outs
        )
        if chunk < CHUNKS - 1:
            halos[chunk + 1] = after(halos[chunk + 1], sums_second)
    decoded, latent_grad = outs

    early = jnp.concatenate(
        [
            sums_first,
            factor * sum(made[4] for made in middles),
            factor * sum(made[5] for made in middles),
        ],
        1,
    )
    early = after(early, halos[-1])
    early = halve(early, digits, pairs, place)
    late = halve(sums_second, digits, pairs, place)
    both = jnp.concatenate([early, late], 1)
    other = lax.ppermute(both, ("dp", "tm"), pairs[1])
    swapped = jnp.concatenate([other[:, -span:], other[:, span:-span], other[:, :span]], 1)
    both = both + swapped
    both = jnp.where(
        at_zero, both, jnp.concatenate([both[:, -span:], both[:, span:-span], both[:, :span]], 1)
    )
    both = double(both.astype(BF), digits[::-1], pairs, place).astype(F32)
    spatial_sums = (both[:, :span], both[:, -span:])
    temporal_sums = both[:, span:-span]

    last_grad = jnp.transpose(spatial_sums[0].reshape(chans, 3, 3, chans), (1, 2, 3, 0))
    first_grad = jnp.transpose(spatial_sums[1].reshape(chans, 3, 3, chans), (1, 2, 0, 3))
    first_grad = first_grad[::-1, ::-1]
    near_grad = jnp.transpose(temporal_sums[:, : TAPS * chans].reshape(chans, TAPS, chans), (1, 2, 0))
    far_grad = jnp.transpose(temporal_sums[:, TAPS * chans :].reshape(chans, TAPS, chans), (1, 0, 2))
    return (decoded[None], latent_grad[None], first_grad, last_grad, near_grad, far_grad)


def on_any_device(dp_size, tm_size, latents, cotangent, *rest):
    clips, slots, rows = latents.shape[:3]
    fits = clips == 1 and tm_size == 4 and slots <= REACH <= 2 * slots and rows % 8 == 0 and slots % 2 == 0
    if fits and dp_size & (dp_size - 1) == 0:
        return on_chip_pair(dp_size, latents, cotangent, *rest)
    return on_device(latents, cotangent, *rest)


def solution(mesh):
    in_specs = (
        P("dp", "tm", None, None, None),
        P("dp", "tm", None, None, None),
        P(),
        P(),
        P(),
        P(),
        P("dp"),
        P(),
    )
    out_specs = (
        P("dp", "tm", None, None, None),
        P("dp", "tm", None, None, None),
        P(),
        P(),
        P(),
        P(),
    )
    return jax.shard_map(
        functools.partial(on_any_device, mesh.shape["dp"], mesh.shape["tm"]), mesh=mesh, in_specs=in_specs, out_specs=out_specs, check_vma=False
    )
```

```python
import functools

import jax
import jax.numpy as jnp
from jax import lax
from jax.experimental import pallas as pl
from jax.experimental.pallas import tpu as pltpu
from jax.sharding import PartitionSpec as P

TAPS = 3
DILATION_MAX = 4


def silu_slope(values):
    sigma = jax.nn.sigmoid(values)
    return sigma * (1.0 + values * (1.0 - sigma))


def spatial(source, kernel):
    row_count, col_count, channels = source.shape[-3:]
    leading = source.shape[:-3]
    padded = jnp.pad(source, [(0, 0)] * len(leading) + [(1, 1), (1, 1), (0, 0)])
    summed = jnp.zeros(leading + (row_count, col_count, kernel.shape[3]), jnp.float32)
    for row_shift in range(3):
        for col_shift in range(3):
            window = padded[
                ..., row_shift : row_shift + row_count, col_shift : col_shift + col_count, :
            ]
            product = jnp.dot(
                window.reshape(-1, channels),
                kernel[row_shift, col_shift],
                preferred_element_type=jnp.float32,
            )
            summed = summed + product.reshape(summed.shape)
    return summed


def spatial_back(incoming, kernel):
    return spatial(incoming, jnp.transpose(kernel[::-1, ::-1], (0, 1, 3, 2)))


def spatial_kernel(source, incoming):
    row_count, col_count, channels = source.shape[-3:]
    leading = source.shape[:-3]
    padded = jnp.pad(source, [(0, 0)] * len(leading) + [(1, 1), (1, 1), (0, 0)])
    flat_in = incoming.reshape(-1, incoming.shape[-1])
    result_rows = []
    for row_shift in range(3):
        result_cols = []
        for col_shift in range(3):
            window = padded[
                ..., row_shift : row_shift + row_count, col_shift : col_shift + col_count, :
            ]
            result_cols.append(
                lax.dot_general(
                    window.reshape(-1, channels),
                    flat_in,
                    (((0,), (0,)), ((), ())),
                    preferred_element_type=jnp.float32,
                )
            )
        result_rows.append(jnp.stack(result_cols))
    return jnp.stack(result_rows)


def temporal(source, kernel, dilation):
    margin = (TAPS - 1) * DILATION_MAX
    slot_count = source.shape[1]
    padded = jnp.pad(source, ((0, 0), (margin, 0), (0, 0), (0, 0), (0, 0)))
    summed = jnp.zeros(source.shape[:-1] + (kernel.shape[2],), jnp.float32)
    for tap_index in range(kernel.shape[0]):
        begin_at = margin - tap_index * dilation
        window = lax.dynamic_slice_in_dim(padded, begin_at, slot_count, 1)
        product = jnp.dot(
            window.reshape(-1, source.shape[-1]),
            kernel[tap_index],
            preferred_element_type=jnp.float32,
        )
        summed = summed + product.reshape(summed.shape)
    return summed


def temporal_back(incoming, kernel, dilation):
    margin = (TAPS - 1) * DILATION_MAX
    slot_count = incoming.shape[1]
    padded = jnp.pad(incoming, ((0, 0), (0, margin), (0, 0), (0, 0), (0, 0)))
    summed = jnp.zeros(incoming.shape[:-1] + (kernel.shape[1],), jnp.float32)
    for tap_index in range(kernel.shape[0]):
        begin_at = tap_index * dilation
        window = lax.dynamic_slice_in_dim(padded, begin_at, slot_count, 1)
        product = jnp.dot(
            window.reshape(-1, incoming.shape[-1]),
            kernel[tap_index].T,
            preferred_element_type=jnp.float32,
        )
        summed = summed + product.reshape(summed.shape)
    return summed


def temporal_kernel(source, incoming, dilation):
    margin = (TAPS - 1) * DILATION_MAX
    slot_count = source.shape[1]
    padded = jnp.pad(source, ((0, 0), (margin, 0), (0, 0), (0, 0), (0, 0)))
    flat_in = incoming.reshape(-1, incoming.shape[-1])
    result = []
    for tap_index in range(TAPS):
        begin_at = margin - tap_index * dilation
        window = lax.dynamic_slice_in_dim(padded, begin_at, slot_count, 1)
        result.append(
            lax.dot_general(
                window.reshape(-1, source.shape[-1]),
                flat_in,
                (((0,), (0,)), ((), ())),
                preferred_element_type=jnp.float32,
            )
        )
    return jnp.stack(result)


def forward_bands(band_in, first_temporal, second_temporal, dilations):
    pre_mid = temporal(band_in, first_temporal, dilations[0])
    act_mid = jax.nn.silu(pre_mid).astype(jnp.bfloat16)
    act_out = temporal(act_mid, second_temporal, dilations[1]).astype(jnp.bfloat16)
    return (pre_mid, act_mid, act_out)


def on_device(
    latents,
    cotangent,
    first_spatial,
    last_spatial,
    first_temporal,
    second_temporal,
    frame_counts,
    dilations,
):
    local_slots = latents.shape[1]
    first_slot = lax.axis_index("tm") * local_slots
    slot_ids = first_slot + jnp.arange(local_slots, dtype=jnp.int32)
    is_valid = (slot_ids[None, :] < frame_counts[:, None])[:, :, None, None, None]
    total_count = (
        latents.shape[0]
        * lax.axis_size("dp")
        * local_slots
        * lax.axis_size("tm")
        * latents.shape[2]
        * latents.shape[3]
    )
    factor = float(total_count) ** (-0.5)
    pre_in = spatial(latents, first_spatial)
    act_in = jax.nn.silu(pre_in).astype(jnp.bfloat16)
    masked = jnp.where(is_valid, cotangent, jnp.zeros_like(cotangent))
    band_in = lax.all_to_all(act_in, "tm", split_axis=2, concat_axis=1, tiled=True)
    pre_mid, act_mid, act_out = forward_bands(band_in, first_temporal, second_temporal, dilations)
    back_out = spatial_back(masked, last_spatial).astype(jnp.bfloat16)
    band_back = lax.all_to_all(back_out, "tm", split_axis=2, concat_axis=1, tiled=True)
    second_grad = temporal_kernel(act_mid, band_back, dilations[1])
    slope_mid = (
        temporal_back(band_back, second_temporal, dilations[1]) * silu_slope(pre_mid)
    ).astype(jnp.bfloat16)
    first_grad = temporal_kernel(band_in, slope_mid, dilations[0])
    back_in = temporal_back(slope_mid, first_temporal, dilations[0]).astype(jnp.bfloat16)
    frame_out, frame_back = (
        lax.all_to_all(act_out, "tm", split_axis=1, concat_axis=2, tiled=True),
        lax.all_to_all(back_in, "tm", split_axis=1, concat_axis=2, tiled=True),
    )
    decoded = jnp.where(
        is_valid, latents.astype(jnp.float32) + spatial(frame_out, last_spatial), jnp.float32(0.0)
    ).astype(jnp.bfloat16)
    last_grad = spatial_kernel(frame_out, masked)
    slope_in = (frame_back.astype(jnp.float32) * silu_slope(pre_in)).astype(jnp.bfloat16)
    spatial_grad = spatial_kernel(latents, slope_in)
    latent_grad = (masked.astype(jnp.float32) + spatial_back(slope_in, first_spatial)).astype(
        jnp.bfloat16
    )
    partials = (
        factor * spatial_grad,
        factor * last_grad,
        factor * first_grad,
        factor * second_grad,
    )
    reduced = lax.psum((partials[0], partials[1], partials[2], partials[3]), ("dp", "tm"))
    return (decoded, latent_grad, reduced[0], reduced[1], reduced[2], reduced[3])


REACH = (TAPS - 1) * DILATION_MAX
CHUNKS = 2
VMEM_LIMIT = 56 * 1024 * 1024
BF = jnp.bfloat16
F32 = jnp.float32


def params():
    return pltpu.CompilerParams(
        dimension_semantics=("arbitrary",), vmem_limit_bytes=VMEM_LIMIT
    )


COST = 0.02


def cost(micros):
    return pl.CostEstimate(flops=int(micros * COST * 1e9), bytes_accessed=1000, transcendentals=0)


def pair_range(chunk, rows):
    size = rows // CHUNKS
    low = 0 if chunk == 0 else chunk * size // 2 - 1
    high = rows // 2 if chunk == CHUNKS - 1 else (chunk + 1) * size // 2 - 1
    return low, high


def seen_rows(low, high, rows):
    return max(0, 2 * low - 1), min(rows, 2 * high + 1)


def zero_borders(pad, pairs, low, high, rows):
    pad[...] = jnp.zeros(pad.shape, F32)
    frames, _, width, lanes = pairs.shape
    for frame in range(frames):
        if low == 0:
            pairs[frame, 0, :, 0 : lanes // 2] = jnp.zeros((width, lanes // 2), BF)
        if 2 * high == rows:
            pairs[frame, high - low, :, lanes // 2 : lanes] = jnp.zeros((width, lanes // 2), BF)


def fill_pairs(read_row, pad, pairs, low, high, rows):
    frames, _, width, lanes = pairs.shape
    chans = lanes // 6
    begin, end = seen_rows(low, high, rows)
    for frame in range(frames):
        for row in range(begin, end):
            pad[frame, row - begin, 8 : 8 + width, :] = read_row(frame, row).astype(F32)
    for frame in range(frames):
        for row in range(begin, end):
            at = (row + 1) // 2 - low
            side = 3 * chans * (1 - row % 2)
            pairs[frame, at, :, side + chans : side + 2 * chans] = read_row(frame, row)
            for shift in (0, 2):
                seen = pad[frame, row - begin, 7 + shift : 7 + shift + width, :].astype(BF)
                lane = side + shift * chans
                pairs[frame, at, :, lane : lane + chans] = seen


def front_kernel(slots, ids, *refs):
    latents, cotangent = refs[0:2], refs[2:4]
    w_in, w_back, act, back, slope, leaving, pads, windows = refs[4:]
    at = pl.program_id(0)
    side, core, shift_rows = ids[0], ids[1], ids[7]
    spread, width, chans = latents[0].shape[1:]
    count = spread // 2 - 1
    lanes = 6 * chans

    @pl.when(at == 0)
    def _():
        pads[...] = jnp.zeros(pads.shape, F32)

    def conv(blocks, weights, pad, pairs):
        for index in range(2):
            for row in range(spread):
                place = index * (spread + 2) + 1 + row
                pad[place, 8 : 8 + width, :] = blocks[index][0, row].astype(F32)
        for index in range(2):
            for row in range(spread):
                place = index * (spread + 2) + 1 + row + shift_rows
                side = 3 * chans * (row % 2)
                to = index * (count + 1) + row // 2
                for shift in range(3):
                    seen = pad[place, 7 + shift : 7 + shift + width, :].astype(BF)
                    pairs[to, :, side + shift * chans : side + (shift + 1) * chans] = seen
        stacked = []
        for lower in range(2):
            both = [
                pairs[index * (count + 1) + lower : index * (count + 1) + lower + count]
                for index in range(2)
            ]
            stacked.append(jnp.concatenate(both, axis=0).reshape(2 * count * width, lanes))
        return jnp.dot(
            jnp.concatenate(stacked, axis=1), weights[...], preferred_element_type=F32
        )

    def store(target, values):
        values = values.reshape(2 * count, width, 2 * chans)
        for index in range(2):
            owner = core if index == 0 else 1 - core
            for row in range(2 * count):
                lane = row % 2 * chans
                target[owner, 0, row] = values[index * count + row // 2, :, lane : lane + chans]

    pre = conv(latents, w_in, pads.at[0], windows.at[0])
    summed = conv(cotangent, w_back, pads.at[1], windows.at[1])
    sigma = jax.nn.sigmoid(pre)
    store(act, (pre * sigma).astype(BF))
    store(slope, (sigma * (1.0 + pre * (1.0 - sigma))).astype(BF))
    half = count * width
    mine = jnp.where(core * slots + at < ids[2], 1.0, 0.0).astype(F32)
    other = jnp.where((1 - core) * slots + at < ids[2], 1.0, 0.0).astype(F32)
    store(back, jnp.concatenate([summed[:half] * mine, summed[half:] * other], 0).astype(BF))

    tail = leaving.shape[0] - slots

    @pl.when(side == 0)
    def _():
        leaving[at + tail] = act[1, 0]

    @pl.when((side == 0) & (at >= slots - tail))
    def _():
        leaving[at - (slots - tail)] = act[0, 0]

    @pl.when(side == 1)
    def _():
        leaving[at] = back[0, 0]

    @pl.when((side == 1) & (at < tail))
    def _():
        leaving[slots + at] = back[1, 0]


def front(ids, latents, cotangent, w_in, w_back):
    slots, spread, width, chans = latents[1].shape
    rows = spread - 2
    own = pl.BlockSpec(
        (pl.Element(1), pl.Element(spread), pl.Element(width), pl.Element(chans)),
        lambda i, ids: (i, ids[6], 0, 0),
    )
    got = pl.BlockSpec((1, spread, width, chans), lambda i, ids: (i, 0, 0, 0))
    target = pl.BlockSpec((2, 1, rows, width, chans), lambda i, ids: (0, i, 0, 0, 0))
    fixed = pl.BlockSpec(w_in.shape, lambda i, ids: (0, 0))
    made = pl.pallas_call(
        functools.partial(front_kernel, slots),
        grid_spec=pltpu.PrefetchScalarGridSpec(
            num_scalar_prefetch=1,
            grid=(slots,),
            in_specs=[own, got, own, got, fixed, fixed],
            out_specs=[
                target, target, target,
                pl.BlockSpec((REACH, rows, width, chans), lambda i, ids: (0, 0, 0, 0)),
            ],
            scratch_shapes=[
                pltpu.VMEM((2, 2 * (spread + 2), width + 16, chans), F32),
                pltpu.VMEM((2, spread, width, 6 * chans), BF),
            ],
        ),
        out_shape=[jax.ShapeDtypeStruct((2, slots, rows, width, chans), BF)] * 3
        + [jax.ShapeDtypeStruct((REACH, rows, width, chans), BF)],
        compiler_params=params(),
        cost_estimate=cost(22.0 / CHUNKS),
        name="front",
    )(ids, *latents, *cotangent, w_in, w_back)
    return [value.reshape(-1, rows, width, chans) for value in made]


def taps_of(held, start, step, count):
    size = held.shape[1]
    chans = held.shape[2]
    seen = []
    for tap in range(TAPS):
        seen.append(held[pl.ds(start + tap * step, count)].reshape(count * size, chans))
    return jnp.concatenate(seen, axis=1)


def outer(left, right):
    return lax.dot_general(left, right, (((0,), (0,)), ((), ())), preferred_element_type=F32)


def middle_kernel(
    ids, act_in, act_back, slope, halo, w_mid, w_mid_back, w_first,
    mid_send, mid_keep, first_keep, first_send, grad_first, grad_second,
    held_in, held_back, held_mid, result,
):
    at = pl.program_id(0)
    side, core, near, far = ids[0], ids[1], ids[3], ids[4]
    frames = act_in.shape[0]
    slots = frames // 2
    mine = core * slots
    other = slots - mine

    @pl.when(at == 0)
    def _():
        blank = jnp.zeros((REACH,) + held_in.shape[1:], BF)
        held_mid[0:REACH] = blank
        held_mid[REACH + frames : 2 * REACH + frames] = blank
        grad_first[...] = jnp.zeros_like(grad_first)
        grad_second[...] = jnp.zeros_like(grad_second)

    held_in[REACH : REACH + frames] = act_in[:, 0]
    held_back[0:frames] = act_back[:, 0]

    one = side.astype(F32)
    held_in[0:REACH] = (halo[:, 0].astype(F32) * one).astype(BF)
    held_back[frames : frames + REACH] = (halo[:, 0].astype(F32) * (1.0 - one)).astype(BF)

    size, chans = held_in.shape[1:]
    taps_in = taps_of(held_in, REACH, -near, frames)
    taps_back = taps_of(held_back, 0, far, frames)
    pre = jnp.dot(taps_in, w_mid[...], preferred_element_type=F32)
    sigma = jax.nn.sigmoid(pre)
    act = (pre * sigma).astype(BF)
    back = jnp.dot(taps_back, w_mid_back[...], preferred_element_type=F32)
    grad = (back * (sigma * (1.0 + pre * (1.0 - sigma)))).astype(BF)
    grad_second[...] += outer(act, taps_back)
    grad_first[...] += outer(grad, taps_in)
    act = act.reshape(frames, size, chans)
    grad = grad.reshape(frames, size, chans)

    ours = jnp.where(side == 0, act, grad)
    held_mid[REACH : REACH + frames] = ours
    mid_keep[:, 0] = jnp.where(side == 0, grad, act)
    mid_send[:, 0] = held_mid[pl.ds(REACH + (1 - side) * (frames - REACH), REACH)]
    step = jnp.where(side == 0, -far, near)
    first = jnp.dot(
        taps_of(held_mid, REACH, step, frames), w_first[...], preferred_element_type=F32
    )
    first = first.astype(BF).reshape(frames, size, chans).astype(F32)
    result[...] = (first * (slope[:, 0].astype(F32) * one + (1.0 - one))).astype(BF)
    first_keep[:, 0] = result[pl.ds(mine, slots)]
    first_send[:, 0] = result[pl.ds(other, slots)]


def middle(ids, act_in, act_back, slope, halo, w_mid, w_mid_back, w_first):
    frames, rows, width, chans = act_in.shape
    slots = frames // 2
    fixed = pl.BlockSpec(w_mid.shape, lambda i, ids: (0, 0))
    sums = pl.BlockSpec((chans, TAPS * chans), lambda i, ids: (0, 0))

    def rowwise(count):
        return pl.BlockSpec((count, 1, width, chans), lambda i, ids: (0, i, 0, 0))

    def shaped(count):
        return jax.ShapeDtypeStruct((count, rows, width, chans), BF)

    summed = jax.ShapeDtypeStruct((chans, TAPS * chans), F32)
    return pl.pallas_call(
        middle_kernel,
        grid_spec=pltpu.PrefetchScalarGridSpec(
            num_scalar_prefetch=1,
            grid=(rows,),
            in_specs=[rowwise(frames)] * 3 + [rowwise(REACH), fixed, fixed, fixed],
            out_specs=[
                rowwise(REACH), rowwise(frames), rowwise(slots), rowwise(slots), sums, sums,
            ],
            scratch_shapes=[
                pltpu.VMEM((REACH + frames, width, chans), BF),
                pltpu.VMEM((REACH + frames, width, chans), BF),
                pltpu.VMEM((2 * REACH + frames, width, chans), BF),
                pltpu.VMEM((frames, width, chans), BF),
            ],
        ),
        out_shape=[
            shaped(REACH), shaped(frames), shaped(slots), shaped(slots), summed, summed,
        ],
        compiler_params=params(),
        cost_estimate=cost(24.0 / CHUNKS),
        name="middle",
    )(ids, act_in, act_back, slope, halo, w_mid, w_mid_back, w_first)


def second_kernel(ids, mid, slope, halo, w_second, keep, send, held, result):
    side, core, near, far = ids[0], ids[1], ids[3], ids[4]
    frames, each = mid.shape[:2]
    slots = frames // 2
    mine = core * slots
    size, chans = held.shape[2:]
    one = side.astype(F32)
    step = jnp.where(side == 0, near, -far)
    for row in range(each):
        held[row, 0:REACH] = (halo[:, row].astype(F32) * one).astype(BF)
        held[row, REACH : REACH + frames] = mid[:, row]
        held[row, REACH + frames :] = (halo[:, row].astype(F32) * (1.0 - one)).astype(BF)
        made = jnp.dot(
            taps_of(held.at[row], REACH, step, frames), w_second[...], preferred_element_type=F32
        )
        made = made.astype(BF).reshape(frames, size, chans).astype(F32)
        result[row] = (made * (slope[:, row].astype(F32) * (1.0 - one) + one)).astype(BF)
        keep[:, row] = result[row, pl.ds(mine, slots)]
        send[:, row] = result[row, pl.ds(slots - mine, slots)]


def second(ids, mid, slope, halo, w_second):
    frames, rows, width, chans = mid.shape
    slots = frames // 2
    each = 2

    def rowwise(count):
        return pl.BlockSpec((count, each, width, chans), lambda i, ids: (0, i, 0, 0))

    shape = jax.ShapeDtypeStruct((slots, rows, width, chans), BF)
    return pl.pallas_call(
        second_kernel,
        grid_spec=pltpu.PrefetchScalarGridSpec(
            num_scalar_prefetch=1,
            grid=(rows // each,),
            in_specs=[
                rowwise(frames), rowwise(frames), rowwise(REACH),
                pl.BlockSpec(w_second.shape, lambda i, ids: (0, 0)),
            ],
            out_specs=[rowwise(slots), rowwise(slots)],
            scratch_shapes=[
                pltpu.VMEM((each, 2 * REACH + frames, width, chans), BF),
                pltpu.VMEM((each, frames, width, chans), BF),
            ],
        ),
        out_shape=[shape, shape],
        compiler_params=params(),
        cost_estimate=cost(10.0 / CHUNKS),
        name="second",
    )(ids, mid, slope, halo, w_second)


def ending_kernel(chunk, rows, factor, with_outs, ids, *refs):
    refs = list(refs)
    used = 1 if chunk == 0 else 2
    own = [refs.pop(0) for _ in range(used)]
    got = [refs.pop(0) for _ in range(used)]
    latents, cotangent, weights, before = [refs.pop(0) for _ in range(4)]
    if with_outs:
        refs.pop(0), refs.pop(0)
    outs = (refs.pop(0), refs.pop(0))
    sums, pad, pairs, frame, buffer, sems, beside, total = refs
    at = pl.program_id(0)
    last = pl.num_programs(0) - 1
    core, role = ids[1], ids[5]
    frames, _, width, lanes = pairs.shape
    chans = lanes // 6
    low, high = pair_range(chunk, rows)
    size = rows // CHUNKS
    half = size // 2
    base = (chunk + 1 - used) * size
    count = high - low

    def each_copy(step, act):
        for way in range(2):
            @pl.when(role == way)
            def _():
                target = outs[way].at[pl.ds(step * frames, frames), pl.ds(2 * low, 2 * count)]
                act(pltpu.make_async_copy(buffer.at[step % 2], target, sems.at[step % 2]))

    @pl.when(at == 0)
    def _():
        zero_borders(pad, pairs, low, high, rows)
        total[...] = jnp.zeros_like(total)

    @pl.when(at >= 2)
    def _():
        each_copy(at - 2, lambda copy: copy.wait())

    for index in range(used):
        frame[:, pl.ds(index * size + core * half, half)] = own[index][...]
        frame[:, pl.ds(index * size + half - core * half, half)] = got[index][...]
    fill_pairs(lambda which, row: frame[which, row - base], pad, pairs, low, high, rows)
    slot = at % 2
    one = jnp.where(role == 1, 1.0, 0.0).astype(F32)
    for which in range(frames):
        place = (core * (last + 1) + at) * frames + which
        valid = jnp.where(place < ids[2], 1.0, 0.0).astype(F32)
        zero = (1.0 - one) * valid
        upper = pairs[which, 0:count].reshape(count * width, lanes)
        lower = pairs[which, 1 : 1 + count].reshape(count * width, lanes)
        made = jnp.dot(
            jnp.concatenate([upper, lower], axis=1), weights[...], preferred_element_type=F32
        )
        made = made.reshape(count, width, 2 * chans)
        for row in range(2 * count):
            lane = row % 2 * chans
            latent = latents[which, row].astype(F32)
            arriving = cotangent[which, row].astype(F32)
            beside[which, row // 2, :, lane : lane + chans] = (
                latent * one + arriving * zero
            ).astype(BF)
            buffer[slot, which, row] = (
                latent * zero
                + arriving * (one * valid)
                + made[row // 2, :, lane : lane + chans] * (one + zero)
            ).astype(BF)
    flat = beside[...].reshape(frames * count * width, 2 * chans)
    for part in range(2):
        seen = pairs[:, part : part + count].reshape(frames * count * width, lanes)
        total[:, part * lanes : (part + 1) * lanes] += outer(flat, seen)
    each_copy(at, lambda copy: copy.start())

    @pl.when(at == last)
    def _():
        span = 9 * chans
        sums[...] = before[...] + factor * (
            total[0:chans, 0:span] + total[chans : 2 * chans, 3 * chans : 3 * chans + span]
        )
        each_copy(at - 1, lambda copy: copy.wait())
        each_copy(at, lambda copy: copy.wait())


def ending(chunk, factor, ids, own, got, latents, cotangent, weights, before, outs=None):
    slots, rows, width, chans = latents.shape
    size = rows // CHUNKS
    low, high = pair_range(chunk, rows)
    count = high - low
    begin, end = seen_rows(low, high, rows)
    used = 1 if chunk == 0 else 2
    each = 2
    area = pl.BlockSpec(
        (pl.Element(each), pl.Element(2 * count), pl.Element(width), pl.Element(chans)),
        lambda i, ids: (i * each, 2 * low, 0, 0),
    )
    part = pl.BlockSpec((each, size // 2, width, chans), lambda i, ids: (i, 0, 0, 0))
    summed = pl.BlockSpec((chans, 9 * chans), lambda i, ids: (0, 0))
    anywhere = pl.BlockSpec(memory_space=pl.ANY)
    pick = slice(chunk + 1 - used, chunk + 1)
    args = [*own[pick], *got[pick], latents, cotangent, weights, before]
    in_specs = [part] * (2 * used) + [area, area]
    in_specs += [pl.BlockSpec(weights.shape, lambda i, ids: (0, 0)), summed]
    aliases = {}
    if outs is not None:
        aliases = {1 + len(args): 0, 2 + len(args): 1}
        args += list(outs)
        in_specs += [anywhere, anywhere]
    return pl.pallas_call(
        functools.partial(ending_kernel, chunk, rows, factor, outs is not None),
        grid_spec=pltpu.PrefetchScalarGridSpec(
            num_scalar_prefetch=1,
            grid=(slots // each,),
            in_specs=in_specs,
            out_specs=[anywhere, anywhere, summed],
            scratch_shapes=[
                pltpu.VMEM((each, end - begin, width + 16, chans), F32),
                pltpu.VMEM((each, count + 1, width, 6 * chans), BF),
                pltpu.VMEM((each, used * size, width, chans), BF),
                pltpu.VMEM((2, each, 2 * count, width, chans), BF),
                pltpu.SemaphoreType.DMA((2,)),
                pltpu.VMEM((each, count, width, 2 * chans), BF),
                pltpu.VMEM((2 * chans, 12 * chans), F32),
            ],
        ),
        out_shape=[
            jax.ShapeDtypeStruct(latents.shape, BF),
            jax.ShapeDtypeStruct(latents.shape, BF),
            jax.ShapeDtypeStruct((chans, 9 * chans), F32),
        ],
        input_output_aliases=aliases,
        compiler_params=params(),
        cost_estimate=cost(26.0 / CHUNKS),
        name="ending",
    )(ids, *args)


def two_row_weights(kernel):
    flat = kernel.reshape(-1, kernel.shape[3])
    shift = 3 * kernel.shape[2]
    return jnp.concatenate(
        [jnp.pad(flat, ((0, shift), (0, 0))), jnp.pad(flat, ((shift, 0), (0, 0)))], axis=1
    )


def after(value, *earlier):
    return lax.optimization_barrier((value,) + earlier)[0]


def turned(kernel):
    return jnp.transpose(kernel[::-1, ::-1], (0, 1, 3, 2))


def flips(dp_size, tm_size):
    count = dp_size * tm_size
    digit = 1
    result = []
    while digit < count:
        result.append([(place, place ^ digit) for place in range(count)])
        digit *= 2
    return result


def halve(values, digits, pairs, place):
    for digit in digits:
        size = values.shape[0] // 2
        upper = (place >> digit) & 1
        keep = lax.dynamic_slice_in_dim(values, upper * size, size, 0)
        send = lax.dynamic_slice_in_dim(values, (1 - upper) * size, size, 0)
        values = keep + lax.ppermute(send, ("dp", "tm"), pairs[digit])
    return values


def double(values, digits, pairs, place, axis=0):
    for digit in digits:
        upper = (place >> digit) & 1
        other = lax.ppermute(values, ("dp", "tm"), pairs[digit])
        values = jnp.where(
            upper == 0,
            jnp.concatenate([values, other], axis),
            jnp.concatenate([other, values], axis),
        )
    return values


def on_chip_pair(
    dp_size,
    latents,
    cotangent,
    first_spatial,
    last_spatial,
    first_temporal,
    second_temporal,
    frame_counts,
    dilations,
):
    latents, cotangent = latents[0], cotangent[0]
    slots, rows, width, chans = latents.shape
    half = rows // 2
    tm_index = lax.axis_index("tm")
    side, core = tm_index // 2, tm_index % 2
    factor = float(dp_size * 4 * slots * rows * width) ** (-0.5)

    def ids_for(role):
        return jnp.stack(
            [side, core, frame_counts[0] - side * 2 * slots, dilations[0], dilations[1], role]
        ).astype(jnp.int32)

    ids = ids_for(side)
    swap_cores = [(0, 1), (1, 0), (2, 3), (3, 2)]
    swap_sides = [(0, 2), (2, 0), (1, 3), (3, 1)]

    w_in = two_row_weights(first_spatial)
    w_out = two_row_weights(last_spatial)
    w_in_back = two_row_weights(turned(first_spatial))
    w_out_back = two_row_weights(turned(last_spatial))
    w_one = first_temporal.reshape(-1, chans)
    w_two = second_temporal.reshape(-1, chans)
    w_one_back = jnp.transpose(first_temporal, (0, 2, 1)).reshape(-1, chans)
    w_two_back = jnp.transpose(second_temporal, (0, 2, 1)).reshape(-1, chans)
    at_zero = side == 0
    w_first = jnp.where(at_zero, w_two, w_one_back)
    w_second = jnp.where(at_zero, w_one_back, w_two)
    w_ending = jnp.where(at_zero, w_out, w_in_back)
    w_other = jnp.where(at_zero, w_in_back, w_out)

    band = rows // CHUNKS // 2
    entries, slopes = [], []
    for chunk in range(CHUNKS):
        start = chunk * 2 * band + (1 - core) * band - 1
        sent = [
            lax.dynamic_slice_in_dim(value, jnp.clip(start, 0, rows - band - 2), band + 2, 1)
            for value in (latents, cotangent)
        ]
        if chunk > 0:
            sent = [after(value, act) for value in sent]
        got = [lax.ppermute(value, "tm", swap_cores) for value in sent]
        start = chunk * 2 * band + core * band - 1
        kept = jnp.clip(start, 0, rows - band - 2)
        front_ids = jnp.concatenate([ids, jnp.stack([kept, start - kept]).astype(jnp.int32)])
        act, back, slope, leaving = front(
            front_ids, [latents, got[0]], [cotangent, got[1]], w_in, w_out_back
        )
        slopes.append(slope)
        if chunk > 0:
            leaving = after(leaving, halo)
        halo = lax.ppermute(leaving, "tm", swap_sides)
        entries.append([act, back, slope, halo])
    middles, halos, own, got = [], [], [], []
    outs = None
    sums_first = jnp.zeros((chans, 9 * chans), F32)
    for chunk in range(CHUNKS):
        act, back, slope, arrived = entries[chunk]
        made = middle(ids, act, back, slope, arrived, w_one, w_two_back, w_first)
        middles.append(made)
        own.append(made[2])
        got.append(lax.ppermute(made[3], "tm", swap_cores))
        *outs, sums_first = ending(
            chunk, factor, ids, own, got, latents, cotangent, w_ending, sums_first, outs
        )
        halo = lax.ppermute(after(made[0], halo, sums_first), "tm", swap_sides)
        halos.append(halo)

    pairs = flips(dp_size, 4)
    place = lax.axis_index("dp") * 4 + tm_index
    digits = [0] + list(range(2, len(pairs)))
    span = 9 * chans
    ids = ids_for(1 - side)
    own, got = [], []
    sums_second = jnp.zeros((chans, span), F32)
    for chunk, made in enumerate(middles):
        keep, leaving = second(ids, made[1], slopes[chunk], halos[chunk], w_second)
        own.append(keep)
        got.append(lax.ppermute(leaving, "tm", swap_cores))
        *outs, sums_second = ending(
            chunk, factor, ids, own, got, latents, cotangent, w_other, sums_second, outs
        )
        if chunk < CHUNKS - 1:
            halos[chunk + 1] = after(halos[chunk + 1], sums_second)
    decoded, latent_grad = outs

    early = jnp.concatenate(
        [
            sums_first,
            factor * sum(made[4] for made in middles),
            factor * sum(made[5] for made in middles),
        ],
        1,
    )
    early = after(early, halos[-1])
    early = halve(early, digits, pairs, place)
    late = halve(sums_second, digits, pairs, place)
    both = jnp.concatenate([early, late], 1)
    other = lax.ppermute(both, ("dp", "tm"), pairs[1])
    swapped = jnp.concatenate([other[:, -span:], other[:, span:-span], other[:, :span]], 1)
    both = both + swapped
    both = jnp.where(
        at_zero, both, jnp.concatenate([both[:, -span:], both[:, span:-span], both[:, :span]], 1)
    )
    both = double(both.astype(BF), digits[::-1], pairs, place).astype(F32)
    spatial_sums = (both[:, :span], both[:, -span:])
    temporal_sums = both[:, span:-span]

    last_grad = jnp.transpose(spatial_sums[0].reshape(chans, 3, 3, chans), (1, 2, 3, 0))
    first_grad = jnp.transpose(spatial_sums[1].reshape(chans, 3, 3, chans), (1, 2, 0, 3))
    first_grad = first_grad[::-1, ::-1]
    near_grad = jnp.transpose(temporal_sums[:, : TAPS * chans].reshape(chans, TAPS, chans), (1, 2, 0))
    far_grad = jnp.transpose(temporal_sums[:, TAPS * chans :].reshape(chans, TAPS, chans), (1, 0, 2))
    return (decoded[None], latent_grad[None], first_grad, last_grad, near_grad, far_grad)


def on_any_device(dp_size, tm_size, latents, cotangent, *rest):
    clips, slots, rows = latents.shape[:3]
    fits = clips == 1 and tm_size == 4 and slots <= REACH <= 2 * slots and rows % 8 == 0 and slots % 2 == 0
    if fits and dp_size & (dp_size - 1) == 0:
        return on_chip_pair(dp_size, latents, cotangent, *rest)
    return on_device(latents, cotangent, *rest)


def solution(mesh):
    in_specs = (
        P("dp", "tm", None, None, None),
        P("dp", "tm", None, None, None),
        P(),
        P(),
        P(),
        P(),
        P("dp"),
        P(),
    )
    out_specs = (
        P("dp", "tm", None, None, None),
        P("dp", "tm", None, None, None),
        P(),
        P(),
        P(),
        P(),
    )
    return jax.shard_map(
        functools.partial(on_any_device, mesh.shape["dp"], mesh.shape["tm"]), mesh=mesh, in_specs=in_specs, out_specs=out_specs, check_vma=False
    )
```

```python
import functools

import jax
import jax.numpy as jnp
from jax import lax
from jax.experimental import pallas as pl
from jax.experimental.pallas import tpu as pltpu
from jax.sharding import PartitionSpec as P

TAPS = 3
DILATION_MAX = 4


def silu_slope(values):
    sigma = jax.nn.sigmoid(values)
    return sigma * (1.0 + values * (1.0 - sigma))


def spatial(source, kernel):
    row_count, col_count, channels = source.shape[-3:]
    leading = source.shape[:-3]
    padded = jnp.pad(source, [(0, 0)] * len(leading) + [(1, 1), (1, 1), (0, 0)])
    summed = jnp.zeros(leading + (row_count, col_count, kernel.shape[3]), jnp.float32)
    for row_shift in range(3):
        for col_shift in range(3):
            window = padded[
                ..., row_shift : row_shift + row_count, col_shift : col_shift + col_count, :
            ]
            product = jnp.dot(
                window.reshape(-1, channels),
                kernel[row_shift, col_shift],
                preferred_element_type=jnp.float32,
            )
            summed = summed + product.reshape(summed.shape)
    return summed


def spatial_back(incoming, kernel):
    return spatial(incoming, jnp.transpose(kernel[::-1, ::-1], (0, 1, 3, 2)))


def spatial_kernel(source, incoming):
    row_count, col_count, channels = source.shape[-3:]
    leading = source.shape[:-3]
    padded = jnp.pad(source, [(0, 0)] * len(leading) + [(1, 1), (1, 1), (0, 0)])
    flat_in = incoming.reshape(-1, incoming.shape[-1])
    result_rows = []
    for row_shift in range(3):
        result_cols = []
        for col_shift in range(3):
            window = padded[
                ..., row_shift : row_shift + row_count, col_shift : col_shift + col_count, :
            ]
            result_cols.append(
                lax.dot_general(
                    window.reshape(-1, channels),
                    flat_in,
                    (((0,), (0,)), ((), ())),
                    preferred_element_type=jnp.float32,
                )
            )
        result_rows.append(jnp.stack(result_cols))
    return jnp.stack(result_rows)


def temporal(source, kernel, dilation):
    margin = (TAPS - 1) * DILATION_MAX
    slot_count = source.shape[1]
    padded = jnp.pad(source, ((0, 0), (margin, 0), (0, 0), (0, 0), (0, 0)))
    summed = jnp.zeros(source.shape[:-1] + (kernel.shape[2],), jnp.float32)
    for tap_index in range(kernel.shape[0]):
        begin_at = margin - tap_index * dilation
        window = lax.dynamic_slice_in_dim(padded, begin_at, slot_count, 1)
        product = jnp.dot(
            window.reshape(-1, source.shape[-1]),
            kernel[tap_index],
            preferred_element_type=jnp.float32,
        )
        summed = summed + product.reshape(summed.shape)
    return summed


def temporal_back(incoming, kernel, dilation):
    margin = (TAPS - 1) * DILATION_MAX
    slot_count = incoming.shape[1]
    padded = jnp.pad(incoming, ((0, 0), (0, margin), (0, 0), (0, 0), (0, 0)))
    summed = jnp.zeros(incoming.shape[:-1] + (kernel.shape[1],), jnp.float32)
    for tap_index in range(kernel.shape[0]):
        begin_at = tap_index * dilation
        window = lax.dynamic_slice_in_dim(padded, begin_at, slot_count, 1)
        product = jnp.dot(
            window.reshape(-1, incoming.shape[-1]),
            kernel[tap_index].T,
            preferred_element_type=jnp.float32,
        )
        summed = summed + product.reshape(summed.shape)
    return summed


def temporal_kernel(source, incoming, dilation):
    margin = (TAPS - 1) * DILATION_MAX
    slot_count = source.shape[1]
    padded = jnp.pad(source, ((0, 0), (margin, 0), (0, 0), (0, 0), (0, 0)))
    flat_in = incoming.reshape(-1, incoming.shape[-1])
    result = []
    for tap_index in range(TAPS):
        begin_at = margin - tap_index * dilation
        window = lax.dynamic_slice_in_dim(padded, begin_at, slot_count, 1)
        result.append(
            lax.dot_general(
                window.reshape(-1, source.shape[-1]),
                flat_in,
                (((0,), (0,)), ((), ())),
                preferred_element_type=jnp.float32,
            )
        )
    return jnp.stack(result)


def forward_bands(band_in, first_temporal, second_temporal, dilations):
    pre_mid = temporal(band_in, first_temporal, dilations[0])
    act_mid = jax.nn.silu(pre_mid).astype(jnp.bfloat16)
    act_out = temporal(act_mid, second_temporal, dilations[1]).astype(jnp.bfloat16)
    return (pre_mid, act_mid, act_out)


def on_device(
    latents,
    cotangent,
    first_spatial,
    last_spatial,
    first_temporal,
    second_temporal,
    frame_counts,
    dilations,
):
    local_slots = latents.shape[1]
    first_slot = lax.axis_index("tm") * local_slots
    slot_ids = first_slot + jnp.arange(local_slots, dtype=jnp.int32)
    is_valid = (slot_ids[None, :] < frame_counts[:, None])[:, :, None, None, None]
    total_count = (
        latents.shape[0]
        * lax.axis_size("dp")
        * local_slots
        * lax.axis_size("tm")
        * latents.shape[2]
        * latents.shape[3]
    )
    factor = float(total_count) ** (-0.5)
    pre_in = spatial(latents, first_spatial)
    act_in = jax.nn.silu(pre_in).astype(jnp.bfloat16)
    masked = jnp.where(is_valid, cotangent, jnp.zeros_like(cotangent))
    band_in = lax.all_to_all(act_in, "tm", split_axis=2, concat_axis=1, tiled=True)
    pre_mid, act_mid, act_out = forward_bands(band_in, first_temporal, second_temporal, dilations)
    back_out = spatial_back(masked, last_spatial).astype(jnp.bfloat16)
    band_back = lax.all_to_all(back_out, "tm", split_axis=2, concat_axis=1, tiled=True)
    second_grad = temporal_kernel(act_mid, band_back, dilations[1])
    slope_mid = (
        temporal_back(band_back, second_temporal, dilations[1]) * silu_slope(pre_mid)
    ).astype(jnp.bfloat16)
    first_grad = temporal_kernel(band_in, slope_mid, dilations[0])
    back_in = temporal_back(slope_mid, first_temporal, dilations[0]).astype(jnp.bfloat16)
    frame_out, frame_back = (
        lax.all_to_all(act_out, "tm", split_axis=1, concat_axis=2, tiled=True),
        lax.all_to_all(back_in, "tm", split_axis=1, concat_axis=2, tiled=True),
    )
    decoded = jnp.where(
        is_valid, latents.astype(jnp.float32) + spatial(frame_out, last_spatial), jnp.float32(0.0)
    ).astype(jnp.bfloat16)
    last_grad = spatial_kernel(frame_out, masked)
    slope_in = (frame_back.astype(jnp.float32) * silu_slope(pre_in)).astype(jnp.bfloat16)
    spatial_grad = spatial_kernel(latents, slope_in)
    latent_grad = (masked.astype(jnp.float32) + spatial_back(slope_in, first_spatial)).astype(
        jnp.bfloat16
    )
    partials = (
        factor * spatial_grad,
        factor * last_grad,
        factor * first_grad,
        factor * second_grad,
    )
    reduced = lax.psum((partials[0], partials[1], partials[2], partials[3]), ("dp", "tm"))
    return (decoded, latent_grad, reduced[0], reduced[1], reduced[2], reduced[3])


REACH = (TAPS - 1) * DILATION_MAX
CHUNKS = 2
VMEM_LIMIT = 52 * 1024 * 1024
BF = jnp.bfloat16
F32 = jnp.float32


def params():
    return pltpu.CompilerParams(
        dimension_semantics=("arbitrary",), vmem_limit_bytes=VMEM_LIMIT
    )


COST = 0.02


def cost(micros):
    return pl.CostEstimate(flops=int(micros * COST * 1e9), bytes_accessed=1000, transcendentals=0)


def pair_range(chunk, rows):
    size = rows // CHUNKS
    low = 0 if chunk == 0 else chunk * size // 2 - 1
    high = rows // 2 if chunk == CHUNKS - 1 else (chunk + 1) * size // 2 - 1
    return low, high


def seen_rows(low, high, rows):
    return max(0, 2 * low - 1), min(rows, 2 * high + 1)


def zero_borders(pad, pairs, low, high, rows):
    pad[...] = jnp.zeros(pad.shape, F32)
    frames, _, width, lanes = pairs.shape
    for frame in range(frames):
        if low == 0:
            pairs[frame, 0, :, 0 : lanes // 2] = jnp.zeros((width, lanes // 2), BF)
        if 2 * high == rows:
            pairs[frame, high - low, :, lanes // 2 : lanes] = jnp.zeros((width, lanes // 2), BF)


def fill_pairs(read_row, pad, pairs, low, high, rows):
    frames, _, width, lanes = pairs.shape
    chans = lanes // 6
    begin, end = seen_rows(low, high, rows)
    for frame in range(frames):
        for row in range(begin, end):
            pad[frame, row - begin, 8 : 8 + width, :] = read_row(frame, row).astype(F32)
    for frame in range(frames):
        for row in range(begin, end):
            at = (row + 1) // 2 - low
            side = 3 * chans * (1 - row % 2)
            pairs[frame, at, :, side + chans : side + 2 * chans] = read_row(frame, row)
            for shift in (0, 2):
                seen = pad[frame, row - begin, 7 + shift : 7 + shift + width, :].astype(BF)
                lane = side + shift * chans
                pairs[frame, at, :, lane : lane + chans] = seen


def front_kernel(slots, ids, *refs):
    latents, cotangent = refs[0:2], refs[2:4]
    w_in, w_back, act, back, slope, leaving, pads, windows = refs[4:]
    at = pl.program_id(0)
    side, core, shift_rows = ids[0], ids[1], ids[7]
    spread, width, chans = latents[0].shape[1:]
    count = spread // 2 - 1
    lanes = 6 * chans

    @pl.when(at == 0)
    def _():
        pads[...] = jnp.zeros(pads.shape, F32)

    def conv(blocks, weights, pad, pairs):
        for index in range(2):
            for row in range(spread):
                place = index * (spread + 2) + 1 + row
                pad[place, 8 : 8 + width, :] = blocks[index][0, row].astype(F32)
        for index in range(2):
            for row in range(spread):
                place = index * (spread + 2) + 1 + row + shift_rows
                side = 3 * chans * (row % 2)
                to = index * (count + 1) + row // 2
                for shift in range(3):
                    seen = pad[place, 7 + shift : 7 + shift + width, :].astype(BF)
                    pairs[to, :, side + shift * chans : side + (shift + 1) * chans] = seen
        stacked = []
        for lower in range(2):
            both = [
                pairs[index * (count + 1) + lower : index * (count + 1) + lower + count]
                for index in range(2)
            ]
            stacked.append(jnp.concatenate(both, axis=0).reshape(2 * count * width, lanes))
        return jnp.dot(
            jnp.concatenate(stacked, axis=1), weights[...], preferred_element_type=F32
        )

    def store(target, values):
        values = values.reshape(2 * count, width, 2 * chans)
        for index in range(2):
            owner = core if index == 0 else 1 - core
            for row in range(2 * count):
                lane = row % 2 * chans
                target[owner, 0, row] = values[index * count + row // 2, :, lane : lane + chans]

    pre = conv(latents, w_in, pads.at[0], windows.at[0])
    summed = conv(cotangent, w_back, pads.at[1], windows.at[1])
    sigma = jax.nn.sigmoid(pre)
    store(act, (pre * sigma).astype(BF))
    store(slope, (sigma * (1.0 + pre * (1.0 - sigma))).astype(BF))
    half = count * width
    mine = jnp.where(core * slots + at < ids[2], 1.0, 0.0).astype(F32)
    other = jnp.where((1 - core) * slots + at < ids[2], 1.0, 0.0).astype(F32)
    store(back, jnp.concatenate([summed[:half] * mine, summed[half:] * other], 0).astype(BF))

    tail = leaving.shape[0] - slots

    @pl.when(side == 0)
    def _():
        leaving[at + tail] = act[1, 0]

    @pl.when((side == 0) & (at >= slots - tail))
    def _():
        leaving[at - (slots - tail)] = act[0, 0]

    @pl.when(side == 1)
    def _():
        leaving[at] = back[0, 0]

    @pl.when((side == 1) & (at < tail))
    def _():
        leaving[slots + at] = back[1, 0]


def front(ids, latents, cotangent, w_in, w_back):
    slots, spread, width, chans = latents[1].shape
    rows = spread - 2
    own = pl.BlockSpec(
        (pl.Element(1), pl.Element(spread), pl.Element(width), pl.Element(chans)),
        lambda i, ids: (i, ids[6], 0, 0),
    )
    got = pl.BlockSpec((1, spread, width, chans), lambda i, ids: (i, 0, 0, 0))
    target = pl.BlockSpec((2, 1, rows, width, chans), lambda i, ids: (0, i, 0, 0, 0))
    fixed = pl.BlockSpec(w_in.shape, lambda i, ids: (0, 0))
    made = pl.pallas_call(
        functools.partial(front_kernel, slots),
        grid_spec=pltpu.PrefetchScalarGridSpec(
            num_scalar_prefetch=1,
            grid=(slots,),
            in_specs=[own, got, own, got, fixed, fixed],
            out_specs=[
                target, target, target,
                pl.BlockSpec((REACH, rows, width, chans), lambda i, ids: (0, 0, 0, 0)),
            ],
            scratch_shapes=[
                pltpu.VMEM((2, 2 * (spread + 2), width + 16, chans), F32),
                pltpu.VMEM((2, spread, width, 6 * chans), BF),
            ],
        ),
        out_shape=[jax.ShapeDtypeStruct((2, slots, rows, width, chans), BF)] * 3
        + [jax.ShapeDtypeStruct((REACH, rows, width, chans), BF)],
        compiler_params=params(),
        cost_estimate=cost(22.0 / CHUNKS),
        name="front",
    )(ids, *latents, *cotangent, w_in, w_back)
    return [value.reshape(-1, rows, width, chans) for value in made]


def taps_of(held, start, step, count):
    size = held.shape[1]
    chans = held.shape[2]
    seen = []
    for tap in range(TAPS):
        seen.append(held[pl.ds(start + tap * step, count)].reshape(count * size, chans))
    return jnp.concatenate(seen, axis=1)


def outer(left, right):
    return lax.dot_general(left, right, (((0,), (0,)), ((), ())), preferred_element_type=F32)


def middle_kernel(
    ids, act_in, act_back, slope, halo, w_mid, w_mid_back, w_first,
    mid_send, mid_keep, first_keep, first_send, grad_first, grad_second,
    held_in, held_back, held_mid, result,
):
    at = pl.program_id(0)
    side, core, near, far = ids[0], ids[1], ids[3], ids[4]
    frames = act_in.shape[0]
    slots = frames // 2
    mine = core * slots
    other = slots - mine

    @pl.when(at == 0)
    def _():
        blank = jnp.zeros((REACH,) + held_in.shape[1:], BF)
        held_mid[0:REACH] = blank
        held_mid[REACH + frames : 2 * REACH + frames] = blank
        grad_first[...] = jnp.zeros_like(grad_first)
        grad_second[...] = jnp.zeros_like(grad_second)

    held_in[REACH : REACH + frames] = act_in[:, 0]
    held_back[0:frames] = act_back[:, 0]

    one = side.astype(F32)
    held_in[0:REACH] = (halo[:, 0].astype(F32) * one).astype(BF)
    held_back[frames : frames + REACH] = (halo[:, 0].astype(F32) * (1.0 - one)).astype(BF)

    size, chans = held_in.shape[1:]
    taps_in = taps_of(held_in, REACH, -near, frames)
    taps_back = taps_of(held_back, 0, far, frames)
    pre = jnp.dot(taps_in, w_mid[...], preferred_element_type=F32)
    sigma = jax.nn.sigmoid(pre)
    act = (pre * sigma).astype(BF)
    back = jnp.dot(taps_back, w_mid_back[...], preferred_element_type=F32)
    grad = (back * (sigma * (1.0 + pre * (1.0 - sigma)))).astype(BF)
    grad_second[...] += outer(act, taps_back)
    grad_first[...] += outer(grad, taps_in)
    act = act.reshape(frames, size, chans)
    grad = grad.reshape(frames, size, chans)

    ours = jnp.where(side == 0, act, grad)
    held_mid[REACH : REACH + frames] = ours
    mid_keep[:, 0] = jnp.where(side == 0, grad, act)
    mid_send[:, 0] = held_mid[pl.ds(REACH + (1 - side) * (frames - REACH), REACH)]
    step = jnp.where(side == 0, -far, near)
    first = jnp.dot(
        taps_of(held_mid, REACH, step, frames), w_first[...], preferred_element_type=F32
    )
    first = first.astype(BF).reshape(frames, size, chans).astype(F32)
    result[...] = (first * (slope[:, 0].astype(F32) * one + (1.0 - one))).astype(BF)
    first_keep[:, 0] = result[pl.ds(mine, slots)]
    first_send[:, 0] = result[pl.ds(other, slots)]


def middle(ids, act_in, act_back, slope, halo, w_mid, w_mid_back, w_first):
    frames, rows, width, chans = act_in.shape
    slots = frames // 2
    fixed = pl.BlockSpec(w_mid.shape, lambda i, ids: (0, 0))
    sums = pl.BlockSpec((chans, TAPS * chans), lambda i, ids: (0, 0))

    def rowwise(count):
        return pl.BlockSpec((count, 1, width, chans), lambda i, ids: (0, i, 0, 0))

    def shaped(count):
        return jax.ShapeDtypeStruct((count, rows, width, chans), BF)

    summed = jax.ShapeDtypeStruct((chans, TAPS * chans), F32)
    return pl.pallas_call(
        middle_kernel,
        grid_spec=pltpu.PrefetchScalarGridSpec(
            num_scalar_prefetch=1,
            grid=(rows,),
            in_specs=[rowwise(frames)] * 3 + [rowwise(REACH), fixed, fixed, fixed],
            out_specs=[
                rowwise(REACH), rowwise(frames), rowwise(slots), rowwise(slots), sums, sums,
            ],
            scratch_shapes=[
                pltpu.VMEM((REACH + frames, width, chans), BF),
                pltpu.VMEM((REACH + frames, width, chans), BF),
                pltpu.VMEM((2 * REACH + frames, width, chans), BF),
                pltpu.VMEM((frames, width, chans), BF),
            ],
        ),
        out_shape=[
            shaped(REACH), shaped(frames), shaped(slots), shaped(slots), summed, summed,
        ],
        compiler_params=params(),
        cost_estimate=cost(24.0 / CHUNKS),
        name="middle",
    )(ids, act_in, act_back, slope, halo, w_mid, w_mid_back, w_first)


def second_kernel(ids, mid, slope, halo, w_second, keep, send, held, result):
    side, core, near, far = ids[0], ids[1], ids[3], ids[4]
    frames, each = mid.shape[:2]
    slots = frames // 2
    mine = core * slots
    size, chans = held.shape[2:]
    one = side.astype(F32)
    step = jnp.where(side == 0, near, -far)
    for row in range(each):
        held[row, 0:REACH] = (halo[:, row].astype(F32) * one).astype(BF)
        held[row, REACH : REACH + frames] = mid[:, row]
        held[row, REACH + frames :] = (halo[:, row].astype(F32) * (1.0 - one)).astype(BF)
        made = jnp.dot(
            taps_of(held.at[row], REACH, step, frames), w_second[...], preferred_element_type=F32
        )
        made = made.astype(BF).reshape(frames, size, chans).astype(F32)
        result[row] = (made * (slope[:, row].astype(F32) * (1.0 - one) + one)).astype(BF)
        keep[:, row] = result[row, pl.ds(mine, slots)]
        send[:, row] = result[row, pl.ds(slots - mine, slots)]


def second(ids, mid, slope, halo, w_second):
    frames, rows, width, chans = mid.shape
    slots = frames // 2
    each = 2

    def rowwise(count):
        return pl.BlockSpec((count, each, width, chans), lambda i, ids: (0, i, 0, 0))

    shape = jax.ShapeDtypeStruct((slots, rows, width, chans), BF)
    return pl.pallas_call(
        second_kernel,
        grid_spec=pltpu.PrefetchScalarGridSpec(
            num_scalar_prefetch=1,
            grid=(rows // each,),
            in_specs=[
                rowwise(frames), rowwise(frames), rowwise(REACH),
                pl.BlockSpec(w_second.shape, lambda i, ids: (0, 0)),
            ],
            out_specs=[rowwise(slots), rowwise(slots)],
            scratch_shapes=[
                pltpu.VMEM((each, 2 * REACH + frames, width, chans), BF),
                pltpu.VMEM((each, frames, width, chans), BF),
            ],
        ),
        out_shape=[shape, shape],
        compiler_params=params(),
        cost_estimate=cost(10.0 / CHUNKS),
        name="second",
    )(ids, mid, slope, halo, w_second)


def ending_kernel(chunk, rows, factor, with_outs, ids, *refs):
    refs = list(refs)
    used = 1 if chunk == 0 else 2
    own = [refs.pop(0) for _ in range(used)]
    got = [refs.pop(0) for _ in range(used)]
    latents, cotangent, weights, before = [refs.pop(0) for _ in range(4)]
    if with_outs:
        refs.pop(0), refs.pop(0)
    outs = (refs.pop(0), refs.pop(0))
    sums, pad, pairs, frame, buffer, sems, beside, total = refs
    at = pl.program_id(0)
    last = pl.num_programs(0) - 1
    core, role = ids[1], ids[5]
    frames, _, width, lanes = pairs.shape
    chans = lanes // 6
    low, high = pair_range(chunk, rows)
    size = rows // CHUNKS
    half = size // 2
    base = (chunk + 1 - used) * size
    count = high - low

    def each_copy(step, act):
        for way in range(2):
            @pl.when(role == way)
            def _():
                target = outs[way].at[pl.ds(step * frames, frames), pl.ds(2 * low, 2 * count)]
                act(pltpu.make_async_copy(buffer.at[step % 2], target, sems.at[step % 2]))

    @pl.when(at == 0)
    def _():
        zero_borders(pad, pairs, low, high, rows)
        total[...] = jnp.zeros_like(total)

    @pl.when(at >= 2)
    def _():
        each_copy(at - 2, lambda copy: copy.wait())

    for index in range(used):
        frame[:, pl.ds(index * size + core * half, half)] = own[index][...]
        frame[:, pl.ds(index * size + half - core * half, half)] = got[index][...]
    fill_pairs(lambda which, row: frame[which, row - base], pad, pairs, low, high, rows)
    slot = at % 2
    one = jnp.where(role == 1, 1.0, 0.0).astype(F32)
    for which in range(frames):
        place = (core * (last + 1) + at) * frames + which
        valid = jnp.where(place < ids[2], 1.0, 0.0).astype(F32)
        zero = (1.0 - one) * valid
        upper = pairs[which, 0:count].reshape(count * width, lanes)
        lower = pairs[which, 1 : 1 + count].reshape(count * width, lanes)
        made = jnp.dot(
            jnp.concatenate([upper, lower], axis=1), weights[...], preferred_element_type=F32
        )
        made = made.reshape(count, width, 2 * chans)
        for row in range(2 * count):
            lane = row % 2 * chans
            latent = latents[which, row].astype(F32)
            arriving = cotangent[which, row].astype(F32)
            beside[which, row // 2, :, lane : lane + chans] = (
                latent * one + arriving * zero
            ).astype(BF)
            buffer[slot, which, row] = (
                latent * zero
                + arriving * (one * valid)
                + made[row // 2, :, lane : lane + chans] * (one + zero)
            ).astype(BF)
    flat = beside[...].reshape(frames * count * width, 2 * chans)
    for part in range(2):
        seen = pairs[:, part : part + count].reshape(frames * count * width, lanes)
        total[:, part * lanes : (part + 1) * lanes] += outer(flat, seen)
    each_copy(at, lambda copy: copy.start())

    @pl.when(at == last)
    def _():
        span = 9 * chans
        sums[...] = before[...] + factor * (
            total[0:chans, 0:span] + total[chans : 2 * chans, 3 * chans : 3 * chans + span]
        )
        each_copy(at - 1, lambda copy: copy.wait())
        each_copy(at, lambda copy: copy.wait())


def ending(chunk, factor, ids, own, got, latents, cotangent, weights, before, outs=None):
    slots, rows, width, chans = latents.shape
    size = rows // CHUNKS
    low, high = pair_range(chunk, rows)
    count = high - low
    begin, end = seen_rows(low, high, rows)
    used = 1 if chunk == 0 else 2
    each = 2
    area = pl.BlockSpec(
        (pl.Element(each), pl.Element(2 * count), pl.Element(width), pl.Element(chans)),
        lambda i, ids: (i * each, 2 * low, 0, 0),
    )
    part = pl.BlockSpec((each, size // 2, width, chans), lambda i, ids: (i, 0, 0, 0))
    summed = pl.BlockSpec((chans, 9 * chans), lambda i, ids: (0, 0))
    anywhere = pl.BlockSpec(memory_space=pl.ANY)
    pick = slice(chunk + 1 - used, chunk + 1)
    args = [*own[pick], *got[pick], latents, cotangent, weights, before]
    in_specs = [part] * (2 * used) + [area, area]
    in_specs += [pl.BlockSpec(weights.shape, lambda i, ids: (0, 0)), summed]
    aliases = {}
    if outs is not None:
        aliases = {1 + len(args): 0, 2 + len(args): 1}
        args += list(outs)
        in_specs += [anywhere, anywhere]
    return pl.pallas_call(
        functools.partial(ending_kernel, chunk, rows, factor, outs is not None),
        grid_spec=pltpu.PrefetchScalarGridSpec(
            num_scalar_prefetch=1,
            grid=(slots // each,),
            in_specs=in_specs,
            out_specs=[anywhere, anywhere, summed],
            scratch_shapes=[
                pltpu.VMEM((each, end - begin, width + 16, chans), F32),
                pltpu.VMEM((each, count + 1, width, 6 * chans), BF),
                pltpu.VMEM((each, used * size, width, chans), BF),
                pltpu.VMEM((2, each, 2 * count, width, chans), BF),
                pltpu.SemaphoreType.DMA((2,)),
                pltpu.VMEM((each, count, width, 2 * chans), BF),
                pltpu.VMEM((2 * chans, 12 * chans), F32),
            ],
        ),
        out_shape=[
            jax.ShapeDtypeStruct(latents.shape, BF),
            jax.ShapeDtypeStruct(latents.shape, BF),
            jax.ShapeDtypeStruct((chans, 9 * chans), F32),
        ],
        input_output_aliases=aliases,
        compiler_params=params(),
        cost_estimate=cost(26.0 / CHUNKS),
        name="ending",
    )(ids, *args)


def two_row_weights(kernel):
    flat = kernel.reshape(-1, kernel.shape[3])
    shift = 3 * kernel.shape[2]
    return jnp.concatenate(
        [jnp.pad(flat, ((0, shift), (0, 0))), jnp.pad(flat, ((shift, 0), (0, 0)))], axis=1
    )


def after(value, *earlier):
    return lax.optimization_barrier((value,) + earlier)[0]


def turned(kernel):
    return jnp.transpose(kernel[::-1, ::-1], (0, 1, 3, 2))


def flips(dp_size, tm_size):
    count = dp_size * tm_size
    digit = 1
    result = []
    while digit < count:
        result.append([(place, place ^ digit) for place in range(count)])
        digit *= 2
    return result


def halve(values, digits, pairs, place):
    for digit in digits:
        size = values.shape[0] // 2
        upper = (place >> digit) & 1
        keep = lax.dynamic_slice_in_dim(values, upper * size, size, 0)
        send = lax.dynamic_slice_in_dim(values, (1 - upper) * size, size, 0)
        values = keep + lax.ppermute(send, ("dp", "tm"), pairs[digit])
    return values


def double(values, digits, pairs, place, axis=0):
    for digit in digits:
        upper = (place >> digit) & 1
        other = lax.ppermute(values, ("dp", "tm"), pairs[digit])
        values = jnp.where(
            upper == 0,
            jnp.concatenate([values, other], axis),
            jnp.concatenate([other, values], axis),
        )
    return values


def on_chip_pair(
    dp_size,
    latents,
    cotangent,
    first_spatial,
    last_spatial,
    first_temporal,
    second_temporal,
    frame_counts,
    dilations,
):
    latents, cotangent = latents[0], cotangent[0]
    slots, rows, width, chans = latents.shape
    half = rows // 2
    tm_index = lax.axis_index("tm")
    side, core = tm_index // 2, tm_index % 2
    factor = float(dp_size * 4 * slots * rows * width) ** (-0.5)

    def ids_for(role):
        return jnp.stack(
            [side, core, frame_counts[0] - side * 2 * slots, dilations[0], dilations[1], role]
        ).astype(jnp.int32)

    ids = ids_for(side)
    swap_cores = [(0, 1), (1, 0), (2, 3), (3, 2)]
    swap_sides = [(0, 2), (2, 0), (1, 3), (3, 1)]

    w_in = two_row_weights(first_spatial)
    w_out = two_row_weights(last_spatial)
    w_in_back = two_row_weights(turned(first_spatial))
    w_out_back = two_row_weights(turned(last_spatial))
    w_one = first_temporal.reshape(-1, chans)
    w_two = second_temporal.reshape(-1, chans)
    w_one_back = jnp.transpose(first_temporal, (0, 2, 1)).reshape(-1, chans)
    w_two_back = jnp.transpose(second_temporal, (0, 2, 1)).reshape(-1, chans)
    at_zero = side == 0
    w_first = jnp.where(at_zero, w_two, w_one_back)
    w_second = jnp.where(at_zero, w_one_back, w_two)
    w_ending = jnp.where(at_zero, w_out, w_in_back)
    w_other = jnp.where(at_zero, w_in_back, w_out)

    band = rows // CHUNKS // 2
    entries, slopes = [], []
    for chunk in range(CHUNKS):
        start = chunk * 2 * band + (1 - core) * band - 1
        sent = [
            lax.dynamic_slice_in_dim(value, jnp.clip(start, 0, rows - band - 2), band + 2, 1)
            for value in (latents, cotangent)
        ]
        if chunk > 0:
            sent = [after(value, act) for value in sent]
        got = [lax.ppermute(value, "tm", swap_cores) for value in sent]
        start = chunk * 2 * band + core * band - 1
        kept = jnp.clip(start, 0, rows - band - 2)
        front_ids = jnp.concatenate([ids, jnp.stack([kept, start - kept]).astype(jnp.int32)])
        act, back, slope, leaving = front(
            front_ids, [latents, got[0]], [cotangent, got[1]], w_in, w_out_back
        )
        slopes.append(slope)
        if chunk > 0:
            leaving = after(leaving, halo)
        halo = lax.ppermute(leaving, "tm", swap_sides)
        entries.append([act, back, slope, halo])
    middles, halos, own, got = [], [], [], []
    outs = None
    sums_first = jnp.zeros((chans, 9 * chans), F32)
    for chunk in range(CHUNKS):
        act, back, slope, arrived = entries[chunk]
        made = middle(ids, act, back, slope, arrived, w_one, w_two_back, w_first)
        middles.append(made)
        own.append(made[2])
        got.append(lax.ppermute(made[3], "tm", swap_cores))
        *outs, sums_first = ending(
            chunk, factor, ids, own, got, latents, cotangent, w_ending, sums_first, outs
        )
        halo = lax.ppermute(after(made[0], halo, sums_first), "tm", swap_sides)
        halos.append(halo)

    pairs = flips(dp_size, 4)
    place = lax.axis_index("dp") * 4 + tm_index
    digits = [0] + list(range(2, len(pairs)))
    span = 9 * chans
    ids = ids_for(1 - side)
    own, got = [], []
    sums_second = jnp.zeros((chans, span), F32)
    for chunk, made in enumerate(middles):
        keep, leaving = second(ids, made[1], slopes[chunk], halos[chunk], w_second)
        own.append(keep)
        got.append(lax.ppermute(leaving, "tm", swap_cores))
        *outs, sums_second = ending(
            chunk, factor, ids, own, got, latents, cotangent, w_other, sums_second, outs
        )
        if chunk < CHUNKS - 1:
            halos[chunk + 1] = after(halos[chunk + 1], sums_second)
    decoded, latent_grad = outs

    early = jnp.concatenate(
        [
            sums_first,
            factor * sum(made[4] for made in middles),
            factor * sum(made[5] for made in middles),
        ],
        1,
    )
    early = after(early, halos[-1])
    early = halve(early, digits, pairs, place)
    late = halve(sums_second, digits, pairs, place)
    both = jnp.concatenate([early, late], 1)
    other = lax.ppermute(both, ("dp", "tm"), pairs[1])
    swapped = jnp.concatenate([other[:, -span:], other[:, span:-span], other[:, :span]], 1)
    both = both + swapped
    both = jnp.where(
        at_zero, both, jnp.concatenate([both[:, -span:], both[:, span:-span], both[:, :span]], 1)
    )
    both = double(both.astype(BF), digits[::-1], pairs, place).astype(F32)
    spatial_sums = (both[:, :span], both[:, -span:])
    temporal_sums = both[:, span:-span]

    last_grad = jnp.transpose(spatial_sums[0].reshape(chans, 3, 3, chans), (1, 2, 3, 0))
    first_grad = jnp.transpose(spatial_sums[1].reshape(chans, 3, 3, chans), (1, 2, 0, 3))
    first_grad = first_grad[::-1, ::-1]
    near_grad = jnp.transpose(temporal_sums[:, : TAPS * chans].reshape(chans, TAPS, chans), (1, 2, 0))
    far_grad = jnp.transpose(temporal_sums[:, TAPS * chans :].reshape(chans, TAPS, chans), (1, 0, 2))
    return (decoded[None], latent_grad[None], first_grad, last_grad, near_grad, far_grad)


def on_any_device(dp_size, tm_size, latents, cotangent, *rest):
    clips, slots, rows = latents.shape[:3]
    fits = clips == 1 and tm_size == 4 and slots <= REACH <= 2 * slots and rows % 8 == 0 and slots % 2 == 0
    if fits and dp_size & (dp_size - 1) == 0:
        return on_chip_pair(dp_size, latents, cotangent, *rest)
    return on_device(latents, cotangent, *rest)


def solution(mesh):
    in_specs = (
        P("dp", "tm", None, None, None),
        P("dp", "tm", None, None, None),
        P(),
        P(),
        P(),
        P(),
        P("dp"),
        P(),
    )
    out_specs = (
        P("dp", "tm", None, None, None),
        P("dp", "tm", None, None, None),
        P(),
        P(),
        P(),
        P(),
    )
    return jax.shard_map(
        functools.partial(on_any_device, mesh.shape["dp"], mesh.shape["tm"]), mesh=mesh, in_specs=in_specs, out_specs=out_specs, check_vma=False
    )
```

```python
import functools

import jax
import jax.numpy as jnp
from jax import lax
from jax.experimental import pallas as pl
from jax.experimental.pallas import tpu as pltpu
from jax.sharding import PartitionSpec as P

TAPS = 3
DILATION_MAX = 4


def silu_slope(values):
    sigma = jax.nn.sigmoid(values)
    return sigma * (1.0 + values * (1.0 - sigma))


def spatial(source, kernel):
    row_count, col_count, channels = source.shape[-3:]
    leading = source.shape[:-3]
    padded = jnp.pad(source, [(0, 0)] * len(leading) + [(1, 1), (1, 1), (0, 0)])
    summed = jnp.zeros(leading + (row_count, col_count, kernel.shape[3]), jnp.float32)
    for row_shift in range(3):
        for col_shift in range(3):
            window = padded[
                ..., row_shift : row_shift + row_count, col_shift : col_shift + col_count, :
            ]
            product = jnp.dot(
                window.reshape(-1, channels),
                kernel[row_shift, col_shift],
                preferred_element_type=jnp.float32,
            )
            summed = summed + product.reshape(summed.shape)
    return summed


def spatial_back(incoming, kernel):
    return spatial(incoming, jnp.transpose(kernel[::-1, ::-1], (0, 1, 3, 2)))


def spatial_kernel(source, incoming):
    row_count, col_count, channels = source.shape[-3:]
    leading = source.shape[:-3]
    padded = jnp.pad(source, [(0, 0)] * len(leading) + [(1, 1), (1, 1), (0, 0)])
    flat_in = incoming.reshape(-1, incoming.shape[-1])
    result_rows = []
    for row_shift in range(3):
        result_cols = []
        for col_shift in range(3):
            window = padded[
                ..., row_shift : row_shift + row_count, col_shift : col_shift + col_count, :
            ]
            result_cols.append(
                lax.dot_general(
                    window.reshape(-1, channels),
                    flat_in,
                    (((0,), (0,)), ((), ())),
                    preferred_element_type=jnp.float32,
                )
            )
        result_rows.append(jnp.stack(result_cols))
    return jnp.stack(result_rows)


def temporal(source, kernel, dilation):
    margin = (TAPS - 1) * DILATION_MAX
    slot_count = source.shape[1]
    padded = jnp.pad(source, ((0, 0), (margin, 0), (0, 0), (0, 0), (0, 0)))
    summed = jnp.zeros(source.shape[:-1] + (kernel.shape[2],), jnp.float32)
    for tap_index in range(kernel.shape[0]):
        begin_at = margin - tap_index * dilation
        window = lax.dynamic_slice_in_dim(padded, begin_at, slot_count, 1)
        product = jnp.dot(
            window.reshape(-1, source.shape[-1]),
            kernel[tap_index],
            preferred_element_type=jnp.float32,
        )
        summed = summed + product.reshape(summed.shape)
    return summed


def temporal_back(incoming, kernel, dilation):
    margin = (TAPS - 1) * DILATION_MAX
    slot_count = incoming.shape[1]
    padded = jnp.pad(incoming, ((0, 0), (0, margin), (0, 0), (0, 0), (0, 0)))
    summed = jnp.zeros(incoming.shape[:-1] + (kernel.shape[1],), jnp.float32)
    for tap_index in range(kernel.shape[0]):
        begin_at = tap_index * dilation
        window = lax.dynamic_slice_in_dim(padded, begin_at, slot_count, 1)
        product = jnp.dot(
            window.reshape(-1, incoming.shape[-1]),
            kernel[tap_index].T,
            preferred_element_type=jnp.float32,
        )
        summed = summed + product.reshape(summed.shape)
    return summed


def temporal_kernel(source, incoming, dilation):
    margin = (TAPS - 1) * DILATION_MAX
    slot_count = source.shape[1]
    padded = jnp.pad(source, ((0, 0), (margin, 0), (0, 0), (0, 0), (0, 0)))
    flat_in = incoming.reshape(-1, incoming.shape[-1])
    result = []
    for tap_index in range(TAPS):
        begin_at = margin - tap_index * dilation
        window = lax.dynamic_slice_in_dim(padded, begin_at, slot_count, 1)
        result.append(
            lax.dot_general(
                window.reshape(-1, source.shape[-1]),
                flat_in,
                (((0,), (0,)), ((), ())),
                preferred_element_type=jnp.float32,
            )
        )
    return jnp.stack(result)


def forward_bands(band_in, first_temporal, second_temporal, dilations):
    pre_mid = temporal(band_in, first_temporal, dilations[0])
    act_mid = jax.nn.silu(pre_mid).astype(jnp.bfloat16)
    act_out = temporal(act_mid, second_temporal, dilations[1]).astype(jnp.bfloat16)
    return (pre_mid, act_mid, act_out)


def on_device(
    latents,
    cotangent,
    first_spatial,
    last_spatial,
    first_temporal,
    second_temporal,
    frame_counts,
    dilations,
):
    local_slots = latents.shape[1]
    first_slot = lax.axis_index("tm") * local_slots
    slot_ids = first_slot + jnp.arange(local_slots, dtype=jnp.int32)
    is_valid = (slot_ids[None, :] < frame_counts[:, None])[:, :, None, None, None]
    total_count = (
        latents.shape[0]
        * lax.axis_size("dp")
        * local_slots
        * lax.axis_size("tm")
        * latents.shape[2]
        * latents.shape[3]
    )
    factor = float(total_count) ** (-0.5)
    pre_in = spatial(latents, first_spatial)
    act_in = jax.nn.silu(pre_in).astype(jnp.bfloat16)
    masked = jnp.where(is_valid, cotangent, jnp.zeros_like(cotangent))
    band_in = lax.all_to_all(act_in, "tm", split_axis=2, concat_axis=1, tiled=True)
    pre_mid, act_mid, act_out = forward_bands(band_in, first_temporal, second_temporal, dilations)
    back_out = spatial_back(masked, last_spatial).astype(jnp.bfloat16)
    band_back = lax.all_to_all(back_out, "tm", split_axis=2, concat_axis=1, tiled=True)
    second_grad = temporal_kernel(act_mid, band_back, dilations[1])
    slope_mid = (
        temporal_back(band_back, second_temporal, dilations[1]) * silu_slope(pre_mid)
    ).astype(jnp.bfloat16)
    first_grad = temporal_kernel(band_in, slope_mid, dilations[0])
    back_in = temporal_back(slope_mid, first_temporal, dilations[0]).astype(jnp.bfloat16)
    frame_out, frame_back = (
        lax.all_to_all(act_out, "tm", split_axis=1, concat_axis=2, tiled=True),
        lax.all_to_all(back_in, "tm", split_axis=1, concat_axis=2, tiled=True),
    )
    decoded = jnp.where(
        is_valid, latents.astype(jnp.float32) + spatial(frame_out, last_spatial), jnp.float32(0.0)
    ).astype(jnp.bfloat16)
    last_grad = spatial_kernel(frame_out, masked)
    slope_in = (frame_back.astype(jnp.float32) * silu_slope(pre_in)).astype(jnp.bfloat16)
    spatial_grad = spatial_kernel(latents, slope_in)
    latent_grad = (masked.astype(jnp.float32) + spatial_back(slope_in, first_spatial)).astype(
        jnp.bfloat16
    )
    partials = (
        factor * spatial_grad,
        factor * last_grad,
        factor * first_grad,
        factor * second_grad,
    )
    reduced = lax.psum((partials[0], partials[1], partials[2], partials[3]), ("dp", "tm"))
    return (decoded, latent_grad, reduced[0], reduced[1], reduced[2], reduced[3])


REACH = (TAPS - 1) * DILATION_MAX
CHUNKS = 2
VMEM_LIMIT = 52 * 1024 * 1024
BF = jnp.bfloat16
F32 = jnp.float32


def params():
    return pltpu.CompilerParams(
        dimension_semantics=("arbitrary",), vmem_limit_bytes=VMEM_LIMIT
    )


COST = 0.02


def cost(micros):
    return pl.CostEstimate(flops=int(micros * COST * 1e9), bytes_accessed=1000, transcendentals=0)


def pair_range(chunk, rows):
    size = rows // CHUNKS
    low = 0 if chunk == 0 else chunk * size // 2 - 1
    high = rows // 2 if chunk == CHUNKS - 1 else (chunk + 1) * size // 2 - 1
    return low, high


def seen_rows(low, high, rows):
    return max(0, 2 * low - 1), min(rows, 2 * high + 1)


def zero_borders(pad, pairs, low, high, rows):
    pad[...] = jnp.zeros(pad.shape, F32)
    frames, _, width, lanes = pairs.shape
    for frame in range(frames):
        if low == 0:
            pairs[frame, 0, :, 0 : lanes // 2] = jnp.zeros((width, lanes // 2), BF)
        if 2 * high == rows:
            pairs[frame, high - low, :, lanes // 2 : lanes] = jnp.zeros((width, lanes // 2), BF)


def fill_pairs(read_row, pad, pairs, low, high, rows):
    frames, _, width, lanes = pairs.shape
    chans = lanes // 6
    begin, end = seen_rows(low, high, rows)
    for frame in range(frames):
        for row in range(begin, end):
            pad[frame, row - begin, 8 : 8 + width, :] = read_row(frame, row).astype(F32)
    for frame in range(frames):
        for row in range(begin, end):
            at = (row + 1) // 2 - low
            side = 3 * chans * (1 - row % 2)
            pairs[frame, at, :, side + chans : side + 2 * chans] = read_row(frame, row)
            for shift in (0, 2):
                seen = pad[frame, row - begin, 7 + shift : 7 + shift + width, :].astype(BF)
                lane = side + shift * chans
                pairs[frame, at, :, lane : lane + chans] = seen


def front_kernel(slots, ids, *refs):
    latents, cotangent = refs[0:2], refs[2:4]
    w_in, w_back, act, back, slope, leaving, pads, windows = refs[4:]
    at = pl.program_id(0)
    side, core, shift_rows = ids[0], ids[1], ids[7]
    spread, width, chans = latents[0].shape[1:]
    count = spread // 2 - 1
    lanes = 6 * chans

    @pl.when(at == 0)
    def _():
        pads[...] = jnp.zeros(pads.shape, F32)

    def conv(blocks, weights, pad, pairs):
        for index in range(2):
            for row in range(spread):
                place = index * (spread + 2) + 1 + row
                pad[place, 8 : 8 + width, :] = blocks[index][0, row].astype(F32)
        for index in range(2):
            for row in range(spread):
                place = index * (spread + 2) + 1 + row + shift_rows
                side = 3 * chans * (row % 2)
                to = index * (count + 1) + row // 2
                for shift in range(3):
                    seen = pad[place, 7 + shift : 7 + shift + width, :].astype(BF)
                    pairs[to, :, side + shift * chans : side + (shift + 1) * chans] = seen
        stacked = []
        for lower in range(2):
            both = [
                pairs[index * (count + 1) + lower : index * (count + 1) + lower + count]
                for index in range(2)
            ]
            stacked.append(jnp.concatenate(both, axis=0).reshape(2 * count * width, lanes))
        return jnp.dot(
            jnp.concatenate(stacked, axis=1), weights[...], preferred_element_type=F32
        )

    def store(target, values):
        values = values.reshape(2 * count, width, 2 * chans)
        for index in range(2):
            owner = core if index == 0 else 1 - core
            for row in range(2 * count):
                lane = row % 2 * chans
                target[owner, 0, row] = values[index * count + row // 2, :, lane : lane + chans]

    pre = conv(latents, w_in, pads.at[0], windows.at[0])
    summed = conv(cotangent, w_back, pads.at[1], windows.at[1])
    sigma = jax.nn.sigmoid(pre)
    store(act, (pre * sigma).astype(BF))
    store(slope, (sigma * (1.0 + pre * (1.0 - sigma))).astype(BF))
    half = count * width
    mine = jnp.where(core * slots + at < ids[2], 1.0, 0.0).astype(F32)
    other = jnp.where((1 - core) * slots + at < ids[2], 1.0, 0.0).astype(F32)
    store(back, jnp.concatenate([summed[:half] * mine, summed[half:] * other], 0).astype(BF))

    tail = leaving.shape[0] - slots

    @pl.when(side == 0)
    def _():
        leaving[at + tail] = act[1, 0]

    @pl.when((side == 0) & (at >= slots - tail))
    def _():
        leaving[at - (slots - tail)] = act[0, 0]

    @pl.when(side == 1)
    def _():
        leaving[at] = back[0, 0]

    @pl.when((side == 1) & (at < tail))
    def _():
        leaving[slots + at] = back[1, 0]


def front(ids, latents, cotangent, w_in, w_back):
    slots, spread, width, chans = latents[1].shape
    rows = spread - 2
    own = pl.BlockSpec(
        (pl.Element(1), pl.Element(spread), pl.Element(width), pl.Element(chans)),
        lambda i, ids: (i, ids[6], 0, 0),
    )
    got = pl.BlockSpec((1, spread, width, chans), lambda i, ids: (i, 0, 0, 0))
    target = pl.BlockSpec((2, 1, rows, width, chans), lambda i, ids: (0, i, 0, 0, 0))
    fixed = pl.BlockSpec(w_in.shape, lambda i, ids: (0, 0))
    made = pl.pallas_call(
        functools.partial(front_kernel, slots),
        grid_spec=pltpu.PrefetchScalarGridSpec(
            num_scalar_prefetch=1,
            grid=(slots,),
            in_specs=[own, got, own, got, fixed, fixed],
            out_specs=[
                target, target, target,
                pl.BlockSpec((REACH, rows, width, chans), lambda i, ids: (0, 0, 0, 0)),
            ],
            scratch_shapes=[
                pltpu.VMEM((2, 2 * (spread + 2), width + 16, chans), F32),
                pltpu.VMEM((2, spread, width, 6 * chans), BF),
            ],
        ),
        out_shape=[jax.ShapeDtypeStruct((2, slots, rows, width, chans), BF)] * 3
        + [jax.ShapeDtypeStruct((REACH, rows, width, chans), BF)],
        compiler_params=params(),
        cost_estimate=cost(22.0 / CHUNKS),
        name="front",
    )(ids, *latents, *cotangent, w_in, w_back)
    return [value.reshape(-1, rows, width, chans) for value in made]


def taps_of(held, start, step, count):
    size = held.shape[1]
    chans = held.shape[2]
    seen = []
    for tap in range(TAPS):
        seen.append(held[pl.ds(start + tap * step, count)].reshape(count * size, chans))
    return jnp.concatenate(seen, axis=1)


def outer(left, right):
    return lax.dot_general(left, right, (((0,), (0,)), ((), ())), preferred_element_type=F32)


def middle_kernel(
    ids, act_in, act_back, slope, halo, w_mid, w_mid_back, w_first,
    mid_send, mid_keep, first_keep, first_send, grad_first, grad_second,
    held_in, held_back, held_mid, result,
):
    at = pl.program_id(0)
    side, core, near, far = ids[0], ids[1], ids[3], ids[4]
    frames = act_in.shape[0]
    slots = frames // 2
    mine = core * slots
    other = slots - mine

    @pl.when(at == 0)
    def _():
        blank = jnp.zeros((REACH,) + held_in.shape[1:], BF)
        held_mid[0:REACH] = blank
        held_mid[REACH + frames : 2 * REACH + frames] = blank
        grad_first[...] = jnp.zeros_like(grad_first)
        grad_second[...] = jnp.zeros_like(grad_second)

    held_in[REACH : REACH + frames] = act_in[:, 0]
    held_back[0:frames] = act_back[:, 0]

    one = side.astype(F32)
    held_in[0:REACH] = (halo[:, 0].astype(F32) * one).astype(BF)
    held_back[frames : frames + REACH] = (halo[:, 0].astype(F32) * (1.0 - one)).astype(BF)

    size, chans = held_in.shape[1:]
    taps_in = taps_of(held_in, REACH, -near, frames)
    taps_back = taps_of(held_back, 0, far, frames)
    pre = jnp.dot(taps_in, w_mid[...], preferred_element_type=F32)
    sigma = jax.nn.sigmoid(pre)
    act = (pre * sigma).astype(BF)
    back = jnp.dot(taps_back, w_mid_back[...], preferred_element_type=F32)
    grad = (back * (sigma * (1.0 + pre * (1.0 - sigma)))).astype(BF)
    grad_second[...] += outer(act, taps_back)
    grad_first[...] += outer(grad, taps_in)
    act = act.reshape(frames, size, chans)
    grad = grad.reshape(frames, size, chans)

    ours = jnp.where(side == 0, act, grad)
    held_mid[REACH : REACH + frames] = ours
    mid_keep[:, 0] = jnp.where(side == 0, grad, act)
    mid_send[:, 0] = held_mid[pl.ds(REACH + (1 - side) * (frames - REACH), REACH)]
    step = jnp.where(side == 0, -far, near)
    first = jnp.dot(
        taps_of(held_mid, REACH, step, frames), w_first[...], preferred_element_type=F32
    )
    first = first.astype(BF).reshape(frames, size, chans).astype(F32)
    result[...] = (first * (slope[:, 0].astype(F32) * one + (1.0 - one))).astype(BF)
    first_keep[:, 0] = result[pl.ds(mine, slots)]
    first_send[:, 0] = result[pl.ds(other, slots)]


def middle(ids, act_in, act_back, slope, halo, w_mid, w_mid_back, w_first):
    frames, rows, width, chans = act_in.shape
    slots = frames // 2
    fixed = pl.BlockSpec(w_mid.shape, lambda i, ids: (0, 0))
    sums = pl.BlockSpec((chans, TAPS * chans), lambda i, ids: (0, 0))

    def rowwise(count):
        return pl.BlockSpec((count, 1, width, chans), lambda i, ids: (0, i, 0, 0))

    def shaped(count):
        return jax.ShapeDtypeStruct((count, rows, width, chans), BF)

    summed = jax.ShapeDtypeStruct((chans, TAPS * chans), F32)
    return pl.pallas_call(
        middle_kernel,
        grid_spec=pltpu.PrefetchScalarGridSpec(
            num_scalar_prefetch=1,
            grid=(rows,),
            in_specs=[rowwise(frames)] * 3 + [rowwise(REACH), fixed, fixed, fixed],
            out_specs=[
                rowwise(REACH), rowwise(frames), rowwise(slots), rowwise(slots), sums, sums,
            ],
            scratch_shapes=[
                pltpu.VMEM((REACH + frames, width, chans), BF),
                pltpu.VMEM((REACH + frames, width, chans), BF),
                pltpu.VMEM((2 * REACH + frames, width, chans), BF),
                pltpu.VMEM((frames, width, chans), BF),
            ],
        ),
        out_shape=[
            shaped(REACH), shaped(frames), shaped(slots), shaped(slots), summed, summed,
        ],
        compiler_params=params(),
        cost_estimate=cost(24.0 / CHUNKS),
        name="middle",
    )(ids, act_in, act_back, slope, halo, w_mid, w_mid_back, w_first)


def second_kernel(ids, mid, slope, halo, w_second, keep, send, held, result):
    side, core, near, far = ids[0], ids[1], ids[3], ids[4]
    frames, each = mid.shape[:2]
    slots = frames // 2
    mine = core * slots
    size, chans = held.shape[2:]
    one = side.astype(F32)
    step = jnp.where(side == 0, near, -far)
    for row in range(each):
        held[row, 0:REACH] = (halo[:, row].astype(F32) * one).astype(BF)
        held[row, REACH : REACH + frames] = mid[:, row]
        held[row, REACH + frames :] = (halo[:, row].astype(F32) * (1.0 - one)).astype(BF)
        made = jnp.dot(
            taps_of(held.at[row], REACH, step, frames), w_second[...], preferred_element_type=F32
        )
        made = made.astype(BF).reshape(frames, size, chans).astype(F32)
        result[row] = (made * (slope[:, row].astype(F32) * (1.0 - one) + one)).astype(BF)
        keep[:, row] = result[row, pl.ds(mine, slots)]
        send[:, row] = result[row, pl.ds(slots - mine, slots)]


def second(ids, mid, slope, halo, w_second):
    frames, rows, width, chans = mid.shape
    slots = frames // 2
    each = 2

    def rowwise(count):
        return pl.BlockSpec((count, each, width, chans), lambda i, ids: (0, i, 0, 0))

    shape = jax.ShapeDtypeStruct((slots, rows, width, chans), BF)
    return pl.pallas_call(
        second_kernel,
        grid_spec=pltpu.PrefetchScalarGridSpec(
            num_scalar_prefetch=1,
            grid=(rows // each,),
            in_specs=[
                rowwise(frames), rowwise(frames), rowwise(REACH),
                pl.BlockSpec(w_second.shape, lambda i, ids: (0, 0)),
            ],
            out_specs=[rowwise(slots), rowwise(slots)],
            scratch_shapes=[
                pltpu.VMEM((each, 2 * REACH + frames, width, chans), BF),
                pltpu.VMEM((each, frames, width, chans), BF),
            ],
        ),
        out_shape=[shape, shape],
        compiler_params=params(),
        cost_estimate=cost(10.0 / CHUNKS),
        name="second",
    )(ids, mid, slope, halo, w_second)


def ending_kernel(chunk, rows, factor, with_outs, ids, *refs):
    refs = list(refs)
    used = 1 if chunk == 0 else 2
    own = [refs.pop(0) for _ in range(used)]
    got = [refs.pop(0) for _ in range(used)]
    latents, cotangent, weights, before = [refs.pop(0) for _ in range(4)]
    if with_outs:
        refs.pop(0), refs.pop(0)
    outs = (refs.pop(0), refs.pop(0))
    sums, pad, pairs, frame, buffer, sems, beside, total = refs
    at = pl.program_id(0)
    last = pl.num_programs(0) - 1
    core, role = ids[1], ids[5]
    frames, _, width, lanes = pairs.shape
    chans = lanes // 6
    low, high = pair_range(chunk, rows)
    size = rows // CHUNKS
    half = size // 2
    base = (chunk + 1 - used) * size
    count = high - low

    def each_copy(step, act):
        for way in range(2):
            @pl.when(role == way)
            def _():
                target = outs[way].at[pl.ds(step * frames, frames), pl.ds(2 * low, 2 * count)]
                act(pltpu.make_async_copy(buffer.at[step % 2], target, sems.at[step % 2]))

    @pl.when(at == 0)
    def _():
        zero_borders(pad, pairs, low, high, rows)
        total[...] = jnp.zeros_like(total)

    @pl.when(at >= 2)
    def _():
        each_copy(at - 2, lambda copy: copy.wait())

    for index in range(used):
        frame[:, pl.ds(index * size + core * half, half)] = own[index][...]
        frame[:, pl.ds(index * size + half - core * half, half)] = got[index][...]
    fill_pairs(lambda which, row: frame[which, row - base], pad, pairs, low, high, rows)
    slot = at % 2
    one = jnp.where(role == 1, 1.0, 0.0).astype(F32)
    for which in range(frames):
        place = (core * (last + 1) + at) * frames + which
        valid = jnp.where(place < ids[2], 1.0, 0.0).astype(F32)
        zero = (1.0 - one) * valid
        upper = pairs[which, 0:count].reshape(count * width, lanes)
        lower = pairs[which, 1 : 1 + count].reshape(count * width, lanes)
        made = jnp.dot(
            jnp.concatenate([upper, lower], axis=1), weights[...], preferred_element_type=F32
        )
        made = made.reshape(count, width, 2 * chans)
        for row in range(2 * count):
            lane = row % 2 * chans
            latent = latents[which, row].astype(F32)
            arriving = cotangent[which, row].astype(F32)
            beside[which, row // 2, :, lane : lane + chans] = (
                latent * one + arriving * zero
            ).astype(BF)
            buffer[slot, which, row] = (
                latent * zero
                + arriving * (one * valid)
                + made[row // 2, :, lane : lane + chans] * (one + zero)
            ).astype(BF)
    flat = beside[...].reshape(frames * count * width, 2 * chans)
    for part in range(2):
        seen = pairs[:, part : part + count].reshape(frames * count * width, lanes)
        total[:, part * lanes : (part + 1) * lanes] += outer(flat, seen)
    each_copy(at, lambda copy: copy.start())

    @pl.when(at == last)
    def _():
        span = 9 * chans
        sums[...] = before[...] + factor * (
            total[0:chans, 0:span] + total[chans : 2 * chans, 3 * chans : 3 * chans + span]
        )
        each_copy(at - 1, lambda copy: copy.wait())
        each_copy(at, lambda copy: copy.wait())


def ending(chunk, factor, ids, own, got, latents, cotangent, weights, before, outs=None):
    slots, rows, width, chans = latents.shape
    size = rows // CHUNKS
    low, high = pair_range(chunk, rows)
    count = high - low
    begin, end = seen_rows(low, high, rows)
    used = 1 if chunk == 0 else 2
    each = 2
    area = pl.BlockSpec(
        (pl.Element(each), pl.Element(2 * count), pl.Element(width), pl.Element(chans)),
        lambda i, ids: (i * each, 2 * low, 0, 0),
    )
    part = pl.BlockSpec((each, size // 2, width, chans), lambda i, ids: (i, 0, 0, 0))
    summed = pl.BlockSpec((chans, 9 * chans), lambda i, ids: (0, 0))
    anywhere = pl.BlockSpec(memory_space=pl.ANY)
    pick = slice(chunk + 1 - used, chunk + 1)
    args = [*own[pick], *got[pick], latents, cotangent, weights, before]
    in_specs = [part] * (2 * used) + [area, area]
    in_specs += [pl.BlockSpec(weights.shape, lambda i, ids: (0, 0)), summed]
    aliases = {}
    if outs is not None:
        aliases = {1 + len(args): 0, 2 + len(args): 1}
        args += list(outs)
        in_specs += [anywhere, anywhere]
    return pl.pallas_call(
        functools.partial(ending_kernel, chunk, rows, factor, outs is not None),
        grid_spec=pltpu.PrefetchScalarGridSpec(
            num_scalar_prefetch=1,
            grid=(slots // each,),
            in_specs=in_specs,
            out_specs=[anywhere, anywhere, summed],
            scratch_shapes=[
                pltpu.VMEM((each, end - begin, width + 16, chans), F32),
                pltpu.VMEM((each, count + 1, width, 6 * chans), BF),
                pltpu.VMEM((each, used * size, width, chans), BF),
                pltpu.VMEM((2, each, 2 * count, width, chans), BF),
                pltpu.SemaphoreType.DMA((2,)),
                pltpu.VMEM((each, count, width, 2 * chans), BF),
                pltpu.VMEM((2 * chans, 12 * chans), F32),
            ],
        ),
        out_shape=[
            jax.ShapeDtypeStruct(latents.shape, BF),
            jax.ShapeDtypeStruct(latents.shape, BF),
            jax.ShapeDtypeStruct((chans, 9 * chans), F32),
        ],
        input_output_aliases=aliases,
        compiler_params=params(),
        cost_estimate=cost(26.0 / CHUNKS),
        name="ending",
    )(ids, *args)


def two_row_weights(kernel):
    flat = kernel.reshape(-1, kernel.shape[3])
    shift = 3 * kernel.shape[2]
    return jnp.concatenate(
        [jnp.pad(flat, ((0, shift), (0, 0))), jnp.pad(flat, ((shift, 0), (0, 0)))], axis=1
    )


def after(value, *earlier):
    return lax.optimization_barrier((value,) + earlier)[0]


def turned(kernel):
    return jnp.transpose(kernel[::-1, ::-1], (0, 1, 3, 2))


def flips(dp_size, tm_size):
    count = dp_size * tm_size
    digit = 1
    result = []
    while digit < count:
        result.append([(place, place ^ digit) for place in range(count)])
        digit *= 2
    return result


def halve(values, digits, pairs, place):
    for digit in digits:
        size = values.shape[0] // 2
        upper = (place >> digit) & 1
        keep = lax.dynamic_slice_in_dim(values, upper * size, size, 0)
        send = lax.dynamic_slice_in_dim(values, (1 - upper) * size, size, 0)
        values = keep + lax.ppermute(send, ("dp", "tm"), pairs[digit])
    return values


def double(values, digits, pairs, place, axis=0):
    for digit in digits:
        upper = (place >> digit) & 1
        other = lax.ppermute(values, ("dp", "tm"), pairs[digit])
        values = jnp.where(
            upper == 0,
            jnp.concatenate([values, other], axis),
            jnp.concatenate([other, values], axis),
        )
    return values


def on_chip_pair(
    dp_size,
    latents,
    cotangent,
    first_spatial,
    last_spatial,
    first_temporal,
    second_temporal,
    frame_counts,
    dilations,
):
    latents, cotangent = latents[0], cotangent[0]
    slots, rows, width, chans = latents.shape
    half = rows // 2
    tm_index = lax.axis_index("tm")
    side, core = tm_index // 2, tm_index % 2
    factor = float(dp_size * 4 * slots * rows * width) ** (-0.5)

    def ids_for(role):
        return jnp.stack(
            [side, core, frame_counts[0] - side * 2 * slots, dilations[0], dilations[1], role]
        ).astype(jnp.int32)

    ids = ids_for(side)
    swap_cores = [(0, 1), (1, 0), (2, 3), (3, 2)]
    swap_sides = [(0, 2), (2, 0), (1, 3), (3, 1)]

    w_in = two_row_weights(first_spatial)
    w_out = two_row_weights(last_spatial)
    w_in_back = two_row_weights(turned(first_spatial))
    w_out_back = two_row_weights(turned(last_spatial))
    w_one = first_temporal.reshape(-1, chans)
    w_two = second_temporal.reshape(-1, chans)
    w_one_back = jnp.transpose(first_temporal, (0, 2, 1)).reshape(-1, chans)
    w_two_back = jnp.transpose(second_temporal, (0, 2, 1)).reshape(-1, chans)
    at_zero = side == 0
    w_first = jnp.where(at_zero, w_two, w_one_back)
    w_second = jnp.where(at_zero, w_one_back, w_two)
    w_ending = jnp.where(at_zero, w_out, w_in_back)
    w_other = jnp.where(at_zero, w_in_back, w_out)

    band = rows // CHUNKS // 2
    entries, slopes = [], []
    for chunk in range(CHUNKS):
        start = chunk * 2 * band + (1 - core) * band - 1
        sent = [
            lax.dynamic_slice_in_dim(value, jnp.clip(start, 0, rows - band - 2), band + 2, 1)
            for value in (latents, cotangent)
        ]
        if chunk > 0:
            sent = [after(value, act) for value in sent]
        got = [lax.ppermute(value, "tm", swap_cores) for value in sent]
        start = chunk * 2 * band + core * band - 1
        kept = jnp.clip(start, 0, rows - band - 2)
        front_ids = jnp.concatenate([ids, jnp.stack([kept, start - kept]).astype(jnp.int32)])
        act, back, slope, leaving = front(
            front_ids, [latents, got[0]], [cotangent, got[1]], w_in, w_out_back
        )
        slopes.append(slope)
        if chunk > 0:
            leaving = after(leaving, halo)
        halo = lax.ppermute(leaving, "tm", swap_sides)
        entries.append([act, back, slope, halo])
    middles, halos, own, got = [], [], [], []
    outs = None
    sums_first = jnp.zeros((chans, 9 * chans), F32)
    for chunk in range(CHUNKS):
        act, back, slope, arrived = entries[chunk]
        made = middle(ids, act, back, slope, arrived, w_one, w_two_back, w_first)
        middles.append(made)
        own.append(made[2])
        got.append(lax.ppermute(made[3], "tm", swap_cores))
        *outs, sums_first = ending(
            chunk, factor, ids, own, got, latents, cotangent, w_ending, sums_first, outs
        )
        halo = lax.ppermute(after(made[0], halo, sums_first), "tm", swap_sides)
        halos.append(halo)

    pairs = flips(dp_size, 4)
    place = lax.axis_index("dp") * 4 + tm_index
    digits = [0] + list(range(2, len(pairs)))
    span = 9 * chans
    ids = ids_for(1 - side)
    own, got = [], []
    sums_second = jnp.zeros((chans, span), F32)
    for chunk, made in enumerate(middles):
        keep, leaving = second(ids, made[1], slopes[chunk], halos[chunk], w_second)
        own.append(keep)
        got.append(lax.ppermute(leaving, "tm", swap_cores))
        *outs, sums_second = ending(
            chunk, factor, ids, own, got, latents, cotangent, w_other, sums_second, outs
        )
        if chunk < CHUNKS - 1:
            halos[chunk + 1] = after(halos[chunk + 1], sums_second)
    decoded, latent_grad = outs

    early = jnp.concatenate(
        [
            sums_first,
            factor * sum(made[4] for made in middles),
            factor * sum(made[5] for made in middles),
        ],
        1,
    )
    early = after(early, halos[-1])
    early = halve(early, digits, pairs, place)
    late = halve(sums_second, digits, pairs, place)
    both = jnp.concatenate([early, late], 1)
    other = lax.ppermute(both, ("dp", "tm"), pairs[1])
    swapped = jnp.concatenate([other[:, -span:], other[:, span:-span], other[:, :span]], 1)
    both = both + swapped
    both = jnp.where(
        at_zero, both, jnp.concatenate([both[:, -span:], both[:, span:-span], both[:, :span]], 1)
    )
    both = double(both.astype(BF), digits[::-1], pairs, place)
    spatial_sums = (both[:, :span], both[:, -span:])
    temporal_sums = both[:, span:-span]

    last_grad = jnp.transpose(spatial_sums[0].reshape(chans, 3, 3, chans), (1, 2, 3, 0))
    first_grad = jnp.transpose(spatial_sums[1].reshape(chans, 3, 3, chans), (1, 2, 0, 3))
    first_grad = first_grad[::-1, ::-1]
    near_grad = jnp.transpose(temporal_sums[:, : TAPS * chans].reshape(chans, TAPS, chans), (1, 2, 0))
    far_grad = jnp.transpose(temporal_sums[:, TAPS * chans :].reshape(chans, TAPS, chans), (1, 0, 2))
    sums = [value.astype(F32) for value in (first_grad, last_grad, near_grad, far_grad)]
    return (decoded[None], latent_grad[None], *sums)


def on_any_device(dp_size, tm_size, latents, cotangent, *rest):
    clips, slots, rows = latents.shape[:3]
    fits = clips == 1 and tm_size == 4 and slots <= REACH <= 2 * slots and rows % 8 == 0 and slots % 2 == 0
    if fits and dp_size & (dp_size - 1) == 0:
        return on_chip_pair(dp_size, latents, cotangent, *rest)
    return on_device(latents, cotangent, *rest)


def solution(mesh):
    in_specs = (
        P("dp", "tm", None, None, None),
        P("dp", "tm", None, None, None),
        P(),
        P(),
        P(),
        P(),
        P("dp"),
        P(),
    )
    out_specs = (
        P("dp", "tm", None, None, None),
        P("dp", "tm", None, None, None),
        P(),
        P(),
        P(),
        P(),
    )
    return jax.shard_map(
        functools.partial(on_any_device, mesh.shape["dp"], mesh.shape["tm"]), mesh=mesh, in_specs=in_specs, out_specs=out_specs, check_vma=False
    )
```
